32 devices in a mesh: seq: 8 (over z, y), tensor: 4 (over x, core).
Axes of the slice: x: 2, y: 2, z: 4, core: 2. Of those that a mesh axis runs over, the one named last changes fastest.
Arguments:
- block_input: bfloat16 [4096, 2048], P(('seq', 'tensor')), may hold values from -6 to 6
- lengths: int32 [4], replicated, may hold values from 1 to 3840, as said below
- norm1_gain: float32 [2048], replicated, may hold values from 0.5 to 1.5
- q_down: bfloat16 [2048, 1024], replicated, may hold values from -0.125 to 0.125
- q_gain: float32 [1024], replicated, may hold values from 0.5 to 1.5
- q_up: bfloat16 [1024, 4096], P(None, 'tensor'), may hold values from -0.25 to 0.25
- kv_weight: bfloat16 [2048, 512], replicated, may hold values from -0.125 to 0.125
- out_weight: bfloat16 [4096, 2048], P('tensor'), may hold values from -0.5 to 0.5
- norm2_gain: float32 [2048], replicated, may hold values from 0.5 to 1.5
- gate_weight: bfloat16 [2048, 5632], P(None, 'tensor'), may hold values from -0.125 to 0.125
- up_weight: bfloat16 [2048, 5632], P(None, 'tensor'), may hold values from -0.125 to 0.125
- down_weight: bfloat16 [5632, 2048], P('tensor'), may hold values from -0.078125 to 0.078125
- cotangent: bfloat16 [4096, 2048], P(('seq', 'tensor')), may hold values from -6 to 6
Outputs:
- block_output: bfloat16 [4096, 2048], P(('seq', 'tensor'))
- input_grad: float32 [4096, 2048], P(('seq', 'tensor'))
- norm1_gain_grad: float32 [2048], P(('seq', 'tensor'))
- q_down_grad: float32 [2048, 1024], P(('seq', 'tensor'))
- q_gain_grad: float32 [1024], P(('seq', 'tensor'))
- q_up_grad: float32 [1024, 4096], P('seq', 'tensor')
- kv_weight_grad: float32 [2048, 512], P(('seq', 'tensor'))
- out_weight_grad: float32 [4096, 2048], P('tensor', 'seq')
- norm2_gain_grad: float32 [2048], P(('seq', 'tensor'))
- gate_grad: float32 [2048, 5632], P('seq', 'tensor')
- up_grad: float32 [2048, 5632], P('seq', 'tensor')
- down_grad: float32 [5632, 2048], P('tensor', 'seq')
The draws below stay inside these ranges and needn't reach their ends.
Inputs may be any that keep to these rules, and one draw needn't show every extreme that they name: `lengths`: 4 sequences packed in token order, summing to 4096; one of them, at a place that differs from draw to draw, has exactly 3840 tokens, so that it starts on the first index of seq and ends on the last; the other three together have 512 // 2 tokens.
All inputs are finite; a program needn't handle non-finite values.
Results may differ from the reference program's by a relative error of at most 0.02.
Values may be sent and summed in bfloat16 or wider, within the bound.
No kernel may reach another device: no remote copies, remote signals or barrier semaphores. Data moves between devices by JAX's collectives and lax.ppermute only.
A program may use at most 320 MiB of HBM per device.

```python
import math
import jax
import jax.numpy as jnp
from jax import lax

D = 2048
QR = 1024
HEADS = 16
HD = 256
FF = 5632
TOK_DEV = 512
NSEQS = 4
KEY_BLOCK = 512
TOKENS = 4096


def draw_lengths(key, part):
    key = jax.random.fold_in(key, 11)
    key_one, key_two, key_three = jax.random.split(key, 3)
    room = TOK_DEV // 2
    first_short = jax.random.randint(key_one, (), 1, TOK_DEV // 6 + 1).astype(jnp.int32)
    second_short = jax.random.randint(key_two, (), 1, TOK_DEV // 6 + 1).astype(jnp.int32)
    shorts = jnp.stack([first_short, second_short, room - first_short - second_short]).astype(jnp.int32)
    place = jax.random.randint(key_three, (), 0, NSEQS).astype(jnp.int32)
    slots = jnp.arange(NSEQS, dtype=jnp.int32)
    before = jnp.concatenate([shorts, shorts[-1:]])
    after = jnp.concatenate([shorts[:1], shorts])
    longest = jnp.full((NSEQS,), TOKENS - room, jnp.int32)
    return jnp.where(slots < place, before, jnp.where(slots == place, longest, after)).astype(jnp.int32)


def levels(rng, dims, cuts, smallest, largest):
    factor_of = 1.0
    for dim, blocks in cuts:
        draws = jax.random.uniform(jax.random.fold_in(jax.random.fold_in(rng, 6), dim), (blocks,), jnp.float32, smallest / len(cuts), largest / len(cuts))
        factor_of = factor_of * jnp.repeat(jnp.exp(draws), dims[dim] // blocks).reshape((-1,) + (1,) * (len(dims) - 1 - dim))
    return factor_of


def centred(rng, shape, scale, reach, pieces=(), held_as=jnp.bfloat16):
    gain = levels(rng, shape, pieces, -0.22, 0.18) if pieces else 1.0
    drawn = jax.random.normal(rng, shape, jnp.float32) * scale * gain
    return jnp.minimum(jnp.maximum(drawn, -reach), reach).astype(held_as)


def setup_inputs(seed: int = 0) -> dict:
    arg_keys = jax.random.split(jax.random.key(seed), 14)
    block_input = centred(arg_keys[0], (TOKENS, D), 1.0, 6.0, ((0, 32),))
    lengths = draw_lengths(jax.random.fold_in(arg_keys[13], 71), 0)
    norm1_gain = jnp.clip(1.0 + 0.1 * jax.random.normal(arg_keys[2], (D,), jnp.float32), 0.5, 1.5)
    q_down = centred(arg_keys[3], (D, QR), D ** -0.5, 0.125)
    q_gain = jnp.clip(1.0 + 0.1 * jax.random.normal(arg_keys[4], (QR,), jnp.float32), 0.5, 1.5)
    q_up = centred(arg_keys[5], (QR, HEADS * HD), (QR // 2) ** -0.5, 0.25, ((1, 4),))
    kv_weight = centred(arg_keys[6], (D, 2 * HD), D ** -0.5, 0.125)
    out_weight = centred(arg_keys[7], (HEADS * HD, D), (HEADS * HD // 32) ** -0.5, 0.5, ((0, 4),))
    norm2_gain = jnp.clip(1.0 + 0.1 * jax.random.normal(arg_keys[8], (D,), jnp.float32), 0.5, 1.5)
    gate_weight = centred(arg_keys[9], (D, FF), D ** -0.5, 0.125, ((1, 4),))
    up_weight = centred(arg_keys[10], (D, FF), D ** -0.5, 0.125, ((1, 4),))
    down_weight = centred(arg_keys[11], (FF, D), FF ** -0.5, 0.078125, ((0, 4),))
    cotangent = centred(arg_keys[12], (TOKENS, D), 1.0, 6.0, ((0, 32),))
    return {"block_input": block_input, "lengths": lengths, "norm1_gain": norm1_gain, "q_down": q_down, "q_gain": q_gain, "q_up": q_up, "kv_weight": kv_weight, "out_weight": out_weight, "norm2_gain": norm2_gain, "gate_weight": gate_weight, "up_weight": up_weight, "down_weight": down_weight, "cotangent": cotangent}


EPS = 1e-06
NEG = -1e+30
HIGH = lax.Precision.HIGHEST

@jax.custom_vjp
def low(v):
    return lax.optimization_barrier(v.astype(jnp.bfloat16)).astype(jnp.float32)

@jax.custom_vjp
def low_back(v):
    return v

def low_keep(v):
    return (low(v), None)

def low_pass(kept, grad):
    return (grad,)

def back_keep(v):
    return (v, None)

def back_low(kept, grad):
    return (low(grad),)
low.defvjp(low_keep, low_pass)
low_back.defvjp(back_keep, back_low)

def product(left, right):
    return jnp.dot(left, right, precision=HIGH)

def rms_scale(values):
    return values * lax.rsqrt(lax.optimization_barrier(jnp.mean(values * values, axis=-1, keepdims=True)) + EPS)

def locate(lengths):
    lengths = lengths.astype(jnp.int32)
    starts = (jnp.cumsum(lengths) - lengths).astype(jnp.int32)
    token_index = jnp.arange(TOKENS, dtype=jnp.int32)
    segment = lax.optimization_barrier(jnp.sum((token_index[:, None] >= starts[None, 1:]).astype(jnp.int32), axis=1)).astype(jnp.int32)
    position = (token_index - starts[segment]).astype(jnp.float32)
    return (token_index, segment, position)

def angles(position):
    halfway = HD // 2
    freq = 10000.0 ** (-(2.0 * jnp.arange(halfway, dtype=jnp.float32)) / HD)
    theta = position[:, None] * freq[None, :]
    return (jnp.cos(theta), jnp.sin(theta))

def rotate(values, cos_table, sin_table):
    halfway = values.shape[-1] // 2
    former = values[..., :halfway]
    latter = values[..., halfway:]
    cos_wide = cos_table[:, None, :]
    sin_wide = sin_table[:, None, :]
    return jnp.concatenate([former * cos_wide - latter * sin_wide, latter * cos_wide + former * sin_wide], axis=-1)

def reference(block_input, lengths, norm1_gain, q_down, q_gain, q_up, kv_weight, out_weight, norm2_gain, gate_weight, up_weight, down_weight, cotangent):
    token_index, segment, position = locate(lengths)
    cos_table, sin_table = angles(position)
    scaling = 1.0 / math.sqrt(HD)
    quarter = KEY_BLOCK // 2
    nblocks = TOKENS // quarter

    def attend(query, keyval):
        keys_all = keyval[:, :HD]
        values_all = keyval[:, HD:]

        def one_block(operands):
            query_tile, tile_index, tile_segment = operands
            logits = low_back(jnp.einsum('qhd,kd->hqk', query_tile, keys_all, precision=HIGH) * scaling)
            allowed = (token_index[None, :] <= tile_index[:, None]) & (segment[None, :] == tile_segment[:, None])
            logits = jnp.where(allowed[None], logits, NEG)
            shifted = logits - lax.optimization_barrier(jnp.max(logits, axis=-1, keepdims=True))
            weights = jnp.exp(shifted)
            probs = weights / lax.optimization_barrier(jnp.sum(weights, axis=-1, keepdims=True))
            return jnp.einsum('hqk,kd->qhd', low(probs), values_all, precision=HIGH)
        result = lax.map(jax.checkpoint(one_block), (query.reshape(nblocks, quarter, HEADS, HD), token_index.reshape(nblocks, quarter), segment.reshape(nblocks, quarter)))
        return result.reshape(TOKENS, HEADS * HD)

    def forward(inputs, gain_one, down_q, gain_q, up_q, weight_kv, weight_out, gain_two, weight_gate, weight_up, weight_down):
        normed = low(rms_scale(inputs) * gain_one)
        compressed = low_back(product(normed, down_q))
        latent = low(rms_scale(compressed) * gain_q)
        query_raw = low_back(product(latent, up_q))
        query = low(rotate(query_raw.reshape(TOKENS, HEADS, HD), cos_table, sin_table))
        kv_raw = low_back(product(normed, weight_kv))
        rotated = rotate(kv_raw[:, None, :HD], cos_table, sin_table)[:, 0]
        keyval = low(jnp.concatenate([rotated, kv_raw[:, HD:]], axis=1))
        attended = low(low_back(attend(query, keyval)))
        branch = low_back(product(attended, weight_out))
        residual = inputs + branch
        normed_two = low(rms_scale(residual) * gain_two)
        gate_pre = low_back(product(normed_two, weight_gate))
        up_pre = low_back(product(normed_two, weight_up))
        hidden = low(jax.nn.silu(gate_pre) * up_pre)
        return residual + low_back(product(hidden, weight_down))
    params = (block_input.astype(jnp.float32), norm1_gain.astype(jnp.float32), q_down.astype(jnp.float32), q_gain.astype(jnp.float32), q_up.astype(jnp.float32), kv_weight.astype(jnp.float32), out_weight.astype(jnp.float32), norm2_gain.astype(jnp.float32), gate_weight.astype(jnp.float32), up_weight.astype(jnp.float32), down_weight.astype(jnp.float32))
    output, pullback = jax.vjp(forward, *params)
    grads = pullback(cotangent.astype(jnp.float32))
    return (output.astype(jnp.bfloat16), grads[0], grads[1], grads[2], grads[3], grads[4], grads[5], grads[6], grads[7], grads[8], grads[9], grads[10])
```

```python
import functools
import math

import jax
import jax.numpy as jnp
from jax import lax
from jax.experimental import pallas as pl
from jax.experimental.pallas import tpu as pltpu
from jax.sharding import PartitionSpec as P

HD = 256
EPS = 1e-06
NEG = -1e30
F32 = jnp.float32
BF16 = jnp.bfloat16
LOG2_SCALE = math.log2(math.e) / math.sqrt(HD)
SCALE = 1.0 / math.sqrt(HD)
MIB = 1 << 20
BRIEF = pl.CostEstimate(flops=1000, bytes_accessed=1000, transcendentals=0)

NN = (((1,), (0,)), ((), ()))
NT = (((1,), (1,)), ((), ()))
TN = (((0,), (0,)), ((), ()))


def dot(left, right, dims=NN):
    return lax.dot_general(left, right, dims, preferred_element_type=F32)


def first_of_segment(token, starts):
    found = jnp.zeros_like(token)
    for start in starts:
        found = jnp.maximum(found, jnp.where(token >= start, start, 0))
    return found


def angles(position):
    halfway = HD // 2
    freq = 10000.0 ** (-(2.0 * jnp.arange(halfway, dtype=F32)) / HD)
    theta = position[:, None] * freq[None, :]
    return jnp.cos(theta), jnp.sin(theta)


def at_index(values, index, axis, keepdims=True):
    start = [jnp.int32(0)] * values.ndim
    start[axis] = index
    size = values.shape[:axis] + (1,) + values.shape[axis + 1 :]
    taken = lax.dynamic_slice(values, start, size, allow_negative_indices=False)
    return taken if keepdims else lax.squeeze(taken, [axis])


def rms_parts(values):
    inverse = lax.rsqrt(jnp.mean(values * values, axis=-1, keepdims=True) + EPS)
    return values * inverse, inverse


def rms_back(grad_out, scaled, inverse, gain):
    inner = grad_out * gain
    return inverse * (inner - scaled * jnp.mean(inner * scaled, axis=-1, keepdims=True))


def key_bias(meta, slot, qi_ref, ql_ref, keys, rows):
    block = keys // 4
    row = lax.broadcasted_iota(jnp.int32, (keys, rows), 0)
    which = row // block
    other = ((which & 1) << 1) | (which >> 1)
    token = meta[0, slot] + (meta[2, 0] ^ other) * block + (row & (block - 1))
    allowed = (token <= qi_ref[0:1, :]) & (token >= ql_ref[0:1, :])
    return jnp.where(allowed, 0.0, NEG)


def fwd_kernel(heads, first, last, slot, meta, q_ref, a_ref, b_ref, qi_ref, ql_ref, *refs):
    if not first:
        held, refs = refs[:3], refs[3:]
    if last:
        o_ref, ot_ref, lse_ref, m_s, l_s, acc_s, bias_s = refs
    else:
        m_s, l_s, acc_s, bias_s = refs
    step = pl.program_id(0)
    slot = slot + step

    @pl.when(step == 0)
    def _():
        if first:
            m_s[...] = jnp.full_like(m_s, NEG)
            l_s[...] = jnp.zeros_like(l_s)
            acc_s[...] = jnp.zeros_like(acc_s)
        else:
            m_s[...] = held[0][...]
            l_s[...] = held[1][...]
            acc_s[...] = held[2][...]

    def tile(masked):
        key = jnp.concatenate([a_ref[0, :, :HD], b_ref[0, :, :HD]], axis=0)
        value = jnp.concatenate([a_ref[0, :, HD:], b_ref[0, :, HD:]], axis=0)
        value_t = value.T
        if masked:
            bias_s[...] = key_bias(meta, slot, qi_ref, ql_ref, *bias_s.shape)

        def score(h):
            return dot(key, q_ref[:, h * HD : (h + 1) * HD], NT)

        following = score(0)
        for h in range(heads):
            scores = following * LOG2_SCALE
            if h + 1 < heads:
                following = score(h + 1)
            if masked:
                scores = scores + bias_s[...]
            old = m_s[h, 0:1, :]
            new = jnp.maximum(old, jnp.max(scores, axis=0, keepdims=True))
            alpha = jnp.exp2(old - new)
            weight = jnp.exp2(scores - new)
            l_s[h, 0:1, :] = l_s[h, 0:1, :] * alpha + jnp.sum(weight, axis=0, keepdims=True)
            m_s[h, 0:1, :] = new
            acc_s[h] = acc_s[h] * alpha + dot(value_t, weight.astype(BF16))

    pl.when(meta[1, slot] == 1)(lambda: tile(False))
    pl.when(meta[1, slot] == 2)(lambda: tile(True))

    if last:

        @pl.when(step == pl.num_programs(0) - 1)
        def _():
            for h in range(heads):
                total = l_s[h, 0:1, :]
                out_t = (acc_s[h] / total).astype(BF16)
                ot_ref[h * HD : (h + 1) * HD, :] = out_t
                o_ref[:, h * HD : (h + 1) * HD] = out_t.T
                lse_ref[h] = jnp.broadcast_to(m_s[h, 0:1, :] + jnp.log2(total), lse_ref.shape[1:])


def attend(meta, slot, query, kv_a, kv_b, q_index, q_low, held, last):
    rows, width = query.shape
    heads = width // HD
    slots, half, wide = kv_a.shape
    keys = 2 * half
    whole = lambda *shape: pl.BlockSpec(shape, lambda i, m: (0,) * len(shape))
    tile = pl.BlockSpec((1, half, wide), lambda i, m: (i, 0, 0))
    state = [(heads, 8, rows), (heads, 8, rows), (heads, HD, rows)]
    bias = pltpu.VMEM((keys, rows), F32)
    if last:
        out = [((rows, width), BF16), ((width, rows), BF16), ((heads, 8, rows), F32)]
        scratch = [pltpu.VMEM(shape, F32) for shape in state] + [bias]
    else:
        out = [(shape, F32) for shape in state]
        scratch = [bias]
    return pl.pallas_call(
        functools.partial(fwd_kernel, heads, not held, last, slot),
        grid_spec=pltpu.PrefetchScalarGridSpec(
            num_scalar_prefetch=1,
            grid=(slots,),
            in_specs=[whole(rows, width), tile, tile, whole(8, rows), whole(8, rows)]
            + [whole(*shape) for shape in state if held],
            out_specs=[whole(*shape) for shape, _ in out],
            scratch_shapes=scratch,
        ),
        out_shape=[jax.ShapeDtypeStruct(*o) for o in out],
        compiler_params=pltpu.CompilerParams(vmem_limit_bytes=24 * MIB),
        cost_estimate=BRIEF,
        name="attend",
    )(meta, query, kv_a, kv_b, q_index, q_low, *held)


def bwd_kernel(heads, meta, q_ref, do_ref, a_ref, b_ref, qi_ref, ql_ref, lse_ref, delta_ref, cos_ref, sin_ref,
               dq_ref, da_ref, db_ref, dq_s, dk_s, dv_s, bias_s):
    slot = pl.program_id(0)
    half = a_ref.shape[1]

    @pl.when(slot == 0)
    def _():
        dq_s[...] = jnp.zeros_like(dq_s)

    @pl.when(meta[1, slot] == 0)
    def _():
        da_ref[...] = jnp.zeros_like(da_ref)
        db_ref[...] = jnp.zeros_like(db_ref)

    def tile(masked):
        key = jnp.concatenate([a_ref[0, :, :HD], b_ref[0, :, :HD]], axis=0)
        value = jnp.concatenate([a_ref[0, :, HD:], b_ref[0, :, HD:]], axis=0)
        key_t = key.T
        if masked:
            bias_s[...] = key_bias(meta, slot, qi_ref, ql_ref, *bias_s.shape)
        for h in range(heads):
            at = slice(h * HD, (h + 1) * HD)
            scores = dot(key, q_ref[:, at], NT) * LOG2_SCALE
            if masked:
                scores = scores + bias_s[...]
            weight = jnp.exp2(scores - lse_ref[h, 0:1, :])
            grad = dot(value, do_ref[:, at], NT)
            ds = (weight * (grad - delta_ref[h, 0:1, :])).astype(BF16)
            dv = dot(weight.astype(BF16), do_ref[:, at])
            dk = dot(ds, q_ref[:, at])
            if h == 0:
                dv_s[...] = dv
                dk_s[...] = dk
            else:
                dv_s[...] += dv
                dk_s[...] += dk
            dq_s[h] += dot(key_t, ds)
        da_ref[0, :, :HD] = (dk_s[:half, :] * SCALE).astype(BF16)
        db_ref[0, :, :HD] = (dk_s[half:, :] * SCALE).astype(BF16)
        da_ref[0, :, HD:] = dv_s[:half, :].astype(BF16)
        db_ref[0, :, HD:] = dv_s[half:, :].astype(BF16)

    pl.when(meta[1, slot] == 1)(lambda: tile(False))
    pl.when(meta[1, slot] == 2)(lambda: tile(True))

    @pl.when(slot == pl.num_programs(0) - 1)
    def _():
        cos, sin = cos_ref[...], sin_ref[...]
        mid = HD // 2
        for h in range(heads):
            grad = (dq_s[h] * SCALE).T
            former, latter = grad[:, :mid], grad[:, mid:]
            dq_ref[:, h * HD : h * HD + mid] = (former * cos + latter * sin).astype(BF16)
            dq_ref[:, h * HD + mid : (h + 1) * HD] = (latter * cos - former * sin).astype(BF16)


def attend_back(meta, query, grad, kv_a, kv_b, q_index, q_low, lse, delta, cos, sin):
    rows, width = query.shape
    heads = width // HD
    slots, half, wide = kv_a.shape
    keys = 2 * half
    whole = lambda *shape: pl.BlockSpec(shape, lambda i, m: (0,) * len(shape))
    tile = pl.BlockSpec((1, half, wide), lambda i, m: (i, 0, 0))
    out_tile = pl.BlockSpec((1, half, wide), lambda i, m: (m[3, i], 0, 0))
    return pl.pallas_call(
        functools.partial(bwd_kernel, heads),
        grid_spec=pltpu.PrefetchScalarGridSpec(
            num_scalar_prefetch=1,
            grid=(slots,),
            in_specs=[
                whole(rows, width), whole(rows, width), tile, tile, whole(8, rows), whole(8, rows),
                whole(heads, 8, rows), whole(heads, 8, rows), whole(rows, HD // 2), whole(rows, HD // 2),
            ],
            out_specs=[whole(rows, width), out_tile, out_tile],
            scratch_shapes=[
                pltpu.VMEM((heads, HD, rows), F32),
                pltpu.VMEM((keys, HD), F32),
                pltpu.VMEM((keys, HD), F32),
                pltpu.VMEM((keys, rows), F32),
            ],
        ),
        out_shape=[
            jax.ShapeDtypeStruct((rows, width), BF16),
            jax.ShapeDtypeStruct((slots, half, wide), BF16),
            jax.ShapeDtypeStruct((slots, half, wide), BF16),
        ],
        compiler_params=pltpu.CompilerParams(vmem_limit_bytes=32 * MIB),
        cost_estimate=BRIEF,
        name="attend_back",
    )(meta, query, grad, kv_a, kv_b, q_index, q_low, lse, delta, cos, sin)


def attended_grad_kernel(gb_ref, w_ref, att_ref, out_ref, delta_ref):
    grad = dot(gb_ref[...], w_ref[...], NT).astype(BF16)
    out_ref[...] = grad
    term = grad.astype(F32) * att_ref[...].astype(F32)
    delta_ref[0] = jnp.broadcast_to(jnp.sum(term.T, axis=0, keepdims=True), delta_ref.shape[1:])


def attended_grad(grad_branch, weight, attended):
    rows, depth = grad_branch.shape
    width = weight.shape[0]
    return pl.pallas_call(
        attended_grad_kernel,
        grid=(width // HD,),
        in_specs=[
            pl.BlockSpec((rows, depth), lambda i: (0, 0)),
            pl.BlockSpec((HD, depth), lambda i: (i, 0)),
            pl.BlockSpec((rows, HD), lambda i: (0, i)),
        ],
        out_specs=[pl.BlockSpec((rows, HD), lambda i: (0, i)), pl.BlockSpec((1, 8, rows), lambda i: (i, 0, 0))],
        out_shape=[
            jax.ShapeDtypeStruct((rows, width), BF16),
            jax.ShapeDtypeStruct((width // HD, 8, rows), F32),
        ],
        compiler_params=pltpu.CompilerParams(vmem_limit_bytes=12 * MIB),
        cost_estimate=BRIEF,
        name="attended_grad",
    )(grad_branch, weight, attended)


def product(lefts, rights, dims):
    cut = lefts[0].shape[0] // 2
    keep = sum(dot(left[:cut], right, dims) for left, right in zip(lefts, rights))
    send = sum(dot(left[cut:], right, dims) for left, right in zip(lefts, rights))
    return keep.astype(BF16), send.astype(BF16)


def project_kernel(x_ref, w_ref, cos_ref, sin_ref, out_ref):
    raw = dot(x_ref[...], w_ref[...])
    cos, sin = cos_ref[...], sin_ref[...]
    mid = HD // 2
    former, latter = raw[:, :mid], raw[:, mid:]
    out_ref[:, :mid] = (former * cos - latter * sin).astype(BF16)
    out_ref[:, mid:] = (latter * cos + former * sin).astype(BF16)


def project_rotate(latent, weight, cos, sin):
    rows, rank = latent.shape
    width = weight.shape[1]
    whole = lambda *shape: pl.BlockSpec(shape, lambda i: (0,) * len(shape))
    return pl.pallas_call(
        project_kernel,
        grid=(width // HD,),
        in_specs=[
            whole(rows, rank),
            pl.BlockSpec((rank, HD), lambda i: (0, i)),
            whole(rows, HD // 2),
            whole(rows, HD // 2),
        ],
        out_specs=pl.BlockSpec((rows, HD), lambda i: (0, i)),
        out_shape=jax.ShapeDtypeStruct((rows, width), BF16),
        compiler_params=pltpu.CompilerParams(vmem_limit_bytes=10 * MIB),
        cost_estimate=BRIEF,
        name="project_rotate",
    )(latent, weight, cos, sin)


def hidden_kernel(x_ref, gate_ref, up_ref, gh_ref, hidden_ref, hidden_t_ref, gg_ref, gu_ref, gate_s, up_s):
    step = pl.program_id(0)
    gate = dot(x_ref[...], gate_ref[...])
    up = dot(x_ref[...], up_ref[...])

    @pl.when(step == 0)
    def _():
        gate_s[...] = gate
        up_s[...] = up

    @pl.when(step > 0)
    def _():
        gate_s[...] += gate
        up_s[...] += up

    @pl.when(step == pl.num_programs(0) - 1)
    def _():
        for first in range(0, gate_s.shape[0], 128):
            at = slice(first, first + 128)
            gate_pre, up_pre, grad = gate_s[at, :], up_s[at, :], gh_ref[at, :]
            sigmoid = jax.nn.sigmoid(gate_pre)
            silu = gate_pre * sigmoid
            hidden = (silu * up_pre).astype(BF16)
            hidden_ref[at, :] = hidden
            hidden_t_ref[:, at] = hidden.T
            gg_ref[at, :] = (grad * up_pre * sigmoid * (1.0 + gate_pre * (1.0 - sigmoid))).astype(BF16)
            gu_ref[at, :] = (grad * silu).astype(BF16)


def hidden_units(normed, gate_weight, up_weight, grad_hidden):
    rows, depth = normed.shape
    units = gate_weight.shape[1]
    cut = 512
    whole = lambda *shape: pl.BlockSpec(shape, lambda i: (0,) * len(shape))
    weight = pl.BlockSpec((cut, units), lambda i: (i, 0))
    plain = jax.ShapeDtypeStruct((rows, units), BF16)
    return pl.pallas_call(
        hidden_kernel,
        grid=(depth // cut,),
        in_specs=[pl.BlockSpec((rows, cut), lambda i: (0, i)), weight, weight, whole(rows, units)],
        out_specs=[whole(rows, units), whole(units, rows), whole(rows, units), whole(rows, units)],
        out_shape=[plain, jax.ShapeDtypeStruct((units, rows), BF16), plain, plain],
        scratch_shapes=[pltpu.VMEM((rows, units), F32), pltpu.VMEM((rows, units), F32)],
        compiler_params=pltpu.CompilerParams(vmem_limit_bytes=36 * MIB),
        cost_estimate=BRIEF,
        name="hidden_units",
    )(normed, gate_weight, up_weight, grad_hidden)


def in_order(values, owner, axis):
    return jnp.stack(
        [at_index(values, owner[j], axis, keepdims=False) for j in range(owner.shape[0])]
    )


def rows_kernel(owner, left_ref, *refs):
    count = len(refs) // 2
    left = left_ref[...]
    for right_ref, out_ref in zip(refs[:count], refs[count:]):
        out_ref[0] = dot(left, right_ref[...], TN).astype(BF16)


def grad_by_rows(owner, left, rights, count):
    slots = owner.shape[0]
    rows, width = left.shape
    cut = width // count
    if cut % 128:
        return [in_order(dot(left, r, TN).astype(BF16).reshape(count, cut, -1), owner, 0) for r in rights]
    return pl.pallas_call(
        rows_kernel,
        grid_spec=pltpu.PrefetchScalarGridSpec(
            num_scalar_prefetch=1,
            grid=(slots,),
            in_specs=[pl.BlockSpec((rows, cut), lambda i, o: (0, o[i]))]
            + [pl.BlockSpec(r.shape, lambda i, o: (0, 0)) for r in rights],
            out_specs=[pl.BlockSpec((1, cut, r.shape[1]), lambda i, o: (i, 0, 0)) for r in rights],
        ),
        out_shape=[jax.ShapeDtypeStruct((slots, cut, r.shape[1]), BF16) for r in rights],
        compiler_params=pltpu.CompilerParams(vmem_limit_bytes=16 * MIB),
        cost_estimate=BRIEF,
        name="grad_by_rows",
    )(owner, left, *rights)


def columns_kernel(owner, left_ref, right_ref, out_ref):
    out_ref[0] = dot(left_ref[...], right_ref[...]).astype(BF16)


def grad_by_columns(owner, left_t, right, count):
    slots = owner.shape[0]
    rows, width = right.shape
    cut = width // count
    tall = left_t.shape[0]
    if cut % 128:
        return in_order(dot(left_t, right).astype(BF16).reshape(tall, count, cut), owner, 1)
    return pl.pallas_call(
        columns_kernel,
        grid_spec=pltpu.PrefetchScalarGridSpec(
            num_scalar_prefetch=1,
            grid=(slots,),
            in_specs=[
                pl.BlockSpec((tall, rows), lambda i, o: (0, 0)),
                pl.BlockSpec((rows, cut), lambda i, o: (0, o[i])),
            ],
            out_specs=pl.BlockSpec((1, tall, cut), lambda i, o: (i, 0, 0)),
        ),
        out_shape=jax.ShapeDtypeStruct((slots, tall, cut), BF16),
        compiler_params=pltpu.CompilerParams(vmem_limit_bytes=16 * MIB),
        cost_estimate=BRIEF,
        name="grad_by_columns",
    )(owner, left_t, right)


def add(*parts):
    total = parts[0].astype(F32)
    for part in parts[1:]:
        total = total + part.astype(F32)
    return total


def near(values):
    return lax.ppermute(values, "tensor", [(i, i ^ 1) for i in range(4)])


def far(values):
    return lax.ppermute(values, "tensor", [(i, i ^ 2) for i in range(4)])


def ring_order(count):
    return list(range(0, count, 2)) + list(range(count - 1, 0, -2))


def ring_shift(values, step, count):
    order = ring_order(count)
    return lax.ppermute(
        values, "seq", [(order[i], order[(i + step) % count]) for i in range(count)]
    )


def seq_at(place, count):
    return jnp.where(place < count // 2, 2 * place, 2 * (count - 1 - place) + 1)


def swap_seq(values, bit, count):
    return lax.ppermute(values, "seq", [(i, i ^ bit) for i in range(count)])


def bits_of(count, first=1):
    bits = [1 << i for i in range(count.bit_length() - 1)]
    return [first] + [b for b in bits if b != first]


def apart_of(bits):
    apart = [0]
    for bit in reversed(bits):
        apart = apart + [bit | a for a in apart]
    return apart


class Order:
    def __init__(self):
        self.last = ()

    def after(self, *values):
        held = lax.optimization_barrier((values, self.last))[0]
        return held if len(values) > 1 else held[0]

    def ran(self, *values):
        self.last = values

    def wait(self, *values):
        self.last = self.last + values


class Halving:
    def __init__(self, order, bits, count, send, *keep):
        self.order, self.bits, self.count = order, list(bits), count
        self.terms = list(keep)
        self.moving = swap_seq(send, self.bits.pop(0), count)

    def keep(self, *values):
        self.terms += values

    def hop(self, go=True):
        arrived = self.order.after(self.moving)
        self.terms.append(arrived)
        cut = arrived.shape[0] // 2
        send = add(*[t[cut:] for t in self.terms]).astype(BF16)
        self.terms = [t[:cut] for t in self.terms]
        self.order.ran(send)
        self.send = send
        if go:
            self.moving = swap_seq(send, self.bits.pop(0), self.count)

    def go(self):
        self.moving = swap_seq(self.order.after(self.send), self.bits.pop(0), self.count)

    def finish(self):
        while self.bits:
            self.hop()
        arrived = self.order.after(self.moving)
        total = add(*[t[0] for t in self.terms], arrived[0])
        self.order.ran(total)
        return total


def swap(values):
    cut = values.shape[0] // 2
    return jnp.concatenate([values[cut:], values[:cut]], axis=0)


def body(
    block_input, lengths, norm1_gain, q_down, q_gain, q_up, kv_weight, out_weight, norm2_gain,
    gate_weight, up_weight, down_weight, cotangent,
):
    group = lax.axis_size("tensor")
    count = lax.axis_size("seq")
    mine = lax.axis_index("tensor").astype(jnp.int32)
    seq = lax.axis_index("seq").astype(jnp.int32)
    own = block_input.shape[0]
    rows = own * group
    heads = q_up.shape[1] // HD
    place = jnp.where((seq & 1) == 0, seq >> 1, count - 1 - (seq >> 1))

    starts = [jnp.int32(0)]
    for i in range(lengths.shape[0] - 1):
        starts.append(starts[-1] + lengths[i])
    blocks = mine ^ jnp.array([0, 2, 1, 3], jnp.int32)
    token = (seq * rows + blocks[:, None] * own + jnp.arange(own, dtype=jnp.int32)[None, :]).reshape(rows)
    low = first_of_segment(token, starts)
    cos_own, sin_own = angles((token - low)[:own].astype(F32))
    offsets = [0]
    for step in range(1, count // 2):
        offsets += [-step, step]
    offsets.append(count // 2)
    slot_seq = seq_at((place + jnp.array(offsets, jnp.int32)) & (count - 1), count)
    ends = first_of_segment(jnp.stack([seq * rows, seq * rows + rows - 1]), starts)
    base = slot_seq * rows
    needed = (slot_seq <= seq) & (slot_seq >= lax.div(ends[0], jnp.int32(rows)))
    bounded = (slot_seq == seq) | (base < ends[1])
    bits, bits_two = bits_of(count), bits_of(count, 2)
    apart = slot_seq ^ seq
    slot_out = sum(((apart >> (bit.bit_length() - 1)) & 1) << (len(bits) - 1 - i) for i, bit in enumerate(bits))
    meta = jnp.stack([base, needed * (1 + bounded), jnp.full((count,), mine), slot_out]).astype(jnp.int32)
    q_index = jnp.broadcast_to(token[None, :], (8, rows))
    q_low = jnp.broadcast_to(low[None, :], (8, rows))
    owner = seq ^ jnp.array(apart_of(bits), jnp.int32)
    owner_two = seq ^ jnp.array(apart_of(bits_two), jnp.int32)

    order = Order()
    half = count // 2

    inputs = block_input.astype(F32)
    scaled_one, inverse_one = rms_parts(inputs)
    normed = (scaled_one * norm1_gain).astype(BF16)
    kv_raw = dot(normed, kv_weight)
    mid = HD // 2
    former, latter = kv_raw[:, :mid], kv_raw[:, mid:HD]
    keyval = jnp.concatenate(
        [
            former * cos_own - latter * sin_own,
            latter * cos_own + former * sin_own,
            kv_raw[:, HD:],
        ],
        axis=1,
    ).astype(BF16)
    order.ran(keyval)
    keyval_far = far(keyval)
    compressed = dot(order.after(normed), q_down)
    latent = (rms_parts(compressed)[0] * q_gain).astype(BF16)
    order.ran(latent)
    latent_far = far(latent)
    pair = jnp.concatenate([keyval, order.after(keyval_far)], axis=0)
    order.ran(pair)
    ahead, back = ring_shift(pair, 1, count), ring_shift(pair, -1, count)
    pair_near = near(pair)
    cos, sin = angles((order.after(token) - low).astype(F32))
    order.ran(cos, sin)
    latent_half = jnp.concatenate([latent, order.after(latent_far)], axis=0)
    order.ran(latent_half)
    latent_near = near(latent_half)
    input_far = far(order.after(block_input))
    grad_far = far(order.after(cotangent))
    kv_a = jnp.zeros((count,) + pair.shape, BF16)
    kv_b = jnp.zeros((count,) + pair.shape, BF16)

    def put(kept, piece, slot):
        return lax.dynamic_update_slice(kept, piece, (slot, 0, 0))

    kv_a, kv_b = put(kv_a, pair[None], 0), put(kv_b, order.after(pair_near)[None], 0)
    for step in range(1, half + 1):
        ahead, back = order.after(ahead, back)
        slot = 2 * step - 1
        if step < half:
            piece = jnp.stack([ahead, back])
            order.ran(ahead, back)
            if step < half - 1:
                ahead, back = ring_shift(ahead, 1, count), ring_shift(back, -1, count)
            else:
                ahead, back = ring_shift(ahead[:own], 1, count), ring_shift(back[own:], -1, count)
        else:
            piece = jnp.concatenate([ahead, back], axis=0)[None]
        piece_near = near(order.after(piece))
        kv_a = put(kv_a, piece, slot)
        if step == 1:
            latent_all = jnp.concatenate([latent_half, order.after(latent_near)], axis=0)
            query = project_rotate(latent_all, q_up, cos, sin)
            order.ran(query)
        if step == half - 1:
            input_half = jnp.concatenate([block_input, order.after(input_far)], axis=0)
            order.ran(input_half)
        if step == half:
            grad_half = jnp.concatenate([cotangent, order.after(grad_far)], axis=0)
            order.ran(grad_half)
            grad_near = near(grad_half)
        kv_b = put(kv_b, order.after(piece_near), slot)
    kv_a, kv_b = order.after(kv_a, kv_b)
    attended, attended_t, lse = attend(meta, 0, order.after(query), kv_a, kv_b, q_index, q_low, (), True)
    order.ran(attended)

    def sum_half(lefts, rights, dims, meanwhile):
        lefts[0] = order.after(lefts[0])
        keep, send = product(lefts, rights, dims)
        order.ran(send)
        chip = add(keep, order.after(near(send))).astype(BF16)
        order.ran(chip)
        moving = far(swap(chip))
        made = meanwhile()
        return add(chip, order.after(moving)), made

    share = q_down.shape[0] // (count * group)

    def before_residual():
        normed_half = (rms_parts(order.after(input_half).astype(F32))[0] * norm1_gain).astype(BF16)
        scaled_q, inverse_q = rms_parts(dot(normed_half, q_down))
        order.ran(scaled_q)

        def picked(which):
            blocks = normed_half.reshape(2 * own, count, group, share)
            return at_index(blocks, which, 2, keepdims=False).reshape(2 * own, count * share)

        picked_near = near(picked(mine ^ 1))
        grad_all = jnp.concatenate([grad_half, order.after(grad_near)], axis=0)
        grad_hidden = dot(grad_all, down_weight, NT)
        order.ran(grad_hidden)
        picked_all = jnp.concatenate([picked(mine), order.after(picked_near)], axis=0)
        order.ran(picked_all)
        return scaled_q, inverse_q, picked_all, grad_all, grad_hidden

    branch, (scaled_q, inverse_q, picked, grad_all, grad_hidden) = sum_half(
        [attended], [out_weight], NN, before_residual
    )
    residual = input_half.astype(F32) + branch
    scaled_two, inverse_two = rms_parts(residual)
    normed_half = (scaled_two * norm2_gain).astype(BF16)
    order.ran(normed_half)
    normed_two = jnp.concatenate([normed_half, order.after(near(normed_half))], axis=0)

    hidden, hidden_t, grad_gate, grad_up = hidden_units(normed_two, gate_weight, up_weight, grad_hidden)
    order.ran(hidden)

    send = grad_by_columns(owner[half:], order.after(hidden_t), grad_all, count)
    order.ran(send)
    down_sum = Halving(order, bits, count, send)
    keep = grad_by_columns(owner[:half], order.after(hidden_t), grad_all, count)
    order.ran(keep)
    down_sum.keep(keep)

    [send] = grad_by_rows(owner_two[half:], order.after(normed_two), [grad_up], count)
    order.ran(send)
    up_sum = Halving(order, bits_two, count, send)
    [keep] = grad_by_rows(owner_two[:half], order.after(normed_two), [grad_up], count)
    order.ran(keep)
    up_sum.keep(keep)

    def after_feed():
        keep, send = product([order.after(hidden)], [down_weight], NN)
        order.ran(send)
        feed_chip = add(keep, order.after(near(send))).astype(BF16)
        order.ran(feed_chip)
        return feed_chip

    back_two, feed_chip = sum_half([grad_gate, grad_up], [gate_weight, up_weight], NT, after_feed)
    grad_residual = grad_half.astype(F32) + rms_back(back_two, scaled_two, inverse_two, norm2_gain)
    branch_half = grad_residual.astype(BF16)
    order.ran(branch_half)
    branch_near = near(branch_half)
    feed_far = far(order.after(feed_chip)[own:])

    [send] = grad_by_rows(owner[half:], order.after(normed_two), [grad_gate], count)
    order.ran(send)
    gate_sum = Halving(order, bits, count, send)
    grad_branch = jnp.concatenate([branch_half, order.after(branch_near)], axis=0)
    grad_attended, delta = attended_grad(grad_branch, out_weight, attended)
    order.ran(grad_attended)
    send_out = grad_by_columns(owner[half:], order.after(attended_t), grad_branch, count)
    order.ran(send_out)
    down_sum.hop()
    [keep] = grad_by_rows(owner[:half], order.after(normed_two), [grad_gate], count)
    order.ran(keep)
    gate_sum.keep(keep)
    up_sum.hop(go=False)

    grad_query_raw, dkv_a, dkv_b = attend_back(
        meta, query, order.after(grad_attended), kv_a, kv_b, q_index, q_low, lse, delta, cos, sin
    )
    order.ran(grad_query_raw)
    dkv_near = near(dkv_b)

    latent_keep, latent_send = product([order.after(grad_query_raw)], [q_up], NT)
    order.ran(latent_send)
    latent_near = near(latent_send)
    down_sum.hop()
    gate_sum.hop()
    up_sum.go()
    chip_kv = add(dkv_a, order.after(dkv_near)).astype(BF16)
    order.ran(chip_kv)
    kv_far = far(chip_kv[:, own:])
    latent_chip = add(latent_keep, order.after(latent_near)).astype(BF16)
    order.ran(latent_chip)
    latent_far = far(swap(latent_chip))
    feed_out = add(feed_chip[:own], order.after(feed_far))
    block_output = (residual[:own] + feed_out).astype(BF16)
    order.ran(block_output)
    keep = grad_by_columns(owner[:half], order.after(attended_t), grad_branch, count)
    order.ran(keep)
    out_sum = Halving(order, bits, count, order.after(send_out), keep)
    [send_query] = grad_by_rows(owner[half:], order.after(latent_all), [grad_query_raw], count)
    order.ran(send_query)
    [keep_query] = grad_by_rows(owner[:half], order.after(latent_all), [grad_query_raw], count)
    order.ran(keep_query)

    chips_kv = add(chip_kv[:, :own], order.after(kv_far)).astype(BF16)
    order.ran(chips_kv)
    kv_sum = Halving(order, bits, count, chips_kv[half:], chips_kv[:half])
    up_sum.hop()

    grad_latent = add(latent_chip, order.after(latent_far))
    grad_compressed = rms_back(grad_latent, scaled_q, inverse_q, q_gain).astype(BF16)
    order.ran(grad_compressed)
    compressed_near = near(grad_compressed)
    down_grad = down_sum.finish()
    kv_sum.hop()


    def shared(values, size):
        blocks = values.reshape(count, group, size)
        return at_index(blocks, mine, 1, keepdims=False)

    compressed_all = jnp.concatenate([grad_compressed, order.after(compressed_near)], axis=0)
    q_down_parts = dot(picked, compressed_all, TN).astype(BF16).reshape(count, share, -1)
    order.ran(q_down_parts)
    q_down_parts = in_order(q_down_parts, owner, 0)
    q_down_sum = Halving(order, bits, count, q_down_parts[half:], q_down_parts[:half])

    out_sum.hop()
    query_sum = Halving(order, bits, count, order.after(send_query), keep_query)
    kv_sum.hop()
    gate_sum.hop()
    up_grad = up_sum.finish()
    kv_own = kv_sum.finish()
    former, latter = kv_own[:, :mid], kv_own[:, mid:HD]
    grad_kv_raw = jnp.concatenate(
        [
            former * cos_own + latter * sin_own,
            latter * cos_own - former * sin_own,
            kv_own[:, HD:],
        ],
        axis=1,
    ).astype(BF16)
    order.ran(grad_kv_raw)
    kv_raw_far = far(grad_kv_raw)
    grad_normed = dot(grad_compressed[:own], q_down, NT) + dot(order.after(grad_kv_raw), kv_weight, NT)
    input_grad = grad_residual[:own] + rms_back(grad_normed, scaled_one, inverse_one, norm1_gain)
    gain_one = jnp.sum(grad_normed * scaled_one, axis=0)
    order.ran(input_grad, gain_one)
    gain_far = far(gain_one)
    kv_half = jnp.concatenate([grad_kv_raw, order.after(kv_raw_far)], axis=0)
    order.ran(kv_half)
    kv_half_near = near(kv_half)
    gain_one = gain_one + order.after(gain_far)
    gain_two = jnp.sum(back_two * scaled_two, axis=0)
    gain_q = jnp.sum(grad_latent * scaled_q, axis=0)
    gains = jnp.concatenate([gain_one, gain_two, gain_q])
    order.ran(gains)
    gains_near = near(gains)
    kv_parts = dot(
        picked, jnp.concatenate([kv_half, order.after(kv_half_near)], axis=0), TN
    ).astype(BF16).reshape(count, share, -1)
    order.ran(kv_parts)
    kv_parts = in_order(kv_parts, owner, 0)
    kv_weight_sum = Halving(order, bits, count, kv_parts[half:], kv_parts[:half])
    gains = gains + order.after(gains_near)
    width = block_input.shape[1]
    gains = jnp.concatenate(
        [
            shared(gains[:width], share),
            shared(gains[width : 2 * width], share),
            shared(gains[2 * width :], q_gain.shape[0] // (count * group)),
        ],
        axis=1,
    )
    order.ran(gains)
    gains = in_order(gains, owner, 0)[:, None, :]
    gains_sum = Halving(order, bits, count, gains[half:], gains[:half])
    q_down_sum.hop()
    query_sum.hop()
    kv_weight_sum.hop()
    gains_sum.hop()
    out_sum.hop()
    gate_grad = gate_sum.finish()
    q_down_sum.hop()
    kv_weight_sum.hop()
    gains_sum.hop()
    query_sum.hop()
    out_weight_grad = out_sum.finish()
    q_down_grad = q_down_sum.finish()
    kv_weight_grad = kv_weight_sum.finish()
    gains = gains_sum.finish()[0]
    q_up_grad = query_sum.finish()
    return (
        block_output,
        input_grad,
        gains[:share],
        q_down_grad,
        gains[2 * share :],
        q_up_grad,
        kv_weight_grad,
        out_weight_grad,
        gains[share : 2 * share],
        gate_grad,
        up_grad,
        down_grad,
    )


def solution(mesh):
    both = P(("seq", "tensor"))
    rows = P(("seq", "tensor"), None)
    return jax.shard_map(
        body,
        mesh=mesh,
        in_specs=(
            rows, P(), P(), P(), P(), P(None, "tensor"), P(), P("tensor", None), P(),
            P(None, "tensor"), P(None, "tensor"), P("tensor", None), rows,
        ),
        out_specs=(
            rows, rows, both, rows, both, P("seq", "tensor"), rows, P("tensor", "seq"), both,
            P("seq", "tensor"), P("seq", "tensor"), P("tensor", "seq"),
        ),
        check_vma=False,
    )
```

```python
import functools
import math

import jax
import jax.numpy as jnp
from jax import lax
from jax.experimental import pallas as pl
from jax.experimental.pallas import tpu as pltpu
from jax.sharding import PartitionSpec as P

HD = 256
EPS = 1e-06
NEG = -1e30
F32 = jnp.float32
BF16 = jnp.bfloat16
LOG2_SCALE = math.log2(math.e) / math.sqrt(HD)
SCALE = 1.0 / math.sqrt(HD)
MIB = 1 << 20
BRIEF = pl.CostEstimate(flops=1000, bytes_accessed=1000, transcendentals=0)

NN = (((1,), (0,)), ((), ()))
NT = (((1,), (1,)), ((), ()))
TN = (((0,), (0,)), ((), ()))


def dot(left, right, dims=NN):
    return lax.dot_general(left, right, dims, preferred_element_type=F32)


def at_index(values, index, axis, keepdims=True):
    start = [jnp.int32(0)] * values.ndim
    start[axis] = index
    size = values.shape[:axis] + (1,) + values.shape[axis + 1 :]
    taken = lax.dynamic_slice(values, start, size, allow_negative_indices=False)
    return taken if keepdims else lax.squeeze(taken, [axis])


def rms_parts(values):
    inverse = lax.rsqrt(jnp.mean(values * values, axis=-1, keepdims=True) + EPS)
    return values * inverse, inverse


def rms_back(grad_out, scaled, inverse, gain):
    inner = grad_out * gain
    return inverse * (inner - scaled * jnp.mean(inner * scaled, axis=-1, keepdims=True))


def place_in_kernel():
    return lax.axis_index("seq").astype(jnp.int32), lax.axis_index("tensor").astype(jnp.int32)


def group_block(row, own):
    block = lax.div(row, jnp.int32(own))
    return ((block & 1) << 1) | (block >> 1), row - block * own


def first_in_kernel(token, lengths):
    found = jnp.zeros_like(token)
    start = jnp.int32(0)
    for i in range(lengths.shape[0] - 1):
        start = start + lengths[i]
        found = jnp.maximum(found, jnp.where(token >= start, start, 0))
    return found


def angles_in_kernel(rows, own, lengths, freq_ref):
    seq, mine = place_in_kernel()
    other, within = group_block(lax.broadcasted_iota(jnp.int32, (rows, HD // 2), 0), own)
    token = seq * (4 * own) + (mine ^ other) * own + within
    theta = (token - first_in_kernel(token, lengths)).astype(F32) * freq_ref[0:1, :]
    return jnp.cos(theta), jnp.sin(theta)


def slot_of(slot, count, seq):
    place = jnp.where((seq & 1) == 0, seq >> 1, count - 1 - (seq >> 1))
    step = (slot + 1) >> 1
    place = (place + jnp.where((slot & 1) == 1, -step, step)) & (count - 1)
    return seq_at(place, count)


def slot_state(lengths, slot, count, rows):
    seq, _ = place_in_kernel()
    source = slot_of(slot, count, seq)
    first = first_in_kernel(seq * rows, lengths)
    last = first_in_kernel(seq * rows + rows - 1, lengths)
    base = source * rows
    needed = (source <= seq) & (source >= lax.div(first, jnp.int32(rows)))
    bounded = (source == seq) | (base < last)
    return base, needed, bounded


def key_bias(lengths, base, keys, rows):
    seq, mine = place_in_kernel()
    own = rows // 4
    other, within = group_block(lax.broadcasted_iota(jnp.int32, (keys, rows), 0), own)
    token = base + (mine ^ other) * own + within
    other, within = group_block(lax.broadcasted_iota(jnp.int32, (8, rows), 1), own)
    query = seq * rows + (mine ^ other) * own + within
    low = first_in_kernel(query, lengths)
    allowed = (token <= query[0:1, :]) & (token >= low[0:1, :])
    return jnp.where(allowed, 0.0, NEG)


def keys_kernel(lengths, x_ref, gain_ref, w_ref, freq_ref, out_ref, normed_ref):
    values = x_ref[...].astype(F32)
    inverse = lax.rsqrt(jnp.mean(values * values, axis=-1, keepdims=True) + EPS)
    normed = (values * inverse * gain_ref[...]).astype(BF16)
    normed_ref[...] = normed
    raw = dot(normed, w_ref[...])
    cos, sin = angles_in_kernel(x_ref.shape[0], x_ref.shape[0], lengths, freq_ref)
    mid = HD // 2
    former, latter = raw[:, :mid], raw[:, mid:HD]
    out_ref[:, :mid] = (former * cos - latter * sin).astype(BF16)
    out_ref[:, mid:HD] = (latter * cos + former * sin).astype(BF16)
    out_ref[:, HD:] = raw[:, HD:].astype(BF16)


def own_keys(lengths, values, gain, weight, freq):
    own, depth = values.shape
    whole = lambda *shape: pl.BlockSpec(shape, lambda i, m: (0,) * len(shape))
    return pl.pallas_call(
        keys_kernel,
        grid_spec=pltpu.PrefetchScalarGridSpec(
            num_scalar_prefetch=1,
            grid=(1,),
            in_specs=[whole(own, depth), whole(1, depth), whole(*weight.shape), whole(1, HD // 2)],
            out_specs=[whole(own, 2 * HD), whole(own, depth)],
        ),
        out_shape=[jax.ShapeDtypeStruct((own, 2 * HD), BF16), jax.ShapeDtypeStruct((own, depth), BF16)],
        compiler_params=pltpu.CompilerParams(vmem_limit_bytes=16 * MIB),
        cost_estimate=BRIEF,
        name="own_keys",
    )(lengths, values, gain, weight, freq)


def fwd_kernel(heads, lengths, q_ref, a_ref, b_ref, o_ref, ot_ref, lse_ref, m_s, l_s, acc_s, bias_s):
    slot = pl.program_id(0)
    count = pl.num_programs(0)
    keys, rows = bias_s.shape
    base, needed, bounded = slot_state(lengths, slot, count, rows)

    @pl.when(slot == 0)
    def _():
        m_s[...] = jnp.full_like(m_s, NEG)
        l_s[...] = jnp.zeros_like(l_s)
        acc_s[...] = jnp.zeros_like(acc_s)

    def tile(masked):
        key = jnp.concatenate([a_ref[0, :, :HD], b_ref[0, :, :HD]], axis=0)
        value = jnp.concatenate([a_ref[0, :, HD:], b_ref[0, :, HD:]], axis=0)
        value_t = value.T
        if masked:
            bias_s[...] = key_bias(lengths, base, keys, rows)

        def score(h):
            return dot(key, q_ref[:, h * HD : (h + 1) * HD], NT)

        following = score(0)
        for h in range(heads):
            scores = following * LOG2_SCALE
            if h + 1 < heads:
                following = score(h + 1)
            if masked:
                scores = scores + bias_s[...]
            old = m_s[h, 0:1, :]
            new = jnp.maximum(old, jnp.max(scores, axis=0, keepdims=True))
            alpha = jnp.exp2(old - new)
            weight = jnp.exp2(scores - new)
            l_s[h, 0:1, :] = l_s[h, 0:1, :] * alpha + jnp.sum(weight, axis=0, keepdims=True)
            m_s[h, 0:1, :] = new
            acc_s[h] = acc_s[h] * alpha + dot(value_t, weight.astype(BF16))

    pl.when(needed & ~bounded)(lambda: tile(False))
    pl.when(needed & bounded)(lambda: tile(True))

    @pl.when(slot == count - 1)
    def _():
        for h in range(heads):
            total = l_s[h, 0:1, :]
            out_t = (acc_s[h] / total).astype(BF16)
            ot_ref[h * HD : (h + 1) * HD, :] = out_t
            o_ref[:, h * HD : (h + 1) * HD] = out_t.T
            lse_ref[h] = jnp.broadcast_to(m_s[h, 0:1, :] + jnp.log2(total), lse_ref.shape[1:])


def attend(lengths, query, kv_a, kv_b):
    rows, width = query.shape
    heads = width // HD
    slots, half, wide = kv_a.shape
    keys = 2 * half
    whole = lambda *shape: pl.BlockSpec(shape, lambda i, m: (0,) * len(shape))
    tile = pl.BlockSpec((1, half, wide), lambda i, m: (i, 0, 0))
    state = [(heads, 8, rows), (heads, 8, rows), (heads, HD, rows), (keys, rows)]
    out = [((rows, width), BF16), ((width, rows), BF16), ((heads, 8, rows), F32)]
    return pl.pallas_call(
        functools.partial(fwd_kernel, heads),
        grid_spec=pltpu.PrefetchScalarGridSpec(
            num_scalar_prefetch=1,
            grid=(slots,),
            in_specs=[whole(rows, width), tile, tile],
            out_specs=[whole(*shape) for shape, _ in out],
            scratch_shapes=[pltpu.VMEM(shape, F32) for shape in state],
        ),
        out_shape=[jax.ShapeDtypeStruct(*o) for o in out],
        compiler_params=pltpu.CompilerParams(vmem_limit_bytes=24 * MIB),
        cost_estimate=BRIEF,
        name="attend",
    )(lengths, query, kv_a, kv_b)


def bwd_kernel(heads, lengths, _, q_ref, do_ref, a_ref, b_ref, lse_ref, delta_ref, cos_ref, sin_ref,
               dq_ref, da_ref, db_ref, dq_s, dk_s, dv_s, bias_s):
    slot = pl.program_id(0)
    keys, rows = bias_s.shape
    base, needed, bounded = slot_state(lengths, slot, pl.num_programs(0), rows)
    half = a_ref.shape[1]

    @pl.when(slot == 0)
    def _():
        dq_s[...] = jnp.zeros_like(dq_s)

    @pl.when(~needed)
    def _():
        da_ref[...] = jnp.zeros_like(da_ref)
        db_ref[...] = jnp.zeros_like(db_ref)

    def tile(masked):
        key = jnp.concatenate([a_ref[0, :, :HD], b_ref[0, :, :HD]], axis=0)
        value = jnp.concatenate([a_ref[0, :, HD:], b_ref[0, :, HD:]], axis=0)
        key_t = key.T
        if masked:
            bias_s[...] = key_bias(lengths, base, keys, rows)
        for h in range(heads):
            at = slice(h * HD, (h + 1) * HD)
            scores = dot(key, q_ref[:, at], NT) * LOG2_SCALE
            if masked:
                scores = scores + bias_s[...]
            weight = jnp.exp2(scores - lse_ref[h, 0:1, :])
            grad = dot(value, do_ref[:, at], NT)
            ds = (weight * (grad - delta_ref[h, 0:1, :])).astype(BF16)
            dv = dot(weight.astype(BF16), do_ref[:, at])
            dk = dot(ds, q_ref[:, at])
            if h == 0:
                dv_s[...] = dv
                dk_s[...] = dk
            else:
                dv_s[...] += dv
                dk_s[...] += dk
            dq_s[h] += dot(key_t, ds)
        da_ref[0, :, :HD] = (dk_s[:half, :] * SCALE).astype(BF16)
        db_ref[0, :, :HD] = (dk_s[half:, :] * SCALE).astype(BF16)
        da_ref[0, :, HD:] = dv_s[:half, :].astype(BF16)
        db_ref[0, :, HD:] = dv_s[half:, :].astype(BF16)

    pl.when(needed & ~bounded)(lambda: tile(False))
    pl.when(needed & bounded)(lambda: tile(True))

    @pl.when(slot == pl.num_programs(0) - 1)
    def _():
        cos, sin = cos_ref[...], sin_ref[...]
        mid = HD // 2
        for h in range(heads):
            grad = (dq_s[h] * SCALE).T
            former, latter = grad[:, :mid], grad[:, mid:]
            dq_ref[:, h * HD : h * HD + mid] = (former * cos + latter * sin).astype(BF16)
            dq_ref[:, h * HD + mid : (h + 1) * HD] = (latter * cos - former * sin).astype(BF16)


def attend_back(lengths, slot_out, query, grad, kv_a, kv_b, lse, delta, cos, sin):
    rows, width = query.shape
    heads = width // HD
    slots, half, wide = kv_a.shape
    keys = 2 * half
    whole = lambda *shape: pl.BlockSpec(shape, lambda i, m, o: (0,) * len(shape))
    tile = pl.BlockSpec((1, half, wide), lambda i, m, o: (i, 0, 0))
    out_tile = pl.BlockSpec((1, half, wide), lambda i, m, o: (o[i], 0, 0))
    return pl.pallas_call(
        functools.partial(bwd_kernel, heads),
        grid_spec=pltpu.PrefetchScalarGridSpec(
            num_scalar_prefetch=2,
            grid=(slots,),
            in_specs=[
                whole(rows, width), whole(rows, width), tile, tile,
                whole(heads, 8, rows), whole(heads, 8, rows), whole(rows, HD // 2), whole(rows, HD // 2),
            ],
            out_specs=[whole(rows, width), out_tile, out_tile],
            scratch_shapes=[
                pltpu.VMEM((heads, HD, rows), F32),
                pltpu.VMEM((keys, HD), F32),
                pltpu.VMEM((keys, HD), F32),
                pltpu.VMEM((keys, rows), F32),
            ],
        ),
        out_shape=[
            jax.ShapeDtypeStruct((rows, width), BF16),
            jax.ShapeDtypeStruct((slots, half, wide), BF16),
            jax.ShapeDtypeStruct((slots, half, wide), BF16),
        ],
        compiler_params=pltpu.CompilerParams(vmem_limit_bytes=32 * MIB),
        cost_estimate=BRIEF,
        name="attend_back",
    )(lengths, slot_out, query, grad, kv_a, kv_b, lse, delta, cos, sin)


def attended_grad_kernel(gb_ref, w_ref, att_ref, out_ref, delta_ref):
    grad = dot(gb_ref[...], w_ref[...], NT).astype(BF16)
    out_ref[...] = grad
    term = grad.astype(F32) * att_ref[...].astype(F32)
    delta_ref[0] = jnp.broadcast_to(jnp.sum(term.T, axis=0, keepdims=True), delta_ref.shape[1:])


def attended_grad(grad_branch, weight, attended):
    rows, depth = grad_branch.shape
    width = weight.shape[0]
    return pl.pallas_call(
        attended_grad_kernel,
        grid=(width // HD,),
        in_specs=[
            pl.BlockSpec((rows, depth), lambda i: (0, 0)),
            pl.BlockSpec((HD, depth), lambda i: (i, 0)),
            pl.BlockSpec((rows, HD), lambda i: (0, i)),
        ],
        out_specs=[pl.BlockSpec((rows, HD), lambda i: (0, i)), pl.BlockSpec((1, 8, rows), lambda i: (i, 0, 0))],
        out_shape=[
            jax.ShapeDtypeStruct((rows, width), BF16),
            jax.ShapeDtypeStruct((width // HD, 8, rows), F32),
        ],
        compiler_params=pltpu.CompilerParams(vmem_limit_bytes=12 * MIB),
        cost_estimate=BRIEF,
        name="attended_grad",
    )(grad_branch, weight, attended)


def product(lefts, rights, dims):
    cut = lefts[0].shape[0] // 2
    keep = sum(dot(left[:cut], right, dims) for left, right in zip(lefts, rights))
    send = sum(dot(left[cut:], right, dims) for left, right in zip(lefts, rights))
    return keep.astype(BF16), send.astype(BF16)


def project_kernel(lengths, x_ref, w_ref, freq_ref, out_ref, cos_ref, sin_ref):
    rows = x_ref.shape[0]

    @pl.when(pl.program_id(0) == 0)
    def _():
        cos_ref[...], sin_ref[...] = angles_in_kernel(rows, rows // 4, lengths, freq_ref)

    raw = dot(x_ref[...], w_ref[...])
    cos, sin = cos_ref[...], sin_ref[...]
    mid = HD // 2
    former, latter = raw[:, :mid], raw[:, mid:]
    out_ref[:, :mid] = (former * cos - latter * sin).astype(BF16)
    out_ref[:, mid:] = (latter * cos + former * sin).astype(BF16)


def project_rotate(lengths, latent, weight, freq):
    rows, rank = latent.shape
    width = weight.shape[1]
    whole = lambda *shape: pl.BlockSpec(shape, lambda i, m: (0,) * len(shape))
    angle = jax.ShapeDtypeStruct((rows, HD // 2), F32)
    return pl.pallas_call(
        project_kernel,
        grid_spec=pltpu.PrefetchScalarGridSpec(
            num_scalar_prefetch=1,
            grid=(width // HD,),
            in_specs=[whole(rows, rank), pl.BlockSpec((rank, HD), lambda i, m: (0, i)), whole(1, HD // 2)],
            out_specs=[
                pl.BlockSpec((rows, HD), lambda i, m: (0, i)), whole(rows, HD // 2), whole(rows, HD // 2),
            ],
        ),
        out_shape=[jax.ShapeDtypeStruct((rows, width), BF16), angle, angle],
        compiler_params=pltpu.CompilerParams(vmem_limit_bytes=10 * MIB),
        cost_estimate=BRIEF,
        name="project_rotate",
    )(lengths, latent, weight, freq)


def hidden_kernel(x_ref, gate_ref, up_ref, gh_ref, hidden_ref, hidden_t_ref, gg_ref, gu_ref, gate_s, up_s):
    step = pl.program_id(0)
    gate = dot(x_ref[...], gate_ref[...])
    up = dot(x_ref[...], up_ref[...])

    @pl.when(step == 0)
    def _():
        gate_s[...] = gate
        up_s[...] = up

    @pl.when(step > 0)
    def _():
        gate_s[...] += gate
        up_s[...] += up

    @pl.when(step == pl.num_programs(0) - 1)
    def _():
        for first in range(0, gate_s.shape[0], 128):
            at = slice(first, first + 128)
            gate_pre, up_pre, grad = gate_s[at, :], up_s[at, :], gh_ref[at, :]
            sigmoid = jax.nn.sigmoid(gate_pre)
            silu = gate_pre * sigmoid
            hidden = (silu * up_pre).astype(BF16)
            hidden_ref[at, :] = hidden
            hidden_t_ref[:, at] = hidden.T
            gg_ref[at, :] = (grad * up_pre * sigmoid * (1.0 + gate_pre * (1.0 - sigmoid))).astype(BF16)
            gu_ref[at, :] = (grad * silu).astype(BF16)


def hidden_units(normed, gate_weight, up_weight, grad_hidden):
    rows, depth = normed.shape
    units = gate_weight.shape[1]
    cut = 512
    whole = lambda *shape: pl.BlockSpec(shape, lambda i: (0,) * len(shape))
    weight = pl.BlockSpec((cut, units), lambda i: (i, 0))
    plain = jax.ShapeDtypeStruct((rows, units), BF16)
    return pl.pallas_call(
        hidden_kernel,
        grid=(depth // cut,),
        in_specs=[pl.BlockSpec((rows, cut), lambda i: (0, i)), weight, weight, whole(rows, units)],
        out_specs=[whole(rows, units), whole(units, rows), whole(rows, units), whole(rows, units)],
        out_shape=[plain, jax.ShapeDtypeStruct((units, rows), BF16), plain, plain],
        scratch_shapes=[pltpu.VMEM((rows, units), F32), pltpu.VMEM((rows, units), F32)],
        compiler_params=pltpu.CompilerParams(vmem_limit_bytes=36 * MIB),
        cost_estimate=BRIEF,
        name="hidden_units",
    )(normed, gate_weight, up_weight, grad_hidden)


def in_order(values, owner, axis):
    return jnp.stack(
        [at_index(values, owner[j], axis, keepdims=False) for j in range(owner.shape[0])]
    )


def rows_kernel(owner, left_ref, *refs):
    count = len(refs) // 2
    left = left_ref[...]
    for right_ref, out_ref in zip(refs[:count], refs[count:]):
        out_ref[0] = dot(left, right_ref[...], TN).astype(BF16)


def grad_by_rows(owner, left, rights, count):
    slots = owner.shape[0]
    rows, width = left.shape
    cut = width // count
    if cut % 128:
        return [in_order(dot(left, r, TN).astype(BF16).reshape(count, cut, -1), owner, 0) for r in rights]
    return pl.pallas_call(
        rows_kernel,
        grid_spec=pltpu.PrefetchScalarGridSpec(
            num_scalar_prefetch=1,
            grid=(slots,),
            in_specs=[pl.BlockSpec((rows, cut), lambda i, o: (0, o[i]))]
            + [pl.BlockSpec(r.shape, lambda i, o: (0, 0)) for r in rights],
            out_specs=[pl.BlockSpec((1, cut, r.shape[1]), lambda i, o: (i, 0, 0)) for r in rights],
        ),
        out_shape=[jax.ShapeDtypeStruct((slots, cut, r.shape[1]), BF16) for r in rights],
        compiler_params=pltpu.CompilerParams(vmem_limit_bytes=16 * MIB),
        cost_estimate=BRIEF,
        name="grad_by_rows",
    )(owner, left, *rights)


def columns_kernel(owner, left_ref, right_ref, out_ref):
    out_ref[0] = dot(left_ref[...], right_ref[...]).astype(BF16)


def grad_by_columns(owner, left_t, right, count, part=0, parts=1):
    slots = owner.shape[0]
    rows, width = right.shape
    cut = width // count
    tall = left_t.shape[0] // parts
    if cut % 128:
        left_t = left_t[part * tall : (part + 1) * tall]
        return in_order(dot(left_t, right).astype(BF16).reshape(tall, count, cut), owner, 1)
    return pl.pallas_call(
        columns_kernel,
        grid_spec=pltpu.PrefetchScalarGridSpec(
            num_scalar_prefetch=1,
            grid=(slots,),
            in_specs=[
                pl.BlockSpec((tall, rows), lambda i, o: (part, 0)),
                pl.BlockSpec((rows, cut), lambda i, o: (0, o[i])),
            ],
            out_specs=pl.BlockSpec((1, tall, cut), lambda i, o: (i, 0, 0)),
        ),
        out_shape=jax.ShapeDtypeStruct((slots, tall, cut), BF16),
        compiler_params=pltpu.CompilerParams(vmem_limit_bytes=16 * MIB),
        cost_estimate=BRIEF,
        name="grad_by_columns",
    )(owner, left_t, right)


def share_kernel(size, meta, x_ref, mine_ref, other_ref, turned_s):
    turned_s[...] = x_ref[...].astype(F32).T
    mine = meta[1, 0]
    mine_ref[...] = turned_s[pl.ds(pl.multiple_of(mine * size, size), size), :].astype(BF16)
    other_ref[...] = turned_s[pl.ds(pl.multiple_of((mine ^ 1) * size, size), size), :].astype(BF16)


def share_of_columns(owner, mine, values, size, group):
    slots = owner.shape[0]
    rows, width = values.shape
    cut = width // slots
    if cut % 128:
        turned = values.T.reshape(slots, group, size, rows)
        return tuple(
            in_order(at_index(turned, which, 1, keepdims=False), owner, 0).reshape(slots * size, rows)
            for which in (mine, mine ^ 1)
        )
    return pl.pallas_call(
        functools.partial(share_kernel, size),
        grid_spec=pltpu.PrefetchScalarGridSpec(
            num_scalar_prefetch=1,
            grid=(slots,),
            in_specs=[pl.BlockSpec((rows, cut), lambda i, m: (0, m[0, i]))],
            out_specs=[pl.BlockSpec((size, rows), lambda i, m: (i, 0))] * 2,
            scratch_shapes=[pltpu.VMEM((cut, rows), F32)],
        ),
        out_shape=[jax.ShapeDtypeStruct((slots * size, rows), BF16)] * 2,
        compiler_params=pltpu.CompilerParams(vmem_limit_bytes=8 * MIB),
        cost_estimate=BRIEF,
        name="share_of_columns",
    )(jnp.stack([owner, jnp.full((slots,), mine)]), values)


def add(*parts):
    total = parts[0].astype(F32)
    for part in parts[1:]:
        total = total + part.astype(F32)
    return total


def near(values):
    return lax.ppermute(values, "tensor", [(i, i ^ 1) for i in range(4)])


def far(values):
    return lax.ppermute(values, "tensor", [(i, i ^ 2) for i in range(4)])


def ring_order(count):
    return list(range(0, count, 2)) + list(range(count - 1, 0, -2))


def ring_shift(values, step, count):
    order = ring_order(count)
    return lax.ppermute(
        values, "seq", [(order[i], order[(i + step) % count]) for i in range(count)]
    )


def seq_at(place, count):
    return jnp.where(place < count // 2, 2 * place, 2 * (count - 1 - place) + 1)


def swap_seq(values, bit, count):
    return lax.ppermute(values, "seq", [(i, i ^ bit) for i in range(count)])


def bits_of(count, first=1):
    bits = [1 << i for i in range(count.bit_length() - 1)]
    return [first] + [b for b in bits if b != first]


def apart_of(bits):
    apart = [0]
    for bit in reversed(bits):
        apart = apart + [bit | a for a in apart]
    return apart


class Order:
    def __init__(self):
        self.last = ()

    def after(self, *values):
        held = lax.optimization_barrier((values, self.last))[0]
        return held if len(values) > 1 else held[0]

    def ran(self, *values):
        self.last = values

    def wait(self, *values):
        self.last = self.last + values


class Halving:
    def __init__(self, order, bits, count, send, *keep):
        self.order, self.bits, self.count = order, list(bits), count
        self.terms = list(keep)
        self.moving = swap_seq(send, self.bits.pop(0), count)

    def keep(self, *values):
        self.terms += values

    def hop(self, go=True):
        arrived = self.order.after(self.moving)
        self.terms.append(arrived)
        cut = arrived.shape[0] // 2
        send = add(*[t[cut:] for t in self.terms]).astype(BF16)
        self.terms = [t[:cut] for t in self.terms]
        self.order.ran(send)
        self.send = send
        if go:
            self.moving = swap_seq(send, self.bits.pop(0), self.count)

    def go(self):
        self.moving = swap_seq(self.order.after(self.send), self.bits.pop(0), self.count)

    def finish(self):
        while self.bits:
            self.hop()
        arrived = self.order.after(self.moving)
        total = add(*[t[0] for t in self.terms], arrived[0])
        self.order.ran(total)
        return total


def swap(values):
    cut = values.shape[0] // 2
    return jnp.concatenate([values[cut:], values[:cut]], axis=0)


def body(
    block_input, lengths, norm1_gain, q_down, q_gain, q_up, kv_weight, out_weight, norm2_gain,
    gate_weight, up_weight, down_weight, cotangent,
):
    group = lax.axis_size("tensor")
    count = lax.axis_size("seq")
    mine = lax.axis_index("tensor").astype(jnp.int32)
    seq = lax.axis_index("seq").astype(jnp.int32)
    own = block_input.shape[0]
    rows = own * group
    heads = q_up.shape[1] // HD
    bits, bits_two = bits_of(count), bits_of(count, 2)
    owner = seq ^ jnp.array(apart_of(bits), jnp.int32)
    owner_two = seq ^ jnp.array(apart_of(bits_two), jnp.int32)

    order = Order()
    half = count // 2

    mid = HD // 2
    freq = 10000.0 ** (-(2.0 * jnp.arange(mid, dtype=F32)) / HD)[None, :]
    keyval, normed = own_keys(lengths, block_input, norm1_gain[None, :], kv_weight, freq)
    order.ran(keyval)
    keyval_far = far(keyval)
    compressed = dot(order.after(normed), q_down)
    latent = (rms_parts(compressed)[0] * q_gain).astype(BF16)
    order.ran(latent)
    latent_far = far(latent)
    pair = jnp.concatenate([keyval, order.after(keyval_far)], axis=0)
    order.ran(pair)
    ahead, back = ring_shift(pair, 1, count), ring_shift(pair, -1, count)
    empty = jnp.zeros((count,) + pair.shape, BF16)
    kv_a, kv_b = lax.dynamic_update_slice(empty, order.after(pair)[None], (0, 0, 0)), empty
    waiting, moving = [pair[None]], []

    def send_near(first):
        piece = waiting[0] if len(waiting) == 1 else jnp.concatenate(waiting)
        moving.append((first, near(order.after(piece))))
        return first + piece.shape[0]

    def take_near(kept):
        first, piece = moving.pop(0)
        return lax.dynamic_update_slice(kept, order.after(piece), (first, 0, 0))

    sent = 0
    for step in range(1, half + 1):
        ahead, back = order.after(ahead, back)
        slot = 2 * step - 1
        if step < half:
            piece = jnp.stack([ahead, back])
            order.ran(ahead, back)
            if step < half - 1:
                ahead, back = ring_shift(ahead, 1, count), ring_shift(back, -1, count)
            else:
                ahead, back = ring_shift(ahead[:own], 1, count), ring_shift(back[own:], -1, count)
        else:
            piece = jnp.concatenate([ahead, back], axis=0)[None]
        waiting.append(piece)
        if step != half - 1:
            sent = send_near(sent)
            waiting = []
        kv_a = lax.dynamic_update_slice(kv_a, piece, (slot, 0, 0))
        if step == 1:
            latent_half = jnp.concatenate([latent, order.after(latent_far)], axis=0)
            order.ran(latent_half)
            latent_near = near(latent_half)
            both_far = far(jnp.concatenate(order.after(block_input, cotangent), axis=0))
        if step == min(2, half - 1):
            latent_all = jnp.concatenate([latent_half, order.after(latent_near)], axis=0)
            query, cos, sin = project_rotate(lengths, latent_all, q_up, freq)
            order.ran(query)
        if step > 2 and moving and step < half:
            kv_b = take_near(kv_b)
    while moving:
        kv_b = take_near(kv_b)
    both_far = order.after(both_far)
    input_half = jnp.concatenate([block_input, both_far[:own]], axis=0)
    grad_half = jnp.concatenate([cotangent, both_far[own:]], axis=0)
    order.ran(input_half, grad_half)
    grad_near = near(grad_half)
    kv_a, kv_b = order.after(kv_a, kv_b)
    attended, attended_t, lse = attend(lengths, order.after(query), kv_a, kv_b)
    order.ran(attended)

    def sum_half(lefts, rights, dims, meanwhile):
        lefts[0] = order.after(lefts[0])
        keep, send = product(lefts, rights, dims)
        order.ran(send)
        chip = add(keep, order.after(near(send))).astype(BF16)
        order.ran(chip)
        moving = far(swap(chip))
        made = meanwhile()
        return add(chip, order.after(moving)), made

    share = q_down.shape[0] // (count * group)
    width = block_input.shape[1]

    def before_residual():
        normed_half = (rms_parts(order.after(input_half).astype(F32))[0] * norm1_gain).astype(BF16)
        scaled_q, inverse_q = rms_parts(dot(normed_half, q_down))
        order.ran(scaled_q)

        picked_mine, picked_other = share_of_columns(owner, mine, normed_half, share, group)
        order.ran(picked_mine)
        picked_near = near(picked_other)
        grad_all = jnp.concatenate([grad_half, order.after(grad_near)], axis=0)
        grad_hidden = dot(grad_all, down_weight, NT)
        order.ran(grad_hidden)
        picked_all = jnp.concatenate([picked_mine, order.after(picked_near)], axis=1)
        order.wait(picked_all)
        return scaled_q, inverse_q, picked_all, grad_all, grad_hidden

    branch, (scaled_q, inverse_q, picked, grad_all, grad_hidden) = sum_half(
        [attended], [out_weight], NN, before_residual
    )
    residual = input_half.astype(F32) + branch
    scaled_two, inverse_two = rms_parts(residual)
    normed_half = (scaled_two * norm2_gain).astype(BF16)
    order.ran(normed_half)
    normed_two = jnp.concatenate([normed_half, order.after(near(normed_half))], axis=0)

    hidden, hidden_t, grad_gate, grad_up = hidden_units(normed_two, gate_weight, up_weight, grad_hidden)
    order.ran(hidden)

    send = grad_by_columns(owner[half:], order.after(hidden_t), grad_all, count)
    order.ran(send)
    down_sum = Halving(order, bits, count, send)
    keep = grad_by_columns(owner[:half], order.after(hidden_t), grad_all, count)
    order.ran(keep)
    down_sum.keep(keep)

    [send] = grad_by_rows(owner_two[half:], order.after(normed_two), [grad_up], count)
    order.ran(send)
    up_sum = Halving(order, bits_two, count, send)
    [keep] = grad_by_rows(owner_two[:half], order.after(normed_two), [grad_up], count)
    order.ran(keep)
    up_sum.keep(keep)

    def after_feed():
        keep, send = product([order.after(hidden)], [down_weight], NN)
        order.ran(send)
        feed_chip = add(keep, order.after(near(send))).astype(BF16)
        order.ran(feed_chip)
        return feed_chip

    back_two, feed_chip = sum_half([grad_gate, grad_up], [gate_weight, up_weight], NT, after_feed)
    grad_residual = grad_half.astype(F32) + rms_back(back_two, scaled_two, inverse_two, norm2_gain)
    branch_half = grad_residual.astype(BF16)
    order.ran(branch_half)
    branch_near = near(branch_half)
    feed_far = far(order.after(feed_chip)[own:])

    [send] = grad_by_rows(owner[half:], order.after(normed_two), [grad_gate], count)
    order.ran(send)
    gate_sum = Halving(order, bits, count, send)
    down_sum.hop()
    grad_branch = jnp.concatenate([branch_half, order.after(branch_near)], axis=0)
    grad_attended, delta = attended_grad(grad_branch, out_weight, attended)
    order.ran(grad_attended)
    send_out = grad_by_columns(owner[half:], order.after(attended_t), grad_branch, count, 0, 2)
    order.ran(send_out)
    send_out_two = grad_by_columns(owner[half:], order.after(attended_t), grad_branch, count, 1, 2)
    order.ran(send_out_two)
    [keep] = grad_by_rows(owner[:half], order.after(normed_two), [grad_gate], count)
    order.ran(keep)
    gate_sum.keep(keep)
    up_sum.hop(go=False)

    slot_out = slot_of(jnp.arange(count, dtype=jnp.int32), count, seq) ^ seq
    slot_out = sum(((slot_out >> (bit.bit_length() - 1)) & 1) << (len(bits) - 1 - i) for i, bit in enumerate(bits))
    grad_query_raw, dkv_a, dkv_b = attend_back(
        lengths, slot_out, query, order.after(grad_attended), kv_a, kv_b, lse, delta, cos, sin
    )
    order.ran(grad_query_raw)
    dkv_near = near(dkv_b)

    latent_keep, latent_send = product([order.after(grad_query_raw)], [q_up], NT)
    order.ran(latent_send)
    latent_near = near(latent_send)
    feed_out = add(feed_chip[:own], order.after(feed_far))
    block_output = (residual[:own] + feed_out).astype(BF16)
    order.ran(block_output)
    down_sum.hop()
    gate_sum.hop()
    chip_kv = add(dkv_a, order.after(dkv_near)).astype(BF16)
    order.ran(chip_kv)
    kv_far = far(chip_kv[:, own:])
    latent_chip = add(latent_keep, order.after(latent_near)).astype(BF16)
    order.ran(latent_chip)
    up_sum.go()
    keep_out = grad_by_columns(owner[:half], order.after(attended_t), grad_branch, count, 0, 2)
    order.ran(keep_out)
    keep_out_two = grad_by_columns(owner[:half], order.after(attended_t), grad_branch, count, 1, 2)
    order.ran(keep_out_two)
    [send_query] = grad_by_rows(owner[half:], order.after(latent_all), [grad_query_raw], count)
    order.ran(send_query)
    [keep_query] = grad_by_rows(owner[:half], order.after(latent_all), [grad_query_raw], count)
    order.ran(keep_query)
    down_grad = down_sum.finish()
    chips_kv = add(chip_kv[:, :own], order.after(kv_far)).astype(BF16)
    order.ran(chips_kv)
    kv_sum = Halving(order, bits, count, chips_kv[half:], chips_kv[:half])
    latent_far = far(swap(order.after(latent_chip)))
    up_sum.hop()
    out_sum = Halving(order, bits, count, order.after(send_out), keep_out)
    kv_sum.hop()
    grad_latent = add(latent_chip, order.after(latent_far))
    grad_compressed = rms_back(grad_latent, scaled_q, inverse_q, q_gain).astype(BF16)
    order.ran(grad_compressed)
    compressed_near = near(grad_compressed)
    kv_sum.hop()
    gain_two = jnp.sum(order.after(back_two) * scaled_two, axis=0)
    gain_q = jnp.sum(grad_latent * scaled_q, axis=0)
    gains = jnp.concatenate([gain_two, gain_q])
    up_grad = up_sum.finish()
    compressed_all = jnp.concatenate([grad_compressed, order.after(compressed_near)], axis=0)
    q_down_parts = dot(picked, compressed_all).astype(BF16)
    order.ran(q_down_parts)
    gate_sum.hop(go=False)

    def by_owner(values, size):
        blocks = lax.dynamic_slice(values.reshape(count, group, size), (0, mine, 0), (count, 1, size))
        same = owner[:, None, None] == jnp.arange(count, dtype=jnp.int32)[None, :, None]
        return jnp.sum(jnp.where(same, blocks[:, 0][None], 0.0), axis=1)[:, None, :]

    kv_own = kv_sum.finish()
    former, latter = kv_own[:, :mid], kv_own[:, mid:HD]
    grad_kv_raw = jnp.concatenate(
        [
            former * cos[:own] + latter * sin[:own],
            latter * cos[:own] - former * sin[:own],
            kv_own[:, HD:],
        ],
        axis=1,
    ).astype(BF16)
    order.ran(grad_kv_raw)
    kv_raw_far = far(grad_kv_raw)
    out_sum.hop()
    out_sum_two = Halving(order, bits, count, order.after(send_out_two), keep_out_two)
    gate_sum.go()
    kv_half = jnp.concatenate([grad_kv_raw, order.after(kv_raw_far)], axis=0)
    order.ran(kv_half)
    kv_half_near = near(kv_half)
    q_down_parts = order.after(q_down_parts).reshape(count, share, -1)
    q_down_sum = Halving(order, bits, count, q_down_parts[half:], q_down_parts[:half])
    kv_half_near = order.after(kv_half_near)
    order.ran(kv_half_near)
    scaled_one, inverse_one = rms_parts(order.after(block_input).astype(F32))
    grad_normed = dot(grad_compressed[:own], q_down, NT) + dot(order.after(grad_kv_raw), kv_weight, NT)
    input_grad = grad_residual[:own] + rms_back(grad_normed, scaled_one, inverse_one, norm1_gain)
    gain_one = jnp.sum(grad_normed * scaled_one, axis=0)
    order.ran(gain_one)
    out_sum.hop()
    gain_far = far(gain_one)
    kv_all = jnp.concatenate([kv_half, kv_half_near], axis=0)
    kv_parts = dot(picked, order.after(kv_all)).astype(BF16)
    order.ran(kv_parts)
    out_sum_two.hop()
    query_sum = Halving(order, bits, count, order.after(send_query), keep_query)
    gain_one = gain_one + order.after(gain_far)
    gains = jnp.concatenate([gain_one, gains])
    order.ran(gains)
    gains_near = near(gains)
    q_down_sum.hop()
    kv_parts = order.after(kv_parts).reshape(count, share, -1)
    kv_weight_sum = Halving(order, bits, count, kv_parts[half:], kv_parts[:half])
    gate_grad = gate_sum.finish()
    query_sum.hop()
    gains = gains + order.after(gains_near)
    gains = jnp.concatenate(
        [
            by_owner(gains[:width], share),
            by_owner(gains[width : 2 * width], share),
            by_owner(gains[2 * width :], q_gain.shape[0] // (count * group)),
        ],
        axis=2,
    )
    order.ran(gains)
    gains_sum = Halving(order, bits, count, gains[half:], gains[:half])
    kv_weight_sum.hop()
    out_sum_two.hop()
    q_down_sum.hop()
    query_sum.hop()
    gains_sum.hop()
    kv_weight_sum.hop()
    out_one = out_sum.finish()
    gains_sum.hop()
    q_down_grad = q_down_sum.finish()
    kv_weight_grad = kv_weight_sum.finish()
    gains = gains_sum.finish()[0]
    out_weight_grad = jnp.concatenate([out_one, out_sum_two.finish()], axis=0)
    q_up_grad = query_sum.finish()
    return (
        block_output,
        input_grad,
        gains[:share],
        q_down_grad,
        gains[2 * share :],
        q_up_grad,
        kv_weight_grad,
        out_weight_grad,
        gains[share : 2 * share],
        gate_grad,
        up_grad,
        down_grad,
    )


def solution(mesh):
    both = P(("seq", "tensor"))
    rows = P(("seq", "tensor"), None)
    return jax.shard_map(
        body,
        mesh=mesh,
        in_specs=(
            rows, P(), P(), P(), P(), P(None, "tensor"), P(), P("tensor", None), P(),
            P(None, "tensor"), P(None, "tensor"), P("tensor", None), rows,
        ),
        out_specs=(
            rows, rows, both, rows, both, P("seq", "tensor"), rows, P("tensor", "seq"), both,
            P("seq", "tensor"), P("seq", "tensor"), P("tensor", "seq"),
        ),
        check_vma=False,
    )
```

```python
import functools
import math

import jax
import jax.numpy as jnp
from jax import lax
from jax.experimental import pallas as pl
from jax.experimental.pallas import tpu as pltpu
from jax.sharding import PartitionSpec as P

HD = 256
EPS = 1e-06
NEG = -1e30
F32 = jnp.float32
BF16 = jnp.bfloat16
LOG2_SCALE = math.log2(math.e) / math.sqrt(HD)
SCALE = 1.0 / math.sqrt(HD)
MIB = 1 << 20
BRIEF = pl.CostEstimate(flops=1000, bytes_accessed=1000, transcendentals=0)

STEPS = (
    "down", "down_keep", "up", "up_keep", "units_back", "units_chip", "feed_product", "feed_chip",
    "branch_grad", "feed_far", "gate", "down_1", "attended_back", "out_send0", "out_send1", "gate_keep",
    "up_1", "attention_back", "latent_product", "feed", "down_2", "gate_1", "chip_keys", "latent_chip",
    "up_go", "out_keep0", "out_keep1", "query_send", "query_keep", "down_end", "keys", "latent_far", "up_2",
    "out_a", "kv_1", "compressed", "kv_2", "out_a_1", "out_b", "up_end", "down_q_parts", "own_keys_grad",
    "gate_2", "half_keys", "normed_grad", "out_b_1", "query", "gains_own", "kv_parts", "kv_w", "out_a_2",
    "gains_1", "kv_w_1", "gate_end", "q_down", "out_a_end", "kv_w_2", "out_b_2", "query_1", "gains_2",
    "q_down_1", "kv_w_end", "gains_3", "q_down_2", "query_2", "out_b_end", "q_down_end", "query_end",
)

NN = (((1,), (0,)), ((), ()))
NT = (((1,), (1,)), ((), ()))
TN = (((0,), (0,)), ((), ()))


def dot(left, right, dims=NN):
    return lax.dot_general(left, right, dims, preferred_element_type=F32)


def at_index(values, index, axis, keepdims=True):
    start = [jnp.int32(0)] * values.ndim
    start[axis] = index
    size = values.shape[:axis] + (1,) + values.shape[axis + 1 :]
    taken = lax.dynamic_slice(values, start, size, allow_negative_indices=False)
    return taken if keepdims else lax.squeeze(taken, [axis])


def rms_parts(values):
    inverse = lax.rsqrt(jnp.mean(values * values, axis=-1, keepdims=True) + EPS)
    return values * inverse, inverse


def rms_back(grad_out, scaled, inverse, gain):
    inner = grad_out * gain
    return inverse * (inner - scaled * jnp.mean(inner * scaled, axis=-1, keepdims=True))


def place_in_kernel():
    return lax.axis_index("seq").astype(jnp.int32), lax.axis_index("tensor").astype(jnp.int32)


def group_block(row, own):
    block = lax.div(row, jnp.int32(own))
    return ((block & 1) << 1) | (block >> 1), row - block * own


def first_in_kernel(token, lengths):
    found = jnp.zeros_like(token)
    start = jnp.int32(0)
    for i in range(lengths.shape[0] - 1):
        start = start + lengths[i]
        found = jnp.maximum(found, jnp.where(token >= start, start, 0))
    return found


def angles_in_kernel(rows, own, lengths, freq_ref):
    seq, mine = place_in_kernel()
    other, within = group_block(lax.broadcasted_iota(jnp.int32, (rows, HD // 2), 0), own)
    token = seq * (4 * own) + (mine ^ other) * own + within
    theta = (token - first_in_kernel(token, lengths)).astype(F32) * freq_ref[0:1, :]
    return jnp.cos(theta), jnp.sin(theta)


def slot_of(slot, count, seq):
    place = jnp.where((seq & 1) == 0, seq >> 1, count - 1 - (seq >> 1))
    step = (slot + 1) >> 1
    place = (place + jnp.where((slot & 1) == 1, -step, step)) & (count - 1)
    return seq_at(place, count)


def slot_state(lengths, slot, count, rows):
    seq, _ = place_in_kernel()
    source = slot_of(slot, count, seq)
    first = first_in_kernel(seq * rows, lengths)
    last = first_in_kernel(seq * rows + rows - 1, lengths)
    base = source * rows
    needed = (source <= seq) & (source >= lax.div(first, jnp.int32(rows)))
    bounded = (source == seq) | (base < last)
    return base, needed, bounded


def key_bias(lengths, base, keys, rows):
    seq, mine = place_in_kernel()
    own = rows // 4
    other, within = group_block(lax.broadcasted_iota(jnp.int32, (keys, rows), 0), own)
    token = base + (mine ^ other) * own + within
    other, within = group_block(lax.broadcasted_iota(jnp.int32, (8, rows), 1), own)
    query = seq * rows + (mine ^ other) * own + within
    low = first_in_kernel(query, lengths)
    allowed = (token <= query[0:1, :]) & (token >= low[0:1, :])
    return jnp.where(allowed, 0.0, NEG)


def keys_kernel(lengths, x_ref, gain_ref, w_ref, freq_ref, out_ref, normed_ref):
    values = x_ref[...].astype(F32)
    inverse = lax.rsqrt(jnp.mean(values * values, axis=-1, keepdims=True) + EPS)
    normed = (values * inverse * gain_ref[...]).astype(BF16)
    normed_ref[...] = normed
    raw = dot(normed, w_ref[...])
    cos, sin = angles_in_kernel(x_ref.shape[0], x_ref.shape[0], lengths, freq_ref)
    mid = HD // 2
    former, latter = raw[:, :mid], raw[:, mid:HD]
    out_ref[:, :mid] = (former * cos - latter * sin).astype(BF16)
    out_ref[:, mid:HD] = (latter * cos + former * sin).astype(BF16)
    out_ref[:, HD:] = raw[:, HD:].astype(BF16)


def own_keys(lengths, values, gain, weight, freq):
    own, depth = values.shape
    whole = lambda *shape: pl.BlockSpec(shape, lambda i, m: (0,) * len(shape))
    return pl.pallas_call(
        keys_kernel,
        grid_spec=pltpu.PrefetchScalarGridSpec(
            num_scalar_prefetch=1,
            grid=(1,),
            in_specs=[whole(own, depth), whole(1, depth), whole(*weight.shape), whole(1, HD // 2)],
            out_specs=[whole(own, 2 * HD), whole(own, depth)],
        ),
        out_shape=[jax.ShapeDtypeStruct((own, 2 * HD), BF16), jax.ShapeDtypeStruct((own, depth), BF16)],
        compiler_params=pltpu.CompilerParams(vmem_limit_bytes=16 * MIB),
        cost_estimate=BRIEF,
        name="own_keys",
    )(lengths, values, gain, weight, freq)


def fwd_kernel(heads, lengths, q_ref, a_ref, b_ref, o_ref, ot_ref, lse_ref, m_s, l_s, acc_s, bias_s):
    slot = pl.program_id(0)
    count = pl.num_programs(0)
    keys, rows = bias_s.shape
    base, needed, bounded = slot_state(lengths, slot, count, rows)

    @pl.when(slot == 0)
    def _():
        m_s[...] = jnp.full_like(m_s, NEG)
        l_s[...] = jnp.zeros_like(l_s)
        acc_s[...] = jnp.zeros_like(acc_s)

    def tile(masked):
        key = jnp.concatenate([a_ref[0, :, :HD], b_ref[0, :, :HD]], axis=0)
        value = jnp.concatenate([a_ref[0, :, HD:], b_ref[0, :, HD:]], axis=0)
        value_t = value.T
        if masked:
            bias_s[...] = key_bias(lengths, base, keys, rows)

        def score(h):
            return dot(key, q_ref[:, h * HD : (h + 1) * HD], NT)

        following = score(0)
        for h in range(heads):
            scores = following * LOG2_SCALE
            if h + 1 < heads:
                following = score(h + 1)
            if masked:
                scores = scores + bias_s[...]
            old = m_s[h, 0:1, :]
            new = jnp.maximum(old, jnp.max(scores, axis=0, keepdims=True))
            alpha = jnp.exp2(old - new)
            weight = jnp.exp2(scores - new)
            l_s[h, 0:1, :] = l_s[h, 0:1, :] * alpha + jnp.sum(weight, axis=0, keepdims=True)
            m_s[h, 0:1, :] = new
            acc_s[h] = acc_s[h] * alpha + dot(value_t, weight.astype(BF16))

    pl.when(needed & ~bounded)(lambda: tile(False))
    pl.when(needed & bounded)(lambda: tile(True))

    @pl.when(slot == count - 1)
    def _():
        for h in range(heads):
            total = l_s[h, 0:1, :]
            out_t = (acc_s[h] / total).astype(BF16)
            ot_ref[h * HD : (h + 1) * HD, :] = out_t
            o_ref[:, h * HD : (h + 1) * HD] = out_t.T
            lse_ref[h] = jnp.broadcast_to(m_s[h, 0:1, :] + jnp.log2(total), lse_ref.shape[1:])


def attend(lengths, query, kv_a, kv_b):
    rows, width = query.shape
    heads = width // HD
    slots, half, wide = kv_a.shape
    keys = 2 * half
    whole = lambda *shape: pl.BlockSpec(shape, lambda i, m: (0,) * len(shape))
    tile = pl.BlockSpec((1, half, wide), lambda i, m: (i, 0, 0))
    state = [(heads, 8, rows), (heads, 8, rows), (heads, HD, rows), (keys, rows)]
    out = [((rows, width), BF16), ((width, rows), BF16), ((heads, 8, rows), F32)]
    return pl.pallas_call(
        functools.partial(fwd_kernel, heads),
        grid_spec=pltpu.PrefetchScalarGridSpec(
            num_scalar_prefetch=1,
            grid=(slots,),
            in_specs=[whole(rows, width), tile, tile],
            out_specs=[whole(*shape) for shape, _ in out],
            scratch_shapes=[pltpu.VMEM(shape, F32) for shape in state],
        ),
        out_shape=[jax.ShapeDtypeStruct(*o) for o in out],
        compiler_params=pltpu.CompilerParams(vmem_limit_bytes=24 * MIB),
        cost_estimate=BRIEF,
        name="attend",
    )(lengths, query, kv_a, kv_b)


def bwd_kernel(heads, lengths, _, q_ref, do_ref, a_ref, b_ref, lse_ref, delta_ref, cos_ref, sin_ref,
               dq_ref, da_ref, db_ref, dq_s, dk_s, dv_s, bias_s):
    slot = pl.program_id(0)
    keys, rows = bias_s.shape
    base, needed, bounded = slot_state(lengths, slot, pl.num_programs(0), rows)
    half = a_ref.shape[1]

    @pl.when(slot == 0)
    def _():
        dq_s[...] = jnp.zeros_like(dq_s)

    @pl.when(~needed)
    def _():
        da_ref[...] = jnp.zeros_like(da_ref)
        db_ref[...] = jnp.zeros_like(db_ref)

    def tile(masked):
        key = jnp.concatenate([a_ref[0, :, :HD], b_ref[0, :, :HD]], axis=0)
        value = jnp.concatenate([a_ref[0, :, HD:], b_ref[0, :, HD:]], axis=0)
        key_t = key.T
        if masked:
            bias_s[...] = key_bias(lengths, base, keys, rows)
        for h in range(heads):
            at = slice(h * HD, (h + 1) * HD)
            scores = dot(key, q_ref[:, at], NT) * LOG2_SCALE
            if masked:
                scores = scores + bias_s[...]
            weight = jnp.exp2(scores - lse_ref[h, 0:1, :])
            grad = dot(value, do_ref[:, at], NT)
            ds = (weight * (grad - delta_ref[h, 0:1, :])).astype(BF16)
            dv = dot(weight.astype(BF16), do_ref[:, at])
            dk = dot(ds, q_ref[:, at])
            if h == 0:
                dv_s[...] = dv
                dk_s[...] = dk
            else:
                dv_s[...] += dv
                dk_s[...] += dk
            dq_s[h] += dot(key_t, ds)
        da_ref[0, :, :HD] = (dk_s[:half, :] * SCALE).astype(BF16)
        db_ref[0, :, :HD] = (dk_s[half:, :] * SCALE).astype(BF16)
        da_ref[0, :, HD:] = dv_s[:half, :].astype(BF16)
        db_ref[0, :, HD:] = dv_s[half:, :].astype(BF16)

    pl.when(needed & ~bounded)(lambda: tile(False))
    pl.when(needed & bounded)(lambda: tile(True))

    @pl.when(slot == pl.num_programs(0) - 1)
    def _():
        cos, sin = cos_ref[...], sin_ref[...]
        mid = HD // 2
        for h in range(heads):
            grad = (dq_s[h] * SCALE).T
            former, latter = grad[:, :mid], grad[:, mid:]
            dq_ref[:, h * HD : h * HD + mid] = (former * cos + latter * sin).astype(BF16)
            dq_ref[:, h * HD + mid : (h + 1) * HD] = (latter * cos - former * sin).astype(BF16)


def attend_back(lengths, slot_out, query, grad, kv_a, kv_b, lse, delta, cos, sin):
    rows, width = query.shape
    heads = width // HD
    slots, half, wide = kv_a.shape
    keys = 2 * half
    whole = lambda *shape: pl.BlockSpec(shape, lambda i, m, o: (0,) * len(shape))
    tile = pl.BlockSpec((1, half, wide), lambda i, m, o: (i, 0, 0))
    out_tile = pl.BlockSpec((1, half, wide), lambda i, m, o: (o[i], 0, 0))
    return pl.pallas_call(
        functools.partial(bwd_kernel, heads),
        grid_spec=pltpu.PrefetchScalarGridSpec(
            num_scalar_prefetch=2,
            grid=(slots,),
            in_specs=[
                whole(rows, width), whole(rows, width), tile, tile,
                whole(heads, 8, rows), whole(heads, 8, rows), whole(rows, HD // 2), whole(rows, HD // 2),
            ],
            out_specs=[whole(rows, width), out_tile, out_tile],
            scratch_shapes=[
                pltpu.VMEM((heads, HD, rows), F32),
                pltpu.VMEM((keys, HD), F32),
                pltpu.VMEM((keys, HD), F32),
                pltpu.VMEM((keys, rows), F32),
            ],
        ),
        out_shape=[
            jax.ShapeDtypeStruct((rows, width), BF16),
            jax.ShapeDtypeStruct((slots, half, wide), BF16),
            jax.ShapeDtypeStruct((slots, half, wide), BF16),
        ],
        compiler_params=pltpu.CompilerParams(vmem_limit_bytes=32 * MIB),
        cost_estimate=BRIEF,
        name="attend_back",
    )(lengths, slot_out, query, grad, kv_a, kv_b, lse, delta, cos, sin)


def attended_grad_kernel(gb_ref, w_ref, att_ref, out_ref, delta_ref):
    grad = dot(gb_ref[...], w_ref[...], NT).astype(BF16)
    out_ref[...] = grad
    term = grad.astype(F32) * att_ref[...].astype(F32)
    delta_ref[0] = jnp.broadcast_to(jnp.sum(term.T, axis=0, keepdims=True), delta_ref.shape[1:])


def attended_grad(grad_branch, weight, attended):
    rows, depth = grad_branch.shape
    width = weight.shape[0]
    return pl.pallas_call(
        attended_grad_kernel,
        grid=(width // HD,),
        in_specs=[
            pl.BlockSpec((rows, depth), lambda i: (0, 0)),
            pl.BlockSpec((HD, depth), lambda i: (i, 0)),
            pl.BlockSpec((rows, HD), lambda i: (0, i)),
        ],
        out_specs=[pl.BlockSpec((rows, HD), lambda i: (0, i)), pl.BlockSpec((1, 8, rows), lambda i: (i, 0, 0))],
        out_shape=[
            jax.ShapeDtypeStruct((rows, width), BF16),
            jax.ShapeDtypeStruct((width // HD, 8, rows), F32),
        ],
        compiler_params=pltpu.CompilerParams(vmem_limit_bytes=12 * MIB),
        cost_estimate=BRIEF,
        name="attended_grad",
    )(grad_branch, weight, attended)


def product(lefts, rights, dims):
    cut = lefts[0].shape[0] // 2
    keep = sum(dot(left[:cut], right, dims) for left, right in zip(lefts, rights))
    send = sum(dot(left[cut:], right, dims) for left, right in zip(lefts, rights))
    return keep.astype(BF16), send.astype(BF16)


def project_kernel(lengths, x_ref, w_ref, freq_ref, out_ref, cos_ref, sin_ref):
    rows = x_ref.shape[0]

    @pl.when(pl.program_id(0) == 0)
    def _():
        cos_ref[...], sin_ref[...] = angles_in_kernel(rows, rows // 4, lengths, freq_ref)

    raw = dot(x_ref[...], w_ref[...])
    cos, sin = cos_ref[...], sin_ref[...]
    mid = HD // 2
    former, latter = raw[:, :mid], raw[:, mid:]
    out_ref[:, :mid] = (former * cos - latter * sin).astype(BF16)
    out_ref[:, mid:] = (latter * cos + former * sin).astype(BF16)


def project_rotate(lengths, latent, weight, freq):
    rows, rank = latent.shape
    width = weight.shape[1]
    whole = lambda *shape: pl.BlockSpec(shape, lambda i, m: (0,) * len(shape))
    angle = jax.ShapeDtypeStruct((rows, HD // 2), F32)
    return pl.pallas_call(
        project_kernel,
        grid_spec=pltpu.PrefetchScalarGridSpec(
            num_scalar_prefetch=1,
            grid=(width // HD,),
            in_specs=[whole(rows, rank), pl.BlockSpec((rank, HD), lambda i, m: (0, i)), whole(1, HD // 2)],
            out_specs=[
                pl.BlockSpec((rows, HD), lambda i, m: (0, i)), whole(rows, HD // 2), whole(rows, HD // 2),
            ],
        ),
        out_shape=[jax.ShapeDtypeStruct((rows, width), BF16), angle, angle],
        compiler_params=pltpu.CompilerParams(vmem_limit_bytes=10 * MIB),
        cost_estimate=BRIEF,
        name="project_rotate",
    )(lengths, latent, weight, freq)


def hidden_kernel(x_ref, gate_ref, up_ref, gh_ref, hidden_ref, hidden_t_ref, gg_ref, gu_ref, gate_s, up_s):
    step = pl.program_id(0)
    gate = dot(x_ref[...], gate_ref[...])
    up = dot(x_ref[...], up_ref[...])

    @pl.when(step == 0)
    def _():
        gate_s[...] = gate
        up_s[...] = up

    @pl.when(step > 0)
    def _():
        gate_s[...] += gate
        up_s[...] += up

    @pl.when(step == pl.num_programs(0) - 1)
    def _():
        for first in range(0, gate_s.shape[0], 128):
            at = slice(first, first + 128)
            gate_pre, up_pre, grad = gate_s[at, :], up_s[at, :], gh_ref[at, :]
            sigmoid = jax.nn.sigmoid(gate_pre)
            silu = gate_pre * sigmoid
            hidden = (silu * up_pre).astype(BF16)
            hidden_ref[at, :] = hidden
            hidden_t_ref[:, at] = hidden.T
            gg_ref[at, :] = (grad * up_pre * sigmoid * (1.0 + gate_pre * (1.0 - sigmoid))).astype(BF16)
            gu_ref[at, :] = (grad * silu).astype(BF16)


def hidden_units(normed, gate_weight, up_weight, grad_hidden):
    rows, depth = normed.shape
    units = gate_weight.shape[1]
    cut = 512
    whole = lambda *shape: pl.BlockSpec(shape, lambda i: (0,) * len(shape))
    weight = pl.BlockSpec((cut, units), lambda i: (i, 0))
    plain = jax.ShapeDtypeStruct((rows, units), BF16)
    return pl.pallas_call(
        hidden_kernel,
        grid=(depth // cut,),
        in_specs=[pl.BlockSpec((rows, cut), lambda i: (0, i)), weight, weight, whole(rows, units)],
        out_specs=[whole(rows, units), whole(units, rows), whole(rows, units), whole(rows, units)],
        out_shape=[plain, jax.ShapeDtypeStruct((units, rows), BF16), plain, plain],
        scratch_shapes=[pltpu.VMEM((rows, units), F32), pltpu.VMEM((rows, units), F32)],
        compiler_params=pltpu.CompilerParams(vmem_limit_bytes=36 * MIB),
        cost_estimate=BRIEF,
        name="hidden_units",
    )(normed, gate_weight, up_weight, grad_hidden)


def in_order(values, owner, axis):
    return jnp.stack(
        [at_index(values, owner[j], axis, keepdims=False) for j in range(owner.shape[0])]
    )


def rows_kernel(owner, left_ref, *refs):
    count = len(refs) // 2
    left = left_ref[...]
    for right_ref, out_ref in zip(refs[:count], refs[count:]):
        out_ref[0] = dot(left, right_ref[...], TN).astype(BF16)


def grad_by_rows(owner, left, rights, count):
    slots = owner.shape[0]
    rows, width = left.shape
    cut = width // count
    if cut % 128:
        return [in_order(dot(left, r, TN).astype(BF16).reshape(count, cut, -1), owner, 0) for r in rights]
    return pl.pallas_call(
        rows_kernel,
        grid_spec=pltpu.PrefetchScalarGridSpec(
            num_scalar_prefetch=1,
            grid=(slots,),
            in_specs=[pl.BlockSpec((rows, cut), lambda i, o: (0, o[i]))]
            + [pl.BlockSpec(r.shape, lambda i, o: (0, 0)) for r in rights],
            out_specs=[pl.BlockSpec((1, cut, r.shape[1]), lambda i, o: (i, 0, 0)) for r in rights],
        ),
        out_shape=[jax.ShapeDtypeStruct((slots, cut, r.shape[1]), BF16) for r in rights],
        compiler_params=pltpu.CompilerParams(vmem_limit_bytes=16 * MIB),
        cost_estimate=BRIEF,
        name="grad_by_rows",
    )(owner, left, *rights)


def columns_kernel(owner, left_ref, right_ref, out_ref):
    out_ref[0] = dot(left_ref[...], right_ref[...]).astype(BF16)


def grad_by_columns(owner, left_t, right, count, part=0, parts=1):
    slots = owner.shape[0]
    rows, width = right.shape
    cut = width // count
    tall = left_t.shape[0] // parts
    if cut % 128:
        left_t = left_t[part * tall : (part + 1) * tall]
        return in_order(dot(left_t, right).astype(BF16).reshape(tall, count, cut), owner, 1)
    return pl.pallas_call(
        columns_kernel,
        grid_spec=pltpu.PrefetchScalarGridSpec(
            num_scalar_prefetch=1,
            grid=(slots,),
            in_specs=[
                pl.BlockSpec((tall, rows), lambda i, o: (part, 0)),
                pl.BlockSpec((rows, cut), lambda i, o: (0, o[i])),
            ],
            out_specs=pl.BlockSpec((1, tall, cut), lambda i, o: (i, 0, 0)),
        ),
        out_shape=jax.ShapeDtypeStruct((slots, tall, cut), BF16),
        compiler_params=pltpu.CompilerParams(vmem_limit_bytes=16 * MIB),
        cost_estimate=BRIEF,
        name="grad_by_columns",
    )(owner, left_t, right)


def share_kernel(size, meta, x_ref, mine_ref, other_ref, turned_s):
    turned_s[...] = x_ref[...].astype(F32).T
    mine = meta[1, 0]
    mine_ref[...] = turned_s[pl.ds(pl.multiple_of(mine * size, size), size), :].astype(BF16)
    other_ref[...] = turned_s[pl.ds(pl.multiple_of((mine ^ 1) * size, size), size), :].astype(BF16)


def share_of_columns(owner, mine, values, size, group):
    slots = owner.shape[0]
    rows, width = values.shape
    cut = width // slots
    if cut % 128:
        turned = values.T.reshape(slots, group, size, rows)
        return tuple(
            in_order(at_index(turned, which, 1, keepdims=False), owner, 0).reshape(slots * size, rows)
            for which in (mine, mine ^ 1)
        )
    return pl.pallas_call(
        functools.partial(share_kernel, size),
        grid_spec=pltpu.PrefetchScalarGridSpec(
            num_scalar_prefetch=1,
            grid=(slots,),
            in_specs=[pl.BlockSpec((rows, cut), lambda i, m: (0, m[0, i]))],
            out_specs=[pl.BlockSpec((size, rows), lambda i, m: (i, 0))] * 2,
            scratch_shapes=[pltpu.VMEM((cut, rows), F32)],
        ),
        out_shape=[jax.ShapeDtypeStruct((slots * size, rows), BF16)] * 2,
        compiler_params=pltpu.CompilerParams(vmem_limit_bytes=8 * MIB),
        cost_estimate=BRIEF,
        name="share_of_columns",
    )(jnp.stack([owner, jnp.full((slots,), mine)]), values)


def add(*parts):
    total = parts[0].astype(F32)
    for part in parts[1:]:
        total = total + part.astype(F32)
    return total


def near(values):
    return lax.ppermute(values, "tensor", [(i, i ^ 1) for i in range(4)])


def far(values):
    return lax.ppermute(values, "tensor", [(i, i ^ 2) for i in range(4)])


def ring_order(count):
    return list(range(0, count, 2)) + list(range(count - 1, 0, -2))


def ring_shift(values, step, count):
    order = ring_order(count)
    return lax.ppermute(
        values, "seq", [(order[i], order[(i + step) % count]) for i in range(count)]
    )


def seq_at(place, count):
    return jnp.where(place < count // 2, 2 * place, 2 * (count - 1 - place) + 1)


def swap_seq(values, bit, count):
    return lax.ppermute(values, "seq", [(i, i ^ bit) for i in range(count)])


def bits_of(count, first=1):
    bits = [1 << i for i in range(count.bit_length() - 1)]
    return [first] + [b for b in bits if b != first]


def apart_of(bits):
    apart = [0]
    for bit in reversed(bits):
        apart = apart + [bit | a for a in apart]
    return apart


class Order:
    def __init__(self):
        self.last = ()

    def after(self, *values):
        held = lax.optimization_barrier((values, self.last))[0]
        return held if len(values) > 1 else held[0]

    def ran(self, *values):
        self.last = values

    def wait(self, *values):
        self.last = self.last + values


class Halving:
    def __init__(self, order, bits, count, send, *keep):
        self.order, self.bits, self.count = order, list(bits), count
        self.terms = list(keep)
        self.moving = swap_seq(send, self.bits.pop(0), count)

    def keep(self, *values):
        self.terms += values

    def hop(self, go=True):
        assert self.terms and self.moving is not None
        arrived = self.order.after(self.moving)
        self.terms.append(arrived)
        self.moving = None
        cut = arrived.shape[0] // 2
        send = add(*[t[cut:] for t in self.terms]).astype(BF16)
        self.terms = [t[:cut] for t in self.terms]
        self.order.ran(send)
        self.send = send
        if go:
            self.moving = swap_seq(send, self.bits.pop(0), self.count)

    def go(self):
        self.moving = swap_seq(self.order.after(self.send), self.bits.pop(0), self.count)

    def finish(self):
        while self.bits:
            self.hop()
        assert self.terms and self.moving is not None
        arrived = self.order.after(self.moving)
        total = add(*[t[0] for t in self.terms], arrived[0])
        self.order.ran(total)
        return total


def swap(values):
    cut = values.shape[0] // 2
    return jnp.concatenate([values[cut:], values[:cut]], axis=0)


def body(
    block_input, lengths, norm1_gain, q_down, q_gain, q_up, kv_weight, out_weight, norm2_gain,
    gate_weight, up_weight, down_weight, cotangent,
):
    group = lax.axis_size("tensor")
    count = lax.axis_size("seq")
    mine = lax.axis_index("tensor").astype(jnp.int32)
    seq = lax.axis_index("seq").astype(jnp.int32)
    own = block_input.shape[0]
    rows = own * group
    heads = q_up.shape[1] // HD
    bits, bits_two = bits_of(count), bits_of(count, 2)
    owner = seq ^ jnp.array(apart_of(bits), jnp.int32)
    owner_two = seq ^ jnp.array(apart_of(bits_two), jnp.int32)

    order = Order()
    half = count // 2

    mid = HD // 2
    freq = 10000.0 ** (-(2.0 * jnp.arange(mid, dtype=F32)) / HD)[None, :]
    keyval, normed = own_keys(lengths, block_input, norm1_gain[None, :], kv_weight, freq)
    order.ran(keyval)
    keyval_far = far(keyval)
    compressed = dot(order.after(normed), q_down)
    latent = (rms_parts(compressed)[0] * q_gain).astype(BF16)
    order.ran(latent)
    latent_far = far(latent)
    pair = jnp.concatenate([keyval, order.after(keyval_far)], axis=0)
    order.ran(pair)
    ahead, back = ring_shift(pair, 1, count), ring_shift(pair, -1, count)
    both_far = far(jnp.concatenate(order.after(block_input, cotangent), axis=0))
    empty = jnp.zeros((count,) + pair.shape, BF16)
    kv_a, kv_b = lax.dynamic_update_slice(empty, order.after(pair)[None], (0, 0, 0)), empty
    waiting, moving = [pair[None]], []

    def send_near(first):
        piece = waiting[0] if len(waiting) == 1 else jnp.concatenate(waiting)
        moving.append((first, near(order.after(piece))))
        return first + piece.shape[0]

    def take_near(kept):
        first, piece = moving.pop(0)
        return lax.dynamic_update_slice(kept, order.after(piece), (first, 0, 0))

    sent = 0
    for step in range(1, half + 1):
        ahead, back = order.after(ahead, back)
        slot = 2 * step - 1
        if step < half:
            piece = jnp.stack([ahead, back])
            order.ran(ahead, back)
            if step < half - 1:
                ahead, back = ring_shift(ahead, 1, count), ring_shift(back, -1, count)
            else:
                ahead, back = ring_shift(ahead[:own], 1, count), ring_shift(back[own:], -1, count)
        else:
            piece = jnp.concatenate([ahead, back], axis=0)[None]
        waiting.append(piece)
        if step != half - 1:
            sent = send_near(sent)
            waiting = []
        kv_a = lax.dynamic_update_slice(kv_a, piece, (slot, 0, 0))
        if step == 1:
            latent_half = jnp.concatenate([latent, order.after(latent_far)], axis=0)
            order.ran(latent_half)
            latent_near = near(latent_half)
        if step == min(2, half - 1):
            latent_all = jnp.concatenate([latent_half, order.after(latent_near)], axis=0)
            query, cos, sin = project_rotate(lengths, latent_all, q_up, freq)
            order.ran(query)
        if step > 2 and moving and step < half:
            kv_b = take_near(kv_b)
    while moving:
        kv_b = take_near(kv_b)
    both_far = order.after(both_far)
    input_half = jnp.concatenate([block_input, both_far[:own]], axis=0)
    grad_half = jnp.concatenate([cotangent, both_far[own:]], axis=0)
    order.ran(input_half, grad_half)
    grad_near = near(grad_half)
    kv_a, kv_b = order.after(kv_a, kv_b)
    attended, attended_t, lse = attend(lengths, order.after(query), kv_a, kv_b)
    order.ran(attended)

    def sum_half(lefts, rights, dims, meanwhile):
        lefts[0] = order.after(lefts[0])
        keep, send = product(lefts, rights, dims)
        order.ran(send)
        chip = add(keep, order.after(near(send))).astype(BF16)
        order.ran(chip)
        moving = far(swap(chip))
        made = meanwhile()
        return add(chip, order.after(moving)), made

    share = q_down.shape[0] // (count * group)
    width = block_input.shape[1]

    def before_residual():
        normed_half = (rms_parts(order.after(input_half).astype(F32))[0] * norm1_gain).astype(BF16)
        scaled_q, inverse_q = rms_parts(dot(normed_half, q_down))
        order.ran(scaled_q)

        picked_mine, picked_other = share_of_columns(owner, mine, normed_half, share, group)
        order.ran(picked_mine)
        picked_near = near(picked_other)
        grad_all = jnp.concatenate([grad_half, order.after(grad_near)], axis=0)
        grad_hidden = dot(grad_all, down_weight, NT)
        order.ran(grad_hidden)
        picked_all = jnp.concatenate([picked_mine, order.after(picked_near)], axis=1)
        order.wait(picked_all)
        return scaled_q, inverse_q, picked_all, grad_all, grad_hidden

    branch, (scaled_q, inverse_q, picked, grad_all, grad_hidden) = sum_half(
        [attended], [out_weight], NN, before_residual
    )
    residual = input_half.astype(F32) + branch
    scaled_two, inverse_two = rms_parts(residual)
    normed_half = (scaled_two * norm2_gain).astype(BF16)
    order.ran(normed_half)
    normed_two = jnp.concatenate([normed_half, order.after(near(normed_half))], axis=0)

    hidden, hidden_t, grad_gate, grad_up = hidden_units(normed_two, gate_weight, up_weight, grad_hidden)
    order.ran(hidden)

    slot_out = slot_of(jnp.arange(count, dtype=jnp.int32), count, seq) ^ seq
    slot_out = sum(((slot_out >> (bit.bit_length() - 1)) & 1) << (len(bits) - 1 - i) for i, bit in enumerate(bits))

    h = {}

    def keep(name, value):
        h[name] = value
        order.ran(value)

    def halving(name, send, kept, bits=bits):
        h[name] = Halving(order, bits, count, order.after(send), kept)

    def started(name, make, bits=bits):
        def step():
            parts = make()
            order.ran(parts)
            h[name] = Halving(order, bits, count, parts)

        return step

    def kept(name, make):
        def step():
            parts = make()
            order.ran(parts)
            h[name].keep(parts)

        return step

    def down_parts(which):
        return lambda: grad_by_columns(which, order.after(hidden_t), grad_all, count)

    def rows_parts(which, right):
        return lambda: grad_by_rows(which, order.after(normed_two), [right], count)[0]

    def units_back():
        h["units_keep"], send = product(
            [order.after(grad_gate), grad_up], [gate_weight, up_weight], NT
        )
        order.ran(send)
        h["units_near"] = near(send)

    def units_chip():
        keep("units_chip", add(h["units_keep"], order.after(h["units_near"])).astype(BF16))
        h["units_far"] = far(swap(h["units_chip"]))

    def feed_product():
        h["feed_keep"], send = product([order.after(hidden)], [down_weight], NN)
        order.ran(send)
        h["feed_near"] = near(send)

    def feed_chip():
        keep("feed_chip", add(h["feed_keep"], order.after(h["feed_near"])).astype(BF16))

    def feed_far():
        h["feed_far"] = far(order.after(h["feed_chip"])[own:])

    def branch_grad():
        h["back_two"] = add(h["units_chip"], order.after(h["units_far"]))
        h["grad_residual"] = grad_half.astype(F32) + rms_back(h["back_two"], scaled_two, inverse_two, norm2_gain)
        keep("branch_half", h["grad_residual"].astype(BF16))
        h["branch_near"] = near(h["branch_half"])

    def attended_back():
        h["grad_branch"] = jnp.concatenate([h["branch_half"], order.after(h["branch_near"])], axis=0)
        h["grad_attended"], h["delta"] = attended_grad(h["grad_branch"], out_weight, attended)
        order.ran(h["grad_attended"])

    def out_part(name, which, part):
        return lambda: keep(
            name, grad_by_columns(which, order.after(attended_t), h["grad_branch"], count, part, 2)
        )

    def attention_back():
        h["grad_query"], h["dkv_a"], dkv_b = attend_back(
            lengths, slot_out, query, order.after(h["grad_attended"]), kv_a, kv_b, lse, h["delta"], cos, sin
        )
        order.ran(h["grad_query"])
        h["dkv_near"] = near(dkv_b)

    def latent_product():
        h["latent_keep"], send = product([order.after(h["grad_query"])], [q_up], NT)
        order.ran(send)
        h["latent_near"] = near(send)

    def latent_chip():
        keep("latent_chip", add(h["latent_keep"], order.after(h["latent_near"])).astype(BF16))

    def latent_far():
        h["latent_far"] = far(swap(order.after(h["latent_chip"])))

    def compressed():
        h["grad_latent"] = add(h["latent_chip"], order.after(h["latent_far"]))
        keep("grad_compressed", rms_back(h["grad_latent"], scaled_q, inverse_q, q_gain).astype(BF16))
        h["compressed_near"] = near(h["grad_compressed"])

    def down_q_parts():
        both = jnp.concatenate([h["grad_compressed"], order.after(h["compressed_near"])], axis=0)
        keep("down_q_parts", dot(picked, both).astype(BF16))

    def feed():
        total = add(h["feed_chip"][:own], order.after(h["feed_far"]))
        keep("block_output", (residual[:own] + total).astype(BF16))

    def chip_keys():
        keep("chip_kv", add(h["dkv_a"], order.after(h["dkv_near"])).astype(BF16))
        h["kv_far"] = far(h["chip_kv"][:, own:])

    def keys():
        keep("chips_kv", add(h["chip_kv"][:, :own], order.after(h["kv_far"])).astype(BF16))
        halving("kv", h["chips_kv"][half:], h["chips_kv"][:half])

    def own_keys_grad():
        total = h["kv"].finish()
        former, latter = total[:, :mid], total[:, mid:HD]
        turned = [
            former * cos[:own] + latter * sin[:own],
            latter * cos[:own] - former * sin[:own],
            total[:, HD:],
        ]
        keep("kv_raw", jnp.concatenate(turned, axis=1).astype(BF16))
        h["kv_raw_far"] = far(h["kv_raw"])

    def half_keys():
        keep("kv_half", jnp.concatenate([h["kv_raw"], order.after(h["kv_raw_far"])], axis=0))
        h["kv_half_near"] = near(h["kv_half"])

    def kv_parts():
        both = jnp.concatenate([h["kv_half"], order.after(h["kv_half_near"])], axis=0)
        keep("kv_parts", dot(picked, both).astype(BF16))

    def normed_grad():
        scaled_one, inverse_one = rms_parts(order.after(block_input).astype(F32))
        grad_normed = dot(h["grad_compressed"][:own], q_down, NT) + dot(h["kv_raw"], kv_weight, NT)
        h["input_grad"] = h["grad_residual"][:own] + rms_back(grad_normed, scaled_one, inverse_one, norm1_gain)
        keep("gain_one", jnp.sum(grad_normed * scaled_one, axis=0))
        h["gain_far"] = far(h["gain_one"])

    def gains_own():
        gain_one = h["gain_one"] + order.after(h["gain_far"])
        gain_two = jnp.sum(h["back_two"] * scaled_two, axis=0)
        gain_q = jnp.sum(h["grad_latent"] * scaled_q, axis=0)
        keep("gains", jnp.concatenate([gain_one, gain_two, gain_q]))
        h["gains_moved"] = near(h["gains"])

    def gains_step(bit):
        def step():
            keep("gains", h["gains"] + order.after(h["gains_moved"]))
            if bit:
                h["gains_moved"] = swap_seq(h["gains"], bit, count)

        return step

    def gains_later():
        for bit in bits[2:]:
            gains_step(bit)()
        gains_step(None)()

    def query_send():
        [parts] = grad_by_rows(owner[half:], order.after(latent_all), [h["grad_query"]], count)
        keep("query_send", parts)

    def query_keep():
        [parts] = grad_by_rows(owner[:half], order.after(latent_all), [h["grad_query"]], count)
        keep("query_keep", parts)

    def shares(name, parts):
        def step():
            by_owner = h[parts].reshape(count, share, -1)
            halving(name, by_owner[half:], by_owner[:half])

        return step

    hop = lambda name: lambda: h[name].hop()
    finish = lambda name: lambda: h.update({name: h[name].finish()})
    steps = {
        "latent_product": latent_product, "latent_chip": latent_chip, "latent_far": latent_far,
        "compressed": compressed, "down_q_parts": down_q_parts, "feed": feed,
        "chip_keys": chip_keys, "keys": keys, "own_keys_grad": own_keys_grad, "half_keys": half_keys,
        "kv_parts": kv_parts, "normed_grad": normed_grad, "gains_own": gains_own,
        "gains_1": gains_step(bits[0]), "gains_2": gains_step(bits[1]), "gains_3": gains_later,
        "out_keep0": out_part("out_keep0", owner[:half], 0), "out_keep1": out_part("out_keep1", owner[:half], 1),
        "out_send0": out_part("out_send0", owner[half:], 0), "out_send1": out_part("out_send1", owner[half:], 1),
        "down": started("down", down_parts(owner[half:])), "down_keep": kept("down", down_parts(owner[:half])),
        "up": started("up", rows_parts(owner_two[half:], grad_up), bits_two),
        "up_keep": kept("up", rows_parts(owner_two[:half], grad_up)),
        "gate": started("gate", rows_parts(owner[half:], grad_gate)),
        "gate_keep": kept("gate", rows_parts(owner[:half], grad_gate)),
        "units_back": units_back, "units_chip": units_chip, "feed_product": feed_product, "feed_chip": feed_chip,
        "feed_far": feed_far, "branch_grad": branch_grad, "attended_back": attended_back,
        "attention_back": attention_back, "down_1": hop("down"), "up_1": lambda: h["up"].hop(go=False),
        "query_send": query_send, "query_keep": query_keep,
        "up_go": lambda: h["up"].go(), "down_2": hop("down"), "down_end": finish("down"), "gate_1": hop("gate"),
        "gate_2": hop("gate"), "gate_end": finish("gate"), "up_2": hop("up"), "up_end": finish("up"),
        "kv_1": hop("kv"), "kv_2": hop("kv"),
        "out_a": lambda: halving("out_a", h["out_send0"], h["out_keep0"]),
        "out_a_1": hop("out_a"), "out_a_2": hop("out_a"), "out_a_end": finish("out_a"),
        "out_b": lambda: halving("out_b", h["out_send1"], h["out_keep1"]),
        "out_b_1": hop("out_b"), "out_b_2": hop("out_b"), "out_b_end": finish("out_b"),
        "query": lambda: halving("query", h["query_send"], h["query_keep"]),
        "query_1": hop("query"), "query_2": hop("query"), "query_end": finish("query"),
        "q_down": shares("q_down", "down_q_parts"),
        "q_down_1": hop("q_down"), "q_down_2": hop("q_down"), "q_down_end": finish("q_down"),
        "kv_w": shares("kv_w", "kv_parts"),
        "kv_w_1": hop("kv_w"), "kv_w_2": hop("kv_w"), "kv_w_end": finish("kv_w"),
    }
    assert sorted(steps) == sorted(STEPS)
    for name in STEPS:
        steps[name]()

    place = seq * group + mine
    q_share = q_gain.shape[0] // (count * group)
    part_of = lambda first, size: lax.dynamic_slice(h["gains"], (first + place * size,), (size,))
    return (
        h["block_output"],
        h["input_grad"],
        part_of(0, share),
        h["q_down"],
        part_of(2 * width, q_share),
        h["query"],
        h["kv_w"],
        jnp.concatenate([h["out_a"], h["out_b"]], axis=0),
        part_of(width, share),
        h["gate"],
        h["up"],
        h["down"],
    )


def solution(mesh):
    both = P(("seq", "tensor"))
    rows = P(("seq", "tensor"), None)
    return jax.shard_map(
        body,
        mesh=mesh,
        in_specs=(
            rows, P(), P(), P(), P(), P(None, "tensor"), P(), P("tensor", None), P(),
            P(None, "tensor"), P(None, "tensor"), P("tensor", None), rows,
        ),
        out_specs=(
            rows, rows, both, rows, both, P("seq", "tensor"), rows, P("tensor", "seq"), both,
            P("seq", "tensor"), P("seq", "tensor"), P("tensor", "seq"),
        ),
        check_vma=False,
    )
```

```python
import functools
import math

import jax
import jax.numpy as jnp
from jax import lax
from jax.experimental import pallas as pl
from jax.experimental.pallas import tpu as pltpu
from jax.sharding import PartitionSpec as P

HD = 256
EPS = 1e-06
NEG = -1e30
F32 = jnp.float32
BF16 = jnp.bfloat16
LOG2_SCALE = math.log2(math.e) / math.sqrt(HD)
SCALE = 1.0 / math.sqrt(HD)
MIB = 1 << 20
BRIEF = pl.CostEstimate(flops=1000, bytes_accessed=1000, transcendentals=0)

STEPS = (
    "down", "down_keep", "up", "up_keep", "units_back", "units_chip", "feed_product", "feed_chip",
    "branch_grad", "feed_far", "gate", "down_1", "attended_back", "out_send0", "out_send1", "gate_keep",
    "up_1", "attention_back", "latent_product", "feed", "down_2", "gate_1", "chip_keys", "latent_chip",
    "up_go", "out_keep0", "out_keep1", "query_send", "query_keep", "down_end", "keys", "latent_far", "up_2",
    "out_a", "kv_1", "compressed", "kv_2", "gate_2", "out_a_1", "out_b", "up_end", "gate_go", "down_q_parts",
    "own_keys_grad", "half_keys", "normed_grad", "out_b_1", "query", "gains_own", "kv_parts", "kv_w",
    "out_a_2", "gains_1", "kv_w_1", "gate_end", "q_down", "out_a_end", "kv_w_2", "out_b_2", "query_1",
    "gains_2", "q_down_1", "gains_3", "query_2", "kv_w_end", "out_b_end", "q_down_2", "gains_4", "q_down_end",
    "query_end",
)

NN = (((1,), (0,)), ((), ()))
NT = (((1,), (1,)), ((), ()))
TN = (((0,), (0,)), ((), ()))


def dot(left, right, dims=NN):
    return lax.dot_general(left, right, dims, preferred_element_type=F32)


def at_index(values, index, axis, keepdims=True):
    start = [jnp.int32(0)] * values.ndim
    start[axis] = index
    size = values.shape[:axis] + (1,) + values.shape[axis + 1 :]
    taken = lax.dynamic_slice(values, start, size, allow_negative_indices=False)
    return taken if keepdims else lax.squeeze(taken, [axis])


def rms_parts(values):
    inverse = lax.rsqrt(jnp.mean(values * values, axis=-1, keepdims=True) + EPS)
    return values * inverse, inverse


def rms_back(grad_out, scaled, inverse, gain):
    inner = grad_out * gain
    return inverse * (inner - scaled * jnp.mean(inner * scaled, axis=-1, keepdims=True))


def place_in_kernel():
    return lax.axis_index("seq").astype(jnp.int32), lax.axis_index("tensor").astype(jnp.int32)


def group_block(row, own):
    block = lax.div(row, jnp.int32(own))
    return ((block & 1) << 1) | (block >> 1), row - block * own


def first_in_kernel(token, lengths):
    found = jnp.zeros_like(token)
    start = jnp.int32(0)
    for i in range(lengths.shape[0] - 1):
        start = start + lengths[i]
        found = jnp.maximum(found, jnp.where(token >= start, start, 0))
    return found


def angles_in_kernel(rows, own, lengths, freq_ref):
    seq, mine = place_in_kernel()
    other, within = group_block(lax.broadcasted_iota(jnp.int32, (rows, HD // 2), 0), own)
    token = seq * (4 * own) + (mine ^ other) * own + within
    theta = (token - first_in_kernel(token, lengths)).astype(F32) * freq_ref[0:1, :]
    return jnp.cos(theta), jnp.sin(theta)


def slot_of(slot, count, seq):
    place = jnp.where((seq & 1) == 0, seq >> 1, count - 1 - (seq >> 1))
    step = (slot + 1) >> 1
    place = (place + jnp.where((slot & 1) == 1, -step, step)) & (count - 1)
    return seq_at(place, count)


def slot_state(lengths, slot, count, rows):
    seq, _ = place_in_kernel()
    source = slot_of(slot, count, seq)
    first = first_in_kernel(seq * rows, lengths)
    last = first_in_kernel(seq * rows + rows - 1, lengths)
    base = source * rows
    needed = (source <= seq) & (source >= lax.div(first, jnp.int32(rows)))
    bounded = (source == seq) | (base < last)
    return base, needed, bounded


def key_bias(lengths, base, keys, rows):
    seq, mine = place_in_kernel()
    own = rows // 4
    other, within = group_block(lax.broadcasted_iota(jnp.int32, (keys, rows), 0), own)
    token = base + (mine ^ other) * own + within
    other, within = group_block(lax.broadcasted_iota(jnp.int32, (8, rows), 1), own)
    query = seq * rows + (mine ^ other) * own + within
    low = first_in_kernel(query, lengths)
    allowed = (token <= query[0:1, :]) & (token >= low[0:1, :])
    return jnp.where(allowed, 0.0, NEG)


def keys_kernel(lengths, x_ref, gain_ref, w_ref, freq_ref, out_ref, normed_ref):
    values = x_ref[...].astype(F32)
    inverse = lax.rsqrt(jnp.mean(values * values, axis=-1, keepdims=True) + EPS)
    normed = (values * inverse * gain_ref[...]).astype(BF16)
    normed_ref[...] = normed
    raw = dot(normed, w_ref[...])
    cos, sin = angles_in_kernel(x_ref.shape[0], x_ref.shape[0], lengths, freq_ref)
    mid = HD // 2
    former, latter = raw[:, :mid], raw[:, mid:HD]
    out_ref[:, :mid] = (former * cos - latter * sin).astype(BF16)
    out_ref[:, mid:HD] = (latter * cos + former * sin).astype(BF16)
    out_ref[:, HD:] = raw[:, HD:].astype(BF16)


def own_keys(lengths, values, gain, weight, freq):
    own, depth = values.shape
    whole = lambda *shape: pl.BlockSpec(shape, lambda i, m: (0,) * len(shape))
    return pl.pallas_call(
        keys_kernel,
        grid_spec=pltpu.PrefetchScalarGridSpec(
            num_scalar_prefetch=1,
            grid=(1,),
            in_specs=[whole(own, depth), whole(1, depth), whole(*weight.shape), whole(1, HD // 2)],
            out_specs=[whole(own, 2 * HD), whole(own, depth)],
        ),
        out_shape=[jax.ShapeDtypeStruct((own, 2 * HD), BF16), jax.ShapeDtypeStruct((own, depth), BF16)],
        compiler_params=pltpu.CompilerParams(vmem_limit_bytes=16 * MIB),
        cost_estimate=BRIEF,
        name="own_keys",
    )(lengths, values, gain, weight, freq)


def fwd_kernel(heads, lengths, q_ref, a_ref, b_ref, w_ref, o_ref, ot_ref, lse_ref, keep_ref, send_ref,
               m_s, l_s, acc_s, bias_s, w_s, w_sem):
    slot = pl.program_id(0)
    count = pl.num_programs(0)
    keys, rows = bias_s.shape
    base, needed, bounded = slot_state(lengths, slot, count, rows)

    fetch = pltpu.make_async_copy(w_ref, w_s, w_sem)

    @pl.when(slot == 0)
    def _():
        fetch.start()
        m_s[...] = jnp.full_like(m_s, NEG)
        l_s[...] = jnp.zeros_like(l_s)
        acc_s[...] = jnp.zeros_like(acc_s)

    def tile(masked):
        key = jnp.concatenate([a_ref[0, :, :HD], b_ref[0, :, :HD]], axis=0)
        value = jnp.concatenate([a_ref[0, :, HD:], b_ref[0, :, HD:]], axis=0)
        value_t = value.T
        if masked:
            bias_s[...] = key_bias(lengths, base, keys, rows)

        def score(h):
            return dot(key, q_ref[:, h * HD : (h + 1) * HD], NT)

        following = score(0)
        for h in range(heads):
            scores = following * LOG2_SCALE
            if h + 1 < heads:
                following = score(h + 1)
            if masked:
                scores = scores + bias_s[...]
            old = m_s[h, 0:1, :]
            new = jnp.maximum(old, jnp.max(scores, axis=0, keepdims=True))
            alpha = jnp.exp2(old - new)
            weight = jnp.exp2(scores - new)
            l_s[h, 0:1, :] = l_s[h, 0:1, :] * alpha + jnp.sum(weight, axis=0, keepdims=True)
            m_s[h, 0:1, :] = new
            acc_s[h] = acc_s[h] * alpha + dot(value_t, weight.astype(BF16))

    pl.when(needed & ~bounded)(lambda: tile(False))
    pl.when(needed & bounded)(lambda: tile(True))

    @pl.when(slot == count - 1)
    def _():
        for h in range(heads):
            total = l_s[h, 0:1, :]
            out_t = (acc_s[h] / total).astype(BF16)
            ot_ref[h * HD : (h + 1) * HD, :] = out_t
            o_ref[:, h * HD : (h + 1) * HD] = out_t.T
            lse_ref[h] = jnp.broadcast_to(m_s[h, 0:1, :] + jnp.log2(total), lse_ref.shape[1:])
        fetch.wait()
        cut = min(512, w_s.shape[1])
        for first in range(0, w_s.shape[1], cut):
            at = slice(first, first + cut)
            part = dot(o_ref[...], w_s[:, at]).astype(BF16)
            keep_ref[:, at] = part[: rows // 2]
            send_ref[:, at] = part[rows // 2 :]


def attend(lengths, query, kv_a, kv_b, weight):
    rows, width = query.shape
    heads = width // HD
    slots, half, wide = kv_a.shape
    keys = 2 * half
    whole = lambda *shape: pl.BlockSpec(shape, lambda i, m: (0,) * len(shape))
    tile = pl.BlockSpec((1, half, wide), lambda i, m: (i, 0, 0))
    state = [(heads, 8, rows), (heads, 8, rows), (heads, HD, rows), (keys, rows)]
    branch = ((rows // 2, weight.shape[1]), BF16)
    out = [((rows, width), BF16), ((width, rows), BF16), ((heads, 8, rows), F32), branch, branch]
    return pl.pallas_call(
        functools.partial(fwd_kernel, heads),
        grid_spec=pltpu.PrefetchScalarGridSpec(
            num_scalar_prefetch=1,
            grid=(slots,),
            in_specs=[whole(rows, width), tile, tile, pl.BlockSpec(memory_space=pl.ANY)],
            out_specs=[whole(*shape) for shape, _ in out],
            scratch_shapes=[pltpu.VMEM(shape, F32) for shape in state]
            + [pltpu.VMEM(weight.shape, BF16), pltpu.SemaphoreType.DMA],
        ),
        out_shape=[jax.ShapeDtypeStruct(*o) for o in out],
        compiler_params=pltpu.CompilerParams(vmem_limit_bytes=32 * MIB),
        cost_estimate=BRIEF,
        name="attend",
    )(lengths, query, kv_a, kv_b, weight)


def bwd_kernel(heads, lengths, _, q_ref, do_ref, a_ref, b_ref, lse_ref, delta_ref, cos_ref, sin_ref,
               dq_ref, da_ref, db_ref, dq_s, dk_s, dv_s, bias_s):
    slot = pl.program_id(0)
    keys, rows = bias_s.shape
    base, needed, bounded = slot_state(lengths, slot, pl.num_programs(0), rows)
    half = a_ref.shape[1]

    @pl.when(slot == 0)
    def _():
        dq_s[...] = jnp.zeros_like(dq_s)

    @pl.when(~needed)
    def _():
        da_ref[...] = jnp.zeros_like(da_ref)
        db_ref[...] = jnp.zeros_like(db_ref)

    def tile(masked):
        key = jnp.concatenate([a_ref[0, :, :HD], b_ref[0, :, :HD]], axis=0)
        value = jnp.concatenate([a_ref[0, :, HD:], b_ref[0, :, HD:]], axis=0)
        key_t = key.T
        if masked:
            bias_s[...] = key_bias(lengths, base, keys, rows)
        for h in range(heads):
            at = slice(h * HD, (h + 1) * HD)
            scores = dot(key, q_ref[:, at], NT) * LOG2_SCALE
            if masked:
                scores = scores + bias_s[...]
            weight = jnp.exp2(scores - lse_ref[h, 0:1, :])
            grad = dot(value, do_ref[:, at], NT)
            ds = (weight * (grad - delta_ref[h, 0:1, :])).astype(BF16)
            dv = dot(weight.astype(BF16), do_ref[:, at])
            dk = dot(ds, q_ref[:, at])
            if h == 0:
                dv_s[...] = dv
                dk_s[...] = dk
            else:
                dv_s[...] += dv
                dk_s[...] += dk
            dq_s[h] += dot(key_t, ds)
        da_ref[0, :, :HD] = (dk_s[:half, :] * SCALE).astype(BF16)
        db_ref[0, :, :HD] = (dk_s[half:, :] * SCALE).astype(BF16)
        da_ref[0, :, HD:] = dv_s[:half, :].astype(BF16)
        db_ref[0, :, HD:] = dv_s[half:, :].astype(BF16)

    pl.when(needed & ~bounded)(lambda: tile(False))
    pl.when(needed & bounded)(lambda: tile(True))

    @pl.when(slot == pl.num_programs(0) - 1)
    def _():
        cos, sin = cos_ref[...], sin_ref[...]
        mid = HD // 2
        for h in range(heads):
            grad = (dq_s[h] * SCALE).T
            former, latter = grad[:, :mid], grad[:, mid:]
            dq_ref[:, h * HD : h * HD + mid] = (former * cos + latter * sin).astype(BF16)
            dq_ref[:, h * HD + mid : (h + 1) * HD] = (latter * cos - former * sin).astype(BF16)


def attend_back(lengths, slot_out, query, grad, kv_a, kv_b, lse, delta, cos, sin):
    rows, width = query.shape
    heads = width // HD
    slots, half, wide = kv_a.shape
    keys = 2 * half
    whole = lambda *shape: pl.BlockSpec(shape, lambda i, m, o: (0,) * len(shape))
    tile = pl.BlockSpec((1, half, wide), lambda i, m, o: (i, 0, 0))
    out_tile = pl.BlockSpec((1, half, wide), lambda i, m, o: (o[i], 0, 0))
    return pl.pallas_call(
        functools.partial(bwd_kernel, heads),
        grid_spec=pltpu.PrefetchScalarGridSpec(
            num_scalar_prefetch=2,
            grid=(slots,),
            in_specs=[
                whole(rows, width), whole(rows, width), tile, tile,
                whole(heads, 8, rows), whole(heads, 8, rows), whole(rows, HD // 2), whole(rows, HD // 2),
            ],
            out_specs=[whole(rows, width), out_tile, out_tile],
            scratch_shapes=[
                pltpu.VMEM((heads, HD, rows), F32),
                pltpu.VMEM((keys, HD), F32),
                pltpu.VMEM((keys, HD), F32),
                pltpu.VMEM((keys, rows), F32),
            ],
        ),
        out_shape=[
            jax.ShapeDtypeStruct((rows, width), BF16),
            jax.ShapeDtypeStruct((slots, half, wide), BF16),
            jax.ShapeDtypeStruct((slots, half, wide), BF16),
        ],
        compiler_params=pltpu.CompilerParams(vmem_limit_bytes=32 * MIB),
        cost_estimate=BRIEF,
        name="attend_back",
    )(lengths, slot_out, query, grad, kv_a, kv_b, lse, delta, cos, sin)


def attended_grad_kernel(gb_ref, w_ref, att_ref, out_ref, delta_ref):
    grad = dot(gb_ref[...], w_ref[...], NT).astype(BF16)
    out_ref[...] = grad
    term = grad.astype(F32) * att_ref[...].astype(F32)
    delta_ref[0] = jnp.broadcast_to(jnp.sum(term.T, axis=0, keepdims=True), delta_ref.shape[1:])


def attended_grad(grad_branch, weight, attended):
    rows, depth = grad_branch.shape
    width = weight.shape[0]
    return pl.pallas_call(
        attended_grad_kernel,
        grid=(width // HD,),
        in_specs=[
            pl.BlockSpec((rows, depth), lambda i: (0, 0)),
            pl.BlockSpec((HD, depth), lambda i: (i, 0)),
            pl.BlockSpec((rows, HD), lambda i: (0, i)),
        ],
        out_specs=[pl.BlockSpec((rows, HD), lambda i: (0, i)), pl.BlockSpec((1, 8, rows), lambda i: (i, 0, 0))],
        out_shape=[
            jax.ShapeDtypeStruct((rows, width), BF16),
            jax.ShapeDtypeStruct((width // HD, 8, rows), F32),
        ],
        compiler_params=pltpu.CompilerParams(vmem_limit_bytes=12 * MIB),
        cost_estimate=BRIEF,
        name="attended_grad",
    )(grad_branch, weight, attended)


def product(lefts, rights, dims):
    cut = lefts[0].shape[0] // 2
    keep = sum(dot(left[:cut], right, dims) for left, right in zip(lefts, rights))
    send = sum(dot(left[cut:], right, dims) for left, right in zip(lefts, rights))
    return keep.astype(BF16), send.astype(BF16)


def project_kernel(lengths, x_ref, w_ref, freq_ref, out_ref, cos_ref, sin_ref):
    rows = x_ref.shape[0]

    @pl.when(pl.program_id(0) == 0)
    def _():
        cos_ref[...], sin_ref[...] = angles_in_kernel(rows, rows // 4, lengths, freq_ref)

    raw = dot(x_ref[...], w_ref[...])
    cos, sin = cos_ref[...], sin_ref[...]
    mid = HD // 2
    former, latter = raw[:, :mid], raw[:, mid:]
    out_ref[:, :mid] = (former * cos - latter * sin).astype(BF16)
    out_ref[:, mid:] = (latter * cos + former * sin).astype(BF16)


def project_rotate(lengths, latent, weight, freq):
    rows, rank = latent.shape
    width = weight.shape[1]
    whole = lambda *shape: pl.BlockSpec(shape, lambda i, m: (0,) * len(shape))
    angle = jax.ShapeDtypeStruct((rows, HD // 2), F32)
    return pl.pallas_call(
        project_kernel,
        grid_spec=pltpu.PrefetchScalarGridSpec(
            num_scalar_prefetch=1,
            grid=(width // HD,),
            in_specs=[whole(rows, rank), pl.BlockSpec((rank, HD), lambda i, m: (0, i)), whole(1, HD // 2)],
            out_specs=[
                pl.BlockSpec((rows, HD), lambda i, m: (0, i)), whole(rows, HD // 2), whole(rows, HD // 2),
            ],
        ),
        out_shape=[jax.ShapeDtypeStruct((rows, width), BF16), angle, angle],
        compiler_params=pltpu.CompilerParams(vmem_limit_bytes=10 * MIB),
        cost_estimate=BRIEF,
        name="project_rotate",
    )(lengths, latent, weight, freq)


def hidden_kernel(x_ref, gate_ref, up_ref, gh_ref, hidden_ref, hidden_t_ref, gg_ref, gu_ref, gate_s, up_s):
    step = pl.program_id(0)
    gate = dot(x_ref[...], gate_ref[...])
    up = dot(x_ref[...], up_ref[...])

    @pl.when(step == 0)
    def _():
        gate_s[...] = gate
        up_s[...] = up

    @pl.when(step > 0)
    def _():
        gate_s[...] += gate
        up_s[...] += up

    @pl.when(step == pl.num_programs(0) - 1)
    def _():
        for first in range(0, gate_s.shape[0], 128):
            at = slice(first, first + 128)
            gate_pre, up_pre, grad = gate_s[at, :], up_s[at, :], gh_ref[at, :]
            sigmoid = jax.nn.sigmoid(gate_pre)
            silu = gate_pre * sigmoid
            hidden = (silu * up_pre).astype(BF16)
            hidden_ref[at, :] = hidden
            hidden_t_ref[:, at] = hidden.T
            gg_ref[at, :] = (grad * up_pre * sigmoid * (1.0 + gate_pre * (1.0 - sigmoid))).astype(BF16)
            gu_ref[at, :] = (grad * silu).astype(BF16)


def hidden_units(normed, gate_weight, up_weight, grad_hidden):
    rows, depth = normed.shape
    units = gate_weight.shape[1]
    cut = 512
    whole = lambda *shape: pl.BlockSpec(shape, lambda i: (0,) * len(shape))
    weight = pl.BlockSpec((cut, units), lambda i: (i, 0))
    plain = jax.ShapeDtypeStruct((rows, units), BF16)
    return pl.pallas_call(
        hidden_kernel,
        grid=(depth // cut,),
        in_specs=[pl.BlockSpec((rows, cut), lambda i: (0, i)), weight, weight, whole(rows, units)],
        out_specs=[whole(rows, units), whole(units, rows), whole(rows, units), whole(rows, units)],
        out_shape=[plain, jax.ShapeDtypeStruct((units, rows), BF16), plain, plain],
        scratch_shapes=[pltpu.VMEM((rows, units), F32), pltpu.VMEM((rows, units), F32)],
        compiler_params=pltpu.CompilerParams(vmem_limit_bytes=36 * MIB),
        cost_estimate=BRIEF,
        name="hidden_units",
    )(normed, gate_weight, up_weight, grad_hidden)


def in_order(values, owner, axis):
    return jnp.stack(
        [at_index(values, owner[j], axis, keepdims=False) for j in range(owner.shape[0])]
    )


def rows_kernel(owner, left_ref, *refs):
    count = len(refs) // 2
    left = left_ref[...]
    for right_ref, out_ref in zip(refs[:count], refs[count:]):
        out_ref[0] = dot(left, right_ref[...], TN).astype(BF16)


def grad_by_rows(owner, left, rights, count):
    slots = owner.shape[0]
    rows, width = left.shape
    cut = width // count
    if cut % 128:
        return [in_order(dot(left, r, TN).astype(BF16).reshape(count, cut, -1), owner, 0) for r in rights]
    return pl.pallas_call(
        rows_kernel,
        grid_spec=pltpu.PrefetchScalarGridSpec(
            num_scalar_prefetch=1,
            grid=(slots,),
            in_specs=[pl.BlockSpec((rows, cut), lambda i, o: (0, o[i]))]
            + [pl.BlockSpec(r.shape, lambda i, o: (0, 0)) for r in rights],
            out_specs=[pl.BlockSpec((1, cut, r.shape[1]), lambda i, o: (i, 0, 0)) for r in rights],
        ),
        out_shape=[jax.ShapeDtypeStruct((slots, cut, r.shape[1]), BF16) for r in rights],
        compiler_params=pltpu.CompilerParams(vmem_limit_bytes=16 * MIB),
        cost_estimate=BRIEF,
        name="grad_by_rows",
    )(owner, left, *rights)


def columns_kernel(owner, left_ref, right_ref, out_ref):
    out_ref[0] = dot(left_ref[...], right_ref[...]).astype(BF16)


def grad_by_columns(owner, left_t, right, count, part=0, parts=1):
    slots = owner.shape[0]
    rows, width = right.shape
    cut = width // count
    tall = left_t.shape[0] // parts
    if cut % 128:
        left_t = left_t[part * tall : (part + 1) * tall]
        return in_order(dot(left_t, right).astype(BF16).reshape(tall, count, cut), owner, 1)
    return pl.pallas_call(
        columns_kernel,
        grid_spec=pltpu.PrefetchScalarGridSpec(
            num_scalar_prefetch=1,
            grid=(slots,),
            in_specs=[
                pl.BlockSpec((tall, rows), lambda i, o: (part, 0)),
                pl.BlockSpec((rows, cut), lambda i, o: (0, o[i])),
            ],
            out_specs=pl.BlockSpec((1, tall, cut), lambda i, o: (i, 0, 0)),
        ),
        out_shape=jax.ShapeDtypeStruct((slots, tall, cut), BF16),
        compiler_params=pltpu.CompilerParams(vmem_limit_bytes=16 * MIB),
        cost_estimate=BRIEF,
        name="grad_by_columns",
    )(owner, left_t, right)


def share_kernel(size, meta, x_ref, mine_ref, other_ref, turned_s):
    turned_s[...] = x_ref[...].astype(F32).T
    mine = meta[1, 0]
    mine_ref[...] = turned_s[pl.ds(pl.multiple_of(mine * size, size), size), :].astype(BF16)
    other_ref[...] = turned_s[pl.ds(pl.multiple_of((mine ^ 1) * size, size), size), :].astype(BF16)


def share_of_columns(owner, mine, values, size, group):
    slots = owner.shape[0]
    rows, width = values.shape
    cut = width // slots
    if cut % 128:
        turned = values.T.reshape(slots, group, size, rows)
        return tuple(
            in_order(at_index(turned, which, 1, keepdims=False), owner, 0).reshape(slots * size, rows)
            for which in (mine, mine ^ 1)
        )
    return pl.pallas_call(
        functools.partial(share_kernel, size),
        grid_spec=pltpu.PrefetchScalarGridSpec(
            num_scalar_prefetch=1,
            grid=(slots,),
            in_specs=[pl.BlockSpec((rows, cut), lambda i, m: (0, m[0, i]))],
            out_specs=[pl.BlockSpec((size, rows), lambda i, m: (i, 0))] * 2,
            scratch_shapes=[pltpu.VMEM((cut, rows), F32)],
        ),
        out_shape=[jax.ShapeDtypeStruct((slots * size, rows), BF16)] * 2,
        compiler_params=pltpu.CompilerParams(vmem_limit_bytes=8 * MIB),
        cost_estimate=BRIEF,
        name="share_of_columns",
    )(jnp.stack([owner, jnp.full((slots,), mine)]), values)


def add(*parts):
    total = parts[0].astype(F32)
    for part in parts[1:]:
        total = total + part.astype(F32)
    return total


def near(values):
    return lax.ppermute(values, "tensor", [(i, i ^ 1) for i in range(4)])


def far(values):
    return lax.ppermute(values, "tensor", [(i, i ^ 2) for i in range(4)])


def ring_order(count):
    return list(range(0, count, 2)) + list(range(count - 1, 0, -2))


def ring_shift(values, step, count):
    order = ring_order(count)
    return lax.ppermute(
        values, "seq", [(order[i], order[(i + step) % count]) for i in range(count)]
    )


def seq_at(place, count):
    return jnp.where(place < count // 2, 2 * place, 2 * (count - 1 - place) + 1)


def swap_seq(values, bit, count):
    return lax.ppermute(values, "seq", [(i, i ^ bit) for i in range(count)])


def bits_of(count, first=1):
    bits = [1 << i for i in range(count.bit_length() - 1)]
    return [first] + [b for b in bits if b != first]


def apart_of(bits):
    apart = [0]
    for bit in reversed(bits):
        apart = apart + [bit | a for a in apart]
    return apart


class Order:
    def __init__(self):
        self.last = ()

    def after(self, *values):
        held = lax.optimization_barrier((values, self.last))[0]
        return held if len(values) > 1 else held[0]

    def ran(self, *values):
        self.last = values

    def wait(self, *values):
        self.last = self.last + values


class Halving:
    def __init__(self, order, bits, count, send, *keep):
        self.order, self.bits, self.count = order, list(bits), count
        self.terms = list(keep)
        self.moving = swap_seq(send, self.bits.pop(0), count)

    def keep(self, *values):
        self.terms += values

    def hop(self, go=True):
        assert self.terms and self.moving is not None
        arrived = self.order.after(self.moving)
        self.terms.append(arrived)
        self.moving = None
        cut = arrived.shape[0] // 2
        send = add(*[t[cut:] for t in self.terms]).astype(BF16)
        self.terms = [t[:cut] for t in self.terms]
        self.order.ran(send)
        self.send = send
        if go:
            self.moving = swap_seq(send, self.bits.pop(0), self.count)

    def go(self):
        self.moving = swap_seq(self.order.after(self.send), self.bits.pop(0), self.count)

    def finish(self):
        while self.bits:
            self.hop()
        assert self.terms and self.moving is not None
        arrived = self.order.after(self.moving)
        total = add(*[t[0] for t in self.terms], arrived[0])
        self.order.ran(total)
        return total


def swap(values):
    cut = values.shape[0] // 2
    return jnp.concatenate([values[cut:], values[:cut]], axis=0)


def body(
    block_input, lengths, norm1_gain, q_down, q_gain, q_up, kv_weight, out_weight, norm2_gain,
    gate_weight, up_weight, down_weight, cotangent,
):
    group = lax.axis_size("tensor")
    count = lax.axis_size("seq")
    mine = lax.axis_index("tensor").astype(jnp.int32)
    seq = lax.axis_index("seq").astype(jnp.int32)
    own = block_input.shape[0]
    rows = own * group
    heads = q_up.shape[1] // HD
    bits, bits_two = bits_of(count), bits_of(count, 2)
    owner = seq ^ jnp.array(apart_of(bits), jnp.int32)
    owner_two = seq ^ jnp.array(apart_of(bits_two), jnp.int32)

    order = Order()
    half = count // 2

    mid = HD // 2
    freq = 10000.0 ** (-(2.0 * jnp.arange(mid, dtype=F32)) / HD)[None, :]
    keyval, normed = own_keys(lengths, block_input, norm1_gain[None, :], kv_weight, freq)
    order.ran(keyval)
    keyval_far = far(keyval)
    compressed = dot(order.after(normed), q_down)
    latent = (rms_parts(compressed)[0] * q_gain).astype(BF16)
    order.ran(latent)
    latent_far = far(latent)
    pair = jnp.concatenate([keyval, order.after(keyval_far)], axis=0)
    order.ran(pair)
    ahead, back = ring_shift(pair, 1, count), ring_shift(pair, -1, count)
    input_far = far(order.after(block_input))
    empty = jnp.zeros((count,) + pair.shape, BF16)
    kv_a, kv_b = lax.dynamic_update_slice(empty, order.after(pair)[None], (0, 0, 0)), empty
    waiting, moving = [pair[None]], []

    def send_near(first):
        piece = waiting[0] if len(waiting) == 1 else jnp.concatenate(waiting)
        moving.append((first, near(order.after(piece))))
        return first + piece.shape[0]

    def take_near(kept):
        first, piece = moving.pop(0)
        return lax.dynamic_update_slice(kept, order.after(piece), (first, 0, 0))

    sent = 0
    for step in range(1, half + 1):
        ahead, back = order.after(ahead, back)
        slot = 2 * step - 1
        if step < half:
            piece = jnp.stack([ahead, back])
            order.ran(ahead, back)
            if step < half - 1:
                ahead, back = ring_shift(ahead, 1, count), ring_shift(back, -1, count)
            else:
                ahead, back = ring_shift(ahead[:own], 1, count), ring_shift(back[own:], -1, count)
        else:
            piece = jnp.concatenate([ahead, back], axis=0)[None]
        waiting.append(piece)
        if step != half - 1:
            sent = send_near(sent)
            waiting = []
        kv_a = lax.dynamic_update_slice(kv_a, piece, (slot, 0, 0))
        if step == 1:
            latent_half = jnp.concatenate([latent, order.after(latent_far)], axis=0)
            order.ran(latent_half)
            latent_near = near(latent_half)
        if step == min(2, half - 1):
            latent_all = jnp.concatenate([latent_half, order.after(latent_near)], axis=0)
            query, cos, sin = project_rotate(lengths, latent_all, q_up, freq)
            order.ran(query)
        if step > 2 and moving and step < half:
            kv_b = take_near(kv_b)
    while moving:
        kv_b = take_near(kv_b)
    grad_far = far(order.after(cotangent))
    input_half = jnp.concatenate([block_input, order.after(input_far)], axis=0)
    order.ran(input_half)
    kv_a, kv_b = order.after(kv_a, kv_b)
    attended, attended_t, lse, branch_keep, branch_send = attend(
        lengths, order.after(query), kv_a, kv_b, out_weight
    )
    order.ran(attended)
    grad_far = order.after(grad_far)
    order.wait(grad_far)

    share = q_down.shape[0] // (count * group)
    width = block_input.shape[1]

    def before_residual():
        grad_half = jnp.concatenate([cotangent, order.after(grad_far)], axis=0)
        order.ran(grad_half)
        grad_near = near(grad_half)
        normed_half = (rms_parts(order.after(input_half).astype(F32))[0] * norm1_gain).astype(BF16)
        scaled_q, inverse_q = rms_parts(dot(normed_half, q_down))
        order.ran(scaled_q)

        picked_mine, picked_other = share_of_columns(owner, mine, normed_half, share, group)
        order.ran(picked_mine)
        picked_near = near(picked_other)
        grad_all = jnp.concatenate([grad_half, order.after(grad_near)], axis=0)
        grad_hidden = dot(grad_all, down_weight, NT)
        order.ran(grad_hidden)
        picked_all = jnp.concatenate([picked_mine, order.after(picked_near)], axis=1)
        order.wait(picked_all)
        return scaled_q, inverse_q, picked_all, grad_half, grad_all, grad_hidden

    branch_near = near(order.after(branch_send))
    branch_chip = add(branch_keep, order.after(branch_near)).astype(BF16)
    order.ran(branch_chip)
    branch_far = far(swap(branch_chip))
    scaled_q, inverse_q, picked, grad_half, grad_all, grad_hidden = before_residual()
    branch = add(branch_chip, order.after(branch_far))
    residual = input_half.astype(F32) + branch
    scaled_two, inverse_two = rms_parts(residual)
    normed_half = (scaled_two * norm2_gain).astype(BF16)
    order.ran(normed_half)
    normed_two = jnp.concatenate([normed_half, order.after(near(normed_half))], axis=0)

    hidden, hidden_t, grad_gate, grad_up = hidden_units(normed_two, gate_weight, up_weight, grad_hidden)
    order.ran(hidden)

    slot_out = slot_of(jnp.arange(count, dtype=jnp.int32), count, seq) ^ seq
    slot_out = sum(((slot_out >> (bit.bit_length() - 1)) & 1) << (len(bits) - 1 - i) for i, bit in enumerate(bits))

    h = {}

    def keep(name, value):
        h[name] = value
        order.ran(value)

    def halving(name, send, kept, bits=bits):
        h[name] = Halving(order, bits, count, order.after(send), kept)

    def started(name, make, bits=bits):
        def step():
            parts = make()
            order.ran(parts)
            h[name] = Halving(order, bits, count, parts)

        return step

    def kept(name, make):
        def step():
            parts = make()
            order.ran(parts)
            h[name].keep(parts)

        return step

    def down_parts(which):
        return lambda: grad_by_columns(which, order.after(hidden_t), grad_all, count)

    def rows_parts(which, right):
        return lambda: grad_by_rows(which, order.after(normed_two), [right], count)[0]

    def units_back():
        h["units_keep"], send = product(
            [order.after(grad_gate), grad_up], [gate_weight, up_weight], NT
        )
        order.ran(send)
        h["units_near"] = near(send)

    def units_chip():
        keep("units_chip", add(h["units_keep"], order.after(h["units_near"])).astype(BF16))
        h["units_far"] = far(swap(h["units_chip"]))

    def feed_product():
        h["feed_keep"], send = product([order.after(hidden)], [down_weight], NN)
        order.ran(send)
        h["feed_near"] = near(send)

    def feed_chip():
        keep("feed_chip", add(h["feed_keep"], order.after(h["feed_near"])).astype(BF16))

    def feed_far():
        h["feed_far"] = far(order.after(h["feed_chip"])[own:])

    def branch_grad():
        h["back_two"] = add(h["units_chip"], order.after(h["units_far"]))
        h["grad_residual"] = grad_half.astype(F32) + rms_back(h["back_two"], scaled_two, inverse_two, norm2_gain)
        keep("branch_half", h["grad_residual"].astype(BF16))
        h["branch_near"] = near(h["branch_half"])

    def attended_back():
        h["grad_branch"] = jnp.concatenate([h["branch_half"], order.after(h["branch_near"])], axis=0)
        h["grad_attended"], h["delta"] = attended_grad(h["grad_branch"], out_weight, attended)
        order.ran(h["grad_attended"])

    def out_part(name, which, part):
        return lambda: keep(
            name, grad_by_columns(which, order.after(attended_t), h["grad_branch"], count, part, 2)
        )

    def attention_back():
        h["grad_query"], h["dkv_a"], dkv_b = attend_back(
            lengths, slot_out, query, order.after(h["grad_attended"]), kv_a, kv_b, lse, h["delta"], cos, sin
        )
        order.ran(h["grad_query"])
        h["dkv_near"] = near(dkv_b)

    def latent_product():
        h["latent_keep"], send = product([order.after(h["grad_query"])], [q_up], NT)
        order.ran(send)
        h["latent_near"] = near(send)

    def latent_chip():
        keep("latent_chip", add(h["latent_keep"], order.after(h["latent_near"])).astype(BF16))

    def latent_far():
        h["latent_far"] = far(swap(order.after(h["latent_chip"])))

    def compressed():
        h["grad_latent"] = add(h["latent_chip"], order.after(h["latent_far"]))
        keep("grad_compressed", rms_back(h["grad_latent"], scaled_q, inverse_q, q_gain).astype(BF16))
        h["compressed_near"] = near(h["grad_compressed"])

    def down_q_parts():
        both = jnp.concatenate([h["grad_compressed"], order.after(h["compressed_near"])], axis=0)
        keep("down_q_parts", dot(picked, both).astype(BF16))

    def feed():
        total = add(h["feed_chip"][:own], order.after(h["feed_far"]))
        keep("block_output", (residual[:own] + total).astype(BF16))

    def chip_keys():
        keep("chip_kv", add(h["dkv_a"], order.after(h["dkv_near"])).astype(BF16))
        h["kv_far"] = far(h["chip_kv"][:, own:])

    def keys():
        keep("chips_kv", add(h["chip_kv"][:, :own], order.after(h["kv_far"])).astype(BF16))
        halving("kv", h["chips_kv"][half:], h["chips_kv"][:half])

    def own_keys_grad():
        total = h["kv"].finish()
        former, latter = total[:, :mid], total[:, mid:HD]
        turned = [
            former * cos[:own] + latter * sin[:own],
            latter * cos[:own] - former * sin[:own],
            total[:, HD:],
        ]
        keep("kv_raw", jnp.concatenate(turned, axis=1).astype(BF16))
        h["kv_raw_far"] = far(h["kv_raw"])

    def half_keys():
        keep("kv_half", jnp.concatenate([h["kv_raw"], order.after(h["kv_raw_far"])], axis=0))
        h["kv_half_near"] = near(h["kv_half"])

    def kv_parts():
        both = jnp.concatenate([h["kv_half"], order.after(h["kv_half_near"])], axis=0)
        keep("kv_parts", dot(picked, both).astype(BF16))

    def normed_grad():
        scaled_one, inverse_one = rms_parts(order.after(block_input).astype(F32))
        grad_normed = dot(h["grad_compressed"][:own], q_down, NT) + dot(h["kv_raw"], kv_weight, NT)
        h["input_grad"] = h["grad_residual"][:own] + rms_back(grad_normed, scaled_one, inverse_one, norm1_gain)
        keep("gain_one", jnp.sum(grad_normed * scaled_one, axis=0))
        h["gain_far"] = far(h["gain_one"])

    def gains_own():
        gain_one = h["gain_one"] + order.after(h["gain_far"])
        gain_two = jnp.sum(h["back_two"] * scaled_two, axis=0)
        gain_q = jnp.sum(h["grad_latent"] * scaled_q, axis=0)
        keep("gains", jnp.concatenate([gain_one, gain_two, gain_q]))
        h["gains_moved"] = near(h["gains"])

    def gains_step(bit):
        def step():
            keep("gains", h["gains"] + order.after(h["gains_moved"]))
            if bit:
                h["gains_moved"] = swap_seq(h["gains"], bit, count)

        return step

    def gains_later():
        for bit in bits[3:]:
            gains_step(bit)()
        gains_step(None)()

    def query_send():
        [parts] = grad_by_rows(owner[half:], order.after(latent_all), [h["grad_query"]], count)
        keep("query_send", parts)

    def query_keep():
        [parts] = grad_by_rows(owner[:half], order.after(latent_all), [h["grad_query"]], count)
        keep("query_keep", parts)

    def shares(name, parts):
        def step():
            by_owner = h[parts].reshape(count, share, -1)
            halving(name, by_owner[half:], by_owner[:half])

        return step

    hop = lambda name: lambda: h[name].hop()
    finish = lambda name: lambda: h.update({name: h[name].finish()})
    steps = {
        "latent_product": latent_product, "latent_chip": latent_chip, "latent_far": latent_far,
        "compressed": compressed, "down_q_parts": down_q_parts, "feed": feed,
        "chip_keys": chip_keys, "keys": keys, "own_keys_grad": own_keys_grad, "half_keys": half_keys,
        "kv_parts": kv_parts, "normed_grad": normed_grad, "gains_own": gains_own,
        "gains_1": gains_step(bits[0]), "gains_2": gains_step(bits[1]), "gains_3": gains_step(bits[2]), "gains_4": gains_later,
        "out_keep0": out_part("out_keep0", owner[:half], 0), "out_keep1": out_part("out_keep1", owner[:half], 1),
        "out_send0": out_part("out_send0", owner[half:], 0), "out_send1": out_part("out_send1", owner[half:], 1),
        "down": started("down", down_parts(owner[half:])), "down_keep": kept("down", down_parts(owner[:half])),
        "up": started("up", rows_parts(owner_two[half:], grad_up), bits_two),
        "up_keep": kept("up", rows_parts(owner_two[:half], grad_up)),
        "gate": started("gate", rows_parts(owner[half:], grad_gate)),
        "gate_keep": kept("gate", rows_parts(owner[:half], grad_gate)),
        "units_back": units_back, "units_chip": units_chip, "feed_product": feed_product, "feed_chip": feed_chip,
        "feed_far": feed_far, "branch_grad": branch_grad, "attended_back": attended_back,
        "attention_back": attention_back, "down_1": hop("down"), "up_1": lambda: h["up"].hop(go=False),
        "query_send": query_send, "query_keep": query_keep,
        "up_go": lambda: h["up"].go(), "down_2": hop("down"), "down_end": finish("down"), "gate_1": hop("gate"),
        "gate_2": lambda: h["gate"].hop(go=False), "gate_go": lambda: h["gate"].go(), "gate_end": finish("gate"), "up_2": hop("up"), "up_end": finish("up"),
        "kv_1": hop("kv"), "kv_2": hop("kv"),
        "out_a": lambda: halving("out_a", h["out_send0"], h["out_keep0"]),
        "out_a_1": hop("out_a"), "out_a_2": hop("out_a"), "out_a_end": finish("out_a"),
        "out_b": lambda: halving("out_b", h["out_send1"], h["out_keep1"]),
        "out_b_1": hop("out_b"), "out_b_2": hop("out_b"), "out_b_end": finish("out_b"),
        "query": lambda: halving("query", h["query_send"], h["query_keep"]),
        "query_1": hop("query"), "query_2": hop("query"), "query_end": finish("query"),
        "q_down": shares("q_down", "down_q_parts"),
        "q_down_1": hop("q_down"), "q_down_2": hop("q_down"), "q_down_end": finish("q_down"),
        "kv_w": shares("kv_w", "kv_parts"),
        "kv_w_1": hop("kv_w"), "kv_w_2": hop("kv_w"), "kv_w_end": finish("kv_w"),
    }
    assert sorted(steps) == sorted(STEPS)
    for name in STEPS:
        steps[name]()

    place = seq * group + mine
    q_share = q_gain.shape[0] // (count * group)
    part_of = lambda first, size: lax.dynamic_slice(h["gains"], (first + place * size,), (size,))
    return (
        h["block_output"],
        h["input_grad"],
        part_of(0, share),
        h["q_down"],
        part_of(2 * width, q_share),
        h["query"],
        h["kv_w"],
        jnp.concatenate([h["out_a"], h["out_b"]], axis=0),
        part_of(width, share),
        h["gate"],
        h["up"],
        h["down"],
    )


def solution(mesh):
    both = P(("seq", "tensor"))
    rows = P(("seq", "tensor"), None)
    return jax.shard_map(
        body,
        mesh=mesh,
        in_specs=(
            rows, P(), P(), P(), P(), P(None, "tensor"), P(), P("tensor", None), P(),
            P(None, "tensor"), P(None, "tensor"), P("tensor", None), rows,
        ),
        out_specs=(
            rows, rows, both, rows, both, P("seq", "tensor"), rows, P("tensor", "seq"), both,
            P("seq", "tensor"), P("seq", "tensor"), P("tensor", "seq"),
        ),
        check_vma=False,
    )
```

```python
import functools
import math

import jax
import jax.numpy as jnp
from jax import lax
from jax.experimental import pallas as pl
from jax.experimental.pallas import tpu as pltpu
from jax.sharding import PartitionSpec as P

HD = 256
EPS = 1e-06
NEG = -1e30
F32 = jnp.float32
BF16 = jnp.bfloat16
LOG2_SCALE = math.log2(math.e) / math.sqrt(HD)
SCALE = 1.0 / math.sqrt(HD)
MIB = 1 << 20
BRIEF = pl.CostEstimate(flops=1000, bytes_accessed=1000, transcendentals=0)

STEPS = (
    "down", "down_keep", "up", "up_keep", "units_back", "units_chip", "feed_product", "feed_chip",
    "branch_grad", "feed_far", "gate", "down_1", "attended_back", "out_send0", "out_send1", "gate_keep",
    "up_1", "attention_back", "latent_product", "feed", "down_2", "gate_1", "chip_keys", "latent_chip",
    "up_go", "out_keep0", "out_keep1", "query_send", "query_keep", "down_end", "keys", "latent_far", "up_2",
    "out_a", "kv_1", "compressed", "kv_2", "gate_2", "out_a_1", "out_b", "up_end", "gate_go", "down_q_parts",
    "own_keys_grad", "half_keys", "normed_grad", "out_b_1", "query", "gains_own", "kv_parts", "kv_w",
    "out_a_2", "gains_1", "kv_w_1", "gate_end", "q_down", "out_a_end", "kv_w_2", "out_b_2", "query_1",
    "gains_2", "q_down_1", "gains_3", "query_2", "kv_w_end", "out_b_end", "q_down_2", "gains_4", "q_down_end",
    "query_end",
)

NN = (((1,), (0,)), ((), ()))
NT = (((1,), (1,)), ((), ()))
TN = (((0,), (0,)), ((), ()))


def dot(left, right, dims=NN):
    return lax.dot_general(left, right, dims, preferred_element_type=F32)


def at_index(values, index, axis, keepdims=True):
    start = [jnp.int32(0)] * values.ndim
    start[axis] = index
    size = values.shape[:axis] + (1,) + values.shape[axis + 1 :]
    taken = lax.dynamic_slice(values, start, size, allow_negative_indices=False)
    return taken if keepdims else lax.squeeze(taken, [axis])


def rms_parts(values):
    inverse = lax.rsqrt(jnp.mean(values * values, axis=-1, keepdims=True) + EPS)
    return values * inverse, inverse


def rms_back(grad_out, scaled, inverse, gain):
    inner = grad_out * gain
    return inverse * (inner - scaled * jnp.mean(inner * scaled, axis=-1, keepdims=True))


def place_in_kernel():
    return lax.axis_index("seq").astype(jnp.int32), lax.axis_index("tensor").astype(jnp.int32)


def group_block(row, own):
    block = lax.div(row, jnp.int32(own))
    return ((block & 1) << 1) | (block >> 1), row - block * own


def first_in_kernel(token, lengths):
    found = jnp.zeros_like(token)
    start = jnp.int32(0)
    for i in range(lengths.shape[0] - 1):
        start = start + lengths[i]
        found = jnp.maximum(found, jnp.where(token >= start, start, 0))
    return found


def angles_in_kernel(rows, own, lengths, freq_ref):
    seq, mine = place_in_kernel()
    other, within = group_block(lax.broadcasted_iota(jnp.int32, (rows, HD // 2), 0), own)
    token = seq * (4 * own) + (mine ^ other) * own + within
    theta = (token - first_in_kernel(token, lengths)).astype(F32) * freq_ref[0:1, :]
    return jnp.cos(theta), jnp.sin(theta)


def slot_of(slot, count, seq):
    place = jnp.where((seq & 1) == 0, seq >> 1, count - 1 - (seq >> 1))
    step = (slot + 1) >> 1
    place = (place + jnp.where((slot & 1) == 1, -step, step)) & (count - 1)
    return seq_at(place, count)


def slot_state(lengths, slot, count, rows):
    seq, _ = place_in_kernel()
    source = slot_of(slot, count, seq)
    first = first_in_kernel(seq * rows, lengths)
    last = first_in_kernel(seq * rows + rows - 1, lengths)
    base = source * rows
    needed = (source <= seq) & (source >= lax.div(first, jnp.int32(rows)))
    bounded = (source == seq) | (base < last)
    return base, needed, bounded


def key_bias(lengths, base, keys, rows):
    seq, mine = place_in_kernel()
    own = rows // 4
    other, within = group_block(lax.broadcasted_iota(jnp.int32, (keys, rows), 0), own)
    token = base + (mine ^ other) * own + within
    other, within = group_block(lax.broadcasted_iota(jnp.int32, (8, rows), 1), own)
    query = seq * rows + (mine ^ other) * own + within
    low = first_in_kernel(query, lengths)
    allowed = (token <= query[0:1, :]) & (token >= low[0:1, :])
    return jnp.where(allowed, 0.0, NEG)


def keys_kernel(lengths, x_ref, gain_ref, w_ref, freq_ref, out_ref, normed_ref):
    values = x_ref[...].astype(F32)
    inverse = lax.rsqrt(jnp.mean(values * values, axis=-1, keepdims=True) + EPS)
    normed = (values * inverse * gain_ref[...]).astype(BF16)
    normed_ref[...] = normed
    raw = dot(normed, w_ref[...])
    cos, sin = angles_in_kernel(x_ref.shape[0], x_ref.shape[0], lengths, freq_ref)
    mid = HD // 2
    former, latter = raw[:, :mid], raw[:, mid:HD]
    out_ref[:, :mid] = (former * cos - latter * sin).astype(BF16)
    out_ref[:, mid:HD] = (latter * cos + former * sin).astype(BF16)
    out_ref[:, HD:] = raw[:, HD:].astype(BF16)


def own_keys(lengths, values, gain, weight, freq):
    own, depth = values.shape
    whole = lambda *shape: pl.BlockSpec(shape, lambda i, m: (0,) * len(shape))
    return pl.pallas_call(
        keys_kernel,
        grid_spec=pltpu.PrefetchScalarGridSpec(
            num_scalar_prefetch=1,
            grid=(1,),
            in_specs=[whole(own, depth), whole(1, depth), whole(*weight.shape), whole(1, HD // 2)],
            out_specs=[whole(own, 2 * HD), whole(own, depth)],
        ),
        out_shape=[jax.ShapeDtypeStruct((own, 2 * HD), BF16), jax.ShapeDtypeStruct((own, depth), BF16)],
        compiler_params=pltpu.CompilerParams(vmem_limit_bytes=16 * MIB),
        cost_estimate=BRIEF,
        name="own_keys",
    )(lengths, values, gain, weight, freq)


def fwd_kernel(heads, lengths, q_ref, a_ref, b_ref, w_ref, o_ref, ot_ref, lse_ref, keep_ref, send_ref,
               m_s, l_s, acc_s, bias_s, w_s, w_sem):
    slot = pl.program_id(0)
    count = pl.num_programs(0)
    keys, rows = bias_s.shape
    base, needed, bounded = slot_state(lengths, slot, count, rows)

    fetch = pltpu.make_async_copy(w_ref, w_s, w_sem)

    @pl.when(slot == 0)
    def _():
        fetch.start()
        m_s[...] = jnp.full_like(m_s, NEG)
        l_s[...] = jnp.zeros_like(l_s)
        acc_s[...] = jnp.zeros_like(acc_s)

    def tile(masked):
        key = jnp.concatenate([a_ref[0, :, :HD], b_ref[0, :, :HD]], axis=0)
        value = jnp.concatenate([a_ref[0, :, HD:], b_ref[0, :, HD:]], axis=0)
        value_t = value.T
        if masked:
            bias_s[...] = key_bias(lengths, base, keys, rows)

        def score(h):
            return dot(key, q_ref[:, h * HD : (h + 1) * HD], NT)

        following = score(0)
        for h in range(heads):
            scores = following * LOG2_SCALE
            if h + 1 < heads:
                following = score(h + 1)
            if masked:
                scores = scores + bias_s[...]
            old = m_s[h, 0:1, :]
            new = jnp.maximum(old, jnp.max(scores, axis=0, keepdims=True))
            alpha = jnp.exp2(old - new)
            weight = jnp.exp2(scores - new)
            l_s[h, 0:1, :] = l_s[h, 0:1, :] * alpha + jnp.sum(weight, axis=0, keepdims=True)
            m_s[h, 0:1, :] = new
            acc_s[h] = acc_s[h] * alpha + dot(value_t, weight.astype(BF16))

    pl.when(needed & ~bounded)(lambda: tile(False))
    pl.when(needed & bounded)(lambda: tile(True))

    @pl.when(slot == count - 1)
    def _():
        for h in range(heads):
            total = l_s[h, 0:1, :]
            out_t = (acc_s[h] / total).astype(BF16)
            ot_ref[h * HD : (h + 1) * HD, :] = out_t
            o_ref[:, h * HD : (h + 1) * HD] = out_t.T
            lse_ref[h] = jnp.broadcast_to(m_s[h, 0:1, :] + jnp.log2(total), lse_ref.shape[1:])
        fetch.wait()
        cut = min(512, w_s.shape[1])
        for first in range(0, w_s.shape[1], cut):
            at = slice(first, first + cut)
            part = dot(o_ref[...], w_s[:, at]).astype(BF16)
            keep_ref[:, at] = part[: rows // 2]
            send_ref[:, at] = part[rows // 2 :]


def attend(lengths, query, kv_a, kv_b, weight):
    rows, width = query.shape
    heads = width // HD
    slots, half, wide = kv_a.shape
    keys = 2 * half
    whole = lambda *shape: pl.BlockSpec(shape, lambda i, m: (0,) * len(shape))
    tile = pl.BlockSpec((1, half, wide), lambda i, m: (i, 0, 0))
    state = [(heads, 8, rows), (heads, 8, rows), (heads, HD, rows), (keys, rows)]
    branch = ((rows // 2, weight.shape[1]), BF16)
    out = [((rows, width), BF16), ((width, rows), BF16), ((heads, 8, rows), F32), branch, branch]
    return pl.pallas_call(
        functools.partial(fwd_kernel, heads),
        grid_spec=pltpu.PrefetchScalarGridSpec(
            num_scalar_prefetch=1,
            grid=(slots,),
            in_specs=[whole(rows, width), tile, tile, pl.BlockSpec(memory_space=pl.ANY)],
            out_specs=[whole(*shape) for shape, _ in out],
            scratch_shapes=[pltpu.VMEM(shape, F32) for shape in state]
            + [pltpu.VMEM(weight.shape, BF16), pltpu.SemaphoreType.DMA],
        ),
        out_shape=[jax.ShapeDtypeStruct(*o) for o in out],
        compiler_params=pltpu.CompilerParams(vmem_limit_bytes=32 * MIB),
        cost_estimate=BRIEF,
        name="attend",
    )(lengths, query, kv_a, kv_b, weight)


def bwd_kernel(heads, lengths, _, q_ref, do_ref, a_ref, b_ref, lse_ref, delta_ref, cos_ref, sin_ref,
               dq_ref, da_ref, db_ref, dq_s, dk_s, dv_s, bias_s):
    slot = pl.program_id(0)
    keys, rows = bias_s.shape
    base, needed, bounded = slot_state(lengths, slot, pl.num_programs(0), rows)
    half = a_ref.shape[1]

    @pl.when(slot == 0)
    def _():
        dq_s[...] = jnp.zeros_like(dq_s)

    @pl.when(~needed)
    def _():
        da_ref[...] = jnp.zeros_like(da_ref)
        db_ref[...] = jnp.zeros_like(db_ref)

    def tile(masked):
        key = jnp.concatenate([a_ref[0, :, :HD], b_ref[0, :, :HD]], axis=0)
        value = jnp.concatenate([a_ref[0, :, HD:], b_ref[0, :, HD:]], axis=0)
        key_t = key.T
        if masked:
            bias_s[...] = key_bias(lengths, base, keys, rows)
        for h in range(heads):
            at = slice(h * HD, (h + 1) * HD)
            scores = dot(key, q_ref[:, at], NT) * LOG2_SCALE
            if masked:
                scores = scores + bias_s[...]
            weight = jnp.exp2(scores - lse_ref[h, 0:1, :])
            grad = dot(value, do_ref[:, at], NT)
            ds = (weight * (grad - delta_ref[h, 0:1, :])).astype(BF16)
            dv = dot(weight.astype(BF16), do_ref[:, at])
            dk = dot(ds, q_ref[:, at])
            if h == 0:
                dv_s[...] = dv
                dk_s[...] = dk
            else:
                dv_s[...] += dv
                dk_s[...] += dk
            dq_s[h] += dot(key_t, ds)
        da_ref[0, :, :HD] = (dk_s[:half, :] * SCALE).astype(BF16)
        db_ref[0, :, :HD] = (dk_s[half:, :] * SCALE).astype(BF16)
        da_ref[0, :, HD:] = dv_s[:half, :].astype(BF16)
        db_ref[0, :, HD:] = dv_s[half:, :].astype(BF16)

    pl.when(needed & ~bounded)(lambda: tile(False))
    pl.when(needed & bounded)(lambda: tile(True))

    @pl.when(slot == pl.num_programs(0) - 1)
    def _():
        cos, sin = cos_ref[...], sin_ref[...]
        mid = HD // 2
        for h in range(heads):
            grad = (dq_s[h] * SCALE).T
            former, latter = grad[:, :mid], grad[:, mid:]
            dq_ref[:, h * HD : h * HD + mid] = (former * cos + latter * sin).astype(BF16)
            dq_ref[:, h * HD + mid : (h + 1) * HD] = (latter * cos - former * sin).astype(BF16)


def attend_back(lengths, slot_out, query, grad, kv_a, kv_b, lse, delta, cos, sin):
    rows, width = query.shape
    heads = width // HD
    slots, half, wide = kv_a.shape
    keys = 2 * half
    whole = lambda *shape: pl.BlockSpec(shape, lambda i, m, o: (0,) * len(shape))
    tile = pl.BlockSpec((1, half, wide), lambda i, m, o: (i, 0, 0))
    out_tile = pl.BlockSpec((1, half, wide), lambda i, m, o: (o[i], 0, 0))
    return pl.pallas_call(
        functools.partial(bwd_kernel, heads),
        grid_spec=pltpu.PrefetchScalarGridSpec(
            num_scalar_prefetch=2,
            grid=(slots,),
            in_specs=[
                whole(rows, width), whole(rows, width), tile, tile,
                whole(heads, 8, rows), whole(heads, 8, rows), whole(rows, HD // 2), whole(rows, HD // 2),
            ],
            out_specs=[whole(rows, width), out_tile, out_tile],
            scratch_shapes=[
                pltpu.VMEM((heads, HD, rows), F32),
                pltpu.VMEM((keys, HD), F32),
                pltpu.VMEM((keys, HD), F32),
                pltpu.VMEM((keys, rows), F32),
            ],
        ),
        out_shape=[
            jax.ShapeDtypeStruct((rows, width), BF16),
            jax.ShapeDtypeStruct((slots, half, wide), BF16),
            jax.ShapeDtypeStruct((slots, half, wide), BF16),
        ],
        compiler_params=pltpu.CompilerParams(vmem_limit_bytes=32 * MIB),
        cost_estimate=BRIEF,
        name="attend_back",
    )(lengths, slot_out, query, grad, kv_a, kv_b, lse, delta, cos, sin)


def attended_grad_kernel(gb_ref, w_ref, att_ref, out_ref, delta_ref):
    grad = dot(gb_ref[...], w_ref[...], NT).astype(BF16)
    out_ref[...] = grad
    term = grad.astype(F32) * att_ref[...].astype(F32)
    delta_ref[0] = jnp.broadcast_to(jnp.sum(term.T, axis=0, keepdims=True), delta_ref.shape[1:])


def attended_grad(grad_branch, weight, attended):
    rows, depth = grad_branch.shape
    width = weight.shape[0]
    return pl.pallas_call(
        attended_grad_kernel,
        grid=(width // HD,),
        in_specs=[
            pl.BlockSpec((rows, depth), lambda i: (0, 0)),
            pl.BlockSpec((HD, depth), lambda i: (i, 0)),
            pl.BlockSpec((rows, HD), lambda i: (0, i)),
        ],
        out_specs=[pl.BlockSpec((rows, HD), lambda i: (0, i)), pl.BlockSpec((1, 8, rows), lambda i: (i, 0, 0))],
        out_shape=[
            jax.ShapeDtypeStruct((rows, width), BF16),
            jax.ShapeDtypeStruct((width // HD, 8, rows), F32),
        ],
        compiler_params=pltpu.CompilerParams(vmem_limit_bytes=12 * MIB),
        cost_estimate=BRIEF,
        name="attended_grad",
    )(grad_branch, weight, attended)


def product(lefts, rights, dims):
    cut = lefts[0].shape[0] // 2
    keep = sum(dot(left[:cut], right, dims) for left, right in zip(lefts, rights))
    send = sum(dot(left[cut:], right, dims) for left, right in zip(lefts, rights))
    return keep.astype(BF16), send.astype(BF16)


def project_kernel(lengths, x_ref, w_ref, freq_ref, out_ref, cos_ref, sin_ref):
    rows = x_ref.shape[0]

    @pl.when(pl.program_id(0) == 0)
    def _():
        cos_ref[...], sin_ref[...] = angles_in_kernel(rows, rows // 4, lengths, freq_ref)

    raw = dot(x_ref[...], w_ref[...])
    cos, sin = cos_ref[...], sin_ref[...]
    mid = HD // 2
    former, latter = raw[:, :mid], raw[:, mid:]
    out_ref[:, :mid] = (former * cos - latter * sin).astype(BF16)
    out_ref[:, mid:] = (latter * cos + former * sin).astype(BF16)


def project_rotate(lengths, latent, weight, freq):
    rows, rank = latent.shape
    width = weight.shape[1]
    whole = lambda *shape: pl.BlockSpec(shape, lambda i, m: (0,) * len(shape))
    angle = jax.ShapeDtypeStruct((rows, HD // 2), F32)
    return pl.pallas_call(
        project_kernel,
        grid_spec=pltpu.PrefetchScalarGridSpec(
            num_scalar_prefetch=1,
            grid=(width // HD,),
            in_specs=[whole(rows, rank), pl.BlockSpec((rank, HD), lambda i, m: (0, i)), whole(1, HD // 2)],
            out_specs=[
                pl.BlockSpec((rows, HD), lambda i, m: (0, i)), whole(rows, HD // 2), whole(rows, HD // 2),
            ],
        ),
        out_shape=[jax.ShapeDtypeStruct((rows, width), BF16), angle, angle],
        compiler_params=pltpu.CompilerParams(vmem_limit_bytes=10 * MIB),
        cost_estimate=BRIEF,
        name="project_rotate",
    )(lengths, latent, weight, freq)


def hidden_kernel(x_ref, gate_ref, up_ref, gh_ref, hidden_ref, hidden_t_ref, gg_ref, gu_ref, gate_s, up_s):
    step = pl.program_id(0)
    final = pl.num_programs(0) - 1

    @pl.when(step == 0)
    def _():
        gate_s[...] = dot(x_ref[...], gate_ref[...])
        up_s[...] = dot(x_ref[...], up_ref[...])

    @pl.when((step > 0) & (step < final))
    def _():
        gate_s[...] += dot(x_ref[...], gate_ref[...])
        up_s[...] += dot(x_ref[...], up_ref[...])

    @pl.when(step == final)
    def _():
        for first in range(0, gate_s.shape[0], 256):
            at = slice(first, first + 256)
            gate_pre = gate_s[at, :] + dot(x_ref[at, :], gate_ref[...])
            up_pre = up_s[at, :] + dot(x_ref[at, :], up_ref[...])
            grad = gh_ref[at, :]
            sigmoid = jax.nn.sigmoid(gate_pre)
            silu = gate_pre * sigmoid
            hidden = (silu * up_pre).astype(BF16)
            hidden_ref[at, :] = hidden
            hidden_t_ref[:, at] = hidden.T
            gg_ref[at, :] = (grad * up_pre * sigmoid * (1.0 + gate_pre * (1.0 - sigmoid))).astype(BF16)
            gu_ref[at, :] = (grad * silu).astype(BF16)


def hidden_units(normed, gate_weight, up_weight, grad_hidden):
    rows, depth = normed.shape
    units = gate_weight.shape[1]
    cut = 512
    whole = lambda *shape: pl.BlockSpec(shape, lambda i: (0,) * len(shape))
    weight = pl.BlockSpec((cut, units), lambda i: (i, 0))
    plain = jax.ShapeDtypeStruct((rows, units), BF16)
    return pl.pallas_call(
        hidden_kernel,
        grid=(depth // cut,),
        in_specs=[pl.BlockSpec((rows, cut), lambda i: (0, i)), weight, weight, whole(rows, units)],
        out_specs=[whole(rows, units), whole(units, rows), whole(rows, units), whole(rows, units)],
        out_shape=[plain, jax.ShapeDtypeStruct((units, rows), BF16), plain, plain],
        scratch_shapes=[pltpu.VMEM((rows, units), F32), pltpu.VMEM((rows, units), F32)],
        compiler_params=pltpu.CompilerParams(vmem_limit_bytes=36 * MIB),
        cost_estimate=BRIEF,
        name="hidden_units",
    )(normed, gate_weight, up_weight, grad_hidden)


def in_order(values, owner, axis):
    return jnp.stack(
        [at_index(values, owner[j], axis, keepdims=False) for j in range(owner.shape[0])]
    )


def rows_kernel(owner, left_ref, *refs):
    count = len(refs) // 2
    left = left_ref[...]
    for right_ref, out_ref in zip(refs[:count], refs[count:]):
        out_ref[0] = dot(left, right_ref[...], TN).astype(BF16)


def grad_by_rows(owner, left, rights, count):
    slots = owner.shape[0]
    rows, width = left.shape
    cut = width // count
    if cut % 128:
        return [in_order(dot(left, r, TN).astype(BF16).reshape(count, cut, -1), owner, 0) for r in rights]
    return pl.pallas_call(
        rows_kernel,
        grid_spec=pltpu.PrefetchScalarGridSpec(
            num_scalar_prefetch=1,
            grid=(slots,),
            in_specs=[pl.BlockSpec((rows, cut), lambda i, o: (0, o[i]))]
            + [pl.BlockSpec(r.shape, lambda i, o: (0, 0)) for r in rights],
            out_specs=[pl.BlockSpec((1, cut, r.shape[1]), lambda i, o: (i, 0, 0)) for r in rights],
        ),
        out_shape=[jax.ShapeDtypeStruct((slots, cut, r.shape[1]), BF16) for r in rights],
        compiler_params=pltpu.CompilerParams(vmem_limit_bytes=16 * MIB),
        cost_estimate=BRIEF,
        name="grad_by_rows",
    )(owner, left, *rights)


def columns_kernel(owner, left_ref, right_ref, out_ref):
    out_ref[0] = dot(left_ref[...], right_ref[...]).astype(BF16)


def grad_by_columns(owner, left_t, right, count, part=0, parts=1):
    slots = owner.shape[0]
    rows, width = right.shape
    cut = width // count
    tall = left_t.shape[0] // parts
    if cut % 128:
        left_t = left_t[part * tall : (part + 1) * tall]
        return in_order(dot(left_t, right).astype(BF16).reshape(tall, count, cut), owner, 1)
    return pl.pallas_call(
        columns_kernel,
        grid_spec=pltpu.PrefetchScalarGridSpec(
            num_scalar_prefetch=1,
            grid=(slots,),
            in_specs=[
                pl.BlockSpec((tall, rows), lambda i, o: (part, 0)),
                pl.BlockSpec((rows, cut), lambda i, o: (0, o[i])),
            ],
            out_specs=pl.BlockSpec((1, tall, cut), lambda i, o: (i, 0, 0)),
        ),
        out_shape=jax.ShapeDtypeStruct((slots, tall, cut), BF16),
        compiler_params=pltpu.CompilerParams(vmem_limit_bytes=16 * MIB),
        cost_estimate=BRIEF,
        name="grad_by_columns",
    )(owner, left_t, right)


def share_kernel(size, meta, x_ref, mine_ref, other_ref, turned_s):
    turned_s[...] = x_ref[...].astype(F32).T
    mine = meta[1, 0]
    mine_ref[...] = turned_s[pl.ds(pl.multiple_of(mine * size, size), size), :].astype(BF16)
    other_ref[...] = turned_s[pl.ds(pl.multiple_of((mine ^ 1) * size, size), size), :].astype(BF16)


def share_of_columns(owner, mine, values, size, group):
    slots = owner.shape[0]
    rows, width = values.shape
    cut = width // slots
    if cut % 128:
        turned = values.T.reshape(slots, group, size, rows)
        return tuple(
            in_order(at_index(turned, which, 1, keepdims=False), owner, 0).reshape(slots * size, rows)
            for which in (mine, mine ^ 1)
        )
    return pl.pallas_call(
        functools.partial(share_kernel, size),
        grid_spec=pltpu.PrefetchScalarGridSpec(
            num_scalar_prefetch=1,
            grid=(slots,),
            in_specs=[pl.BlockSpec((rows, cut), lambda i, m: (0, m[0, i]))],
            out_specs=[pl.BlockSpec((size, rows), lambda i, m: (i, 0))] * 2,
            scratch_shapes=[pltpu.VMEM((cut, rows), F32)],
        ),
        out_shape=[jax.ShapeDtypeStruct((slots * size, rows), BF16)] * 2,
        compiler_params=pltpu.CompilerParams(vmem_limit_bytes=8 * MIB),
        cost_estimate=BRIEF,
        name="share_of_columns",
    )(jnp.stack([owner, jnp.full((slots,), mine)]), values)


def add(*parts):
    total = parts[0].astype(F32)
    for part in parts[1:]:
        total = total + part.astype(F32)
    return total


def near(values):
    return lax.ppermute(values, "tensor", [(i, i ^ 1) for i in range(4)])


def far(values):
    return lax.ppermute(values, "tensor", [(i, i ^ 2) for i in range(4)])


def ring_order(count):
    return list(range(0, count, 2)) + list(range(count - 1, 0, -2))


def ring_shift(values, step, count):
    order = ring_order(count)
    return lax.ppermute(
        values, "seq", [(order[i], order[(i + step) % count]) for i in range(count)]
    )


def seq_at(place, count):
    return jnp.where(place < count // 2, 2 * place, 2 * (count - 1 - place) + 1)


def swap_seq(values, bit, count):
    return lax.ppermute(values, "seq", [(i, i ^ bit) for i in range(count)])


def bits_of(count, first=1):
    bits = [1 << i for i in range(count.bit_length() - 1)]
    return [first] + [b for b in bits if b != first]


def apart_of(bits):
    apart = [0]
    for bit in reversed(bits):
        apart = apart + [bit | a for a in apart]
    return apart


class Order:
    def __init__(self):
        self.last = ()

    def after(self, *values):
        held = lax.optimization_barrier((values, self.last))[0]
        return held if len(values) > 1 else held[0]

    def ran(self, *values):
        self.last = values

    def wait(self, *values):
        self.last = self.last + values


class Halving:
    def __init__(self, order, bits, count, send, *keep):
        self.order, self.bits, self.count = order, list(bits), count
        self.terms = list(keep)
        self.moving = swap_seq(send, self.bits.pop(0), count)

    def keep(self, *values):
        self.terms += values

    def hop(self, go=True):
        assert self.terms and self.moving is not None
        arrived = self.order.after(self.moving)
        self.terms.append(arrived)
        self.moving = None
        cut = arrived.shape[0] // 2
        send = add(*[t[cut:] for t in self.terms]).astype(BF16)
        self.terms = [t[:cut] for t in self.terms]
        self.order.ran(send)
        self.send = send
        if go:
            self.moving = swap_seq(send, self.bits.pop(0), self.count)

    def go(self):
        self.moving = swap_seq(self.order.after(self.send), self.bits.pop(0), self.count)

    def finish(self):
        while self.bits:
            self.hop()
        assert self.terms and self.moving is not None
        arrived = self.order.after(self.moving)
        total = add(*[t[0] for t in self.terms], arrived[0])
        self.order.ran(total)
        return total


def swap(values):
    cut = values.shape[0] // 2
    return jnp.concatenate([values[cut:], values[:cut]], axis=0)


def body(
    block_input, lengths, norm1_gain, q_down, q_gain, q_up, kv_weight, out_weight, norm2_gain,
    gate_weight, up_weight, down_weight, cotangent,
):
    group = lax.axis_size("tensor")
    count = lax.axis_size("seq")
    mine = lax.axis_index("tensor").astype(jnp.int32)
    seq = lax.axis_index("seq").astype(jnp.int32)
    own = block_input.shape[0]
    rows = own * group
    heads = q_up.shape[1] // HD
    bits, bits_two = bits_of(count), bits_of(count, 2)
    owner = seq ^ jnp.array(apart_of(bits), jnp.int32)
    owner_two = seq ^ jnp.array(apart_of(bits_two), jnp.int32)

    order = Order()
    half = count // 2

    mid = HD // 2
    freq = 10000.0 ** (-(2.0 * jnp.arange(mid, dtype=F32)) / HD)[None, :]
    keyval, normed = own_keys(lengths, block_input, norm1_gain[None, :], kv_weight, freq)
    order.ran(keyval)
    keyval_far = far(keyval)
    compressed = dot(order.after(normed), q_down)
    latent = (rms_parts(compressed)[0] * q_gain).astype(BF16)
    order.ran(latent)
    latent_far = far(latent)
    pair = jnp.concatenate([keyval, order.after(keyval_far)], axis=0)
    order.ran(pair)
    ahead, back = ring_shift(pair, 1, count), ring_shift(pair, -1, count)
    input_far = far(order.after(block_input))
    empty = jnp.zeros((count,) + pair.shape, BF16)
    kv_a, kv_b = lax.dynamic_update_slice(empty, order.after(pair)[None], (0, 0, 0)), empty
    waiting, moving = [pair[None]], []

    def send_near(first):
        piece = waiting[0] if len(waiting) == 1 else jnp.concatenate(waiting)
        moving.append((first, near(order.after(piece))))
        return first + piece.shape[0]

    def take_near(kept):
        first, piece = moving.pop(0)
        return lax.dynamic_update_slice(kept, order.after(piece), (first, 0, 0))

    sent = 0
    for step in range(1, half + 1):
        ahead, back = order.after(ahead, back)
        slot = 2 * step - 1
        if step < half:
            piece = jnp.stack([ahead, back])
            order.ran(ahead, back)
            if step < half - 1:
                ahead, back = ring_shift(ahead, 1, count), ring_shift(back, -1, count)
            else:
                ahead, back = ring_shift(ahead[:own], 1, count), ring_shift(back[own:], -1, count)
        else:
            piece = jnp.concatenate([ahead, back], axis=0)[None]
        waiting.append(piece)
        if step != half - 1:
            sent = send_near(sent)
            waiting = []
        kv_a = lax.dynamic_update_slice(kv_a, piece, (slot, 0, 0))
        if step == 1:
            latent_half = jnp.concatenate([latent, order.after(latent_far)], axis=0)
            order.ran(latent_half)
            latent_near = near(latent_half)
        if step == min(2, half - 1):
            latent_all = jnp.concatenate([latent_half, order.after(latent_near)], axis=0)
            query, cos, sin = project_rotate(lengths, latent_all, q_up, freq)
            order.ran(query)
        if step > 2 and moving and step < half:
            kv_b = take_near(kv_b)
    while moving:
        kv_b = take_near(kv_b)
    grad_far = far(order.after(cotangent))
    input_half = jnp.concatenate([block_input, order.after(input_far)], axis=0)
    order.ran(input_half)
    kv_a, kv_b = order.after(kv_a, kv_b)
    attended, attended_t, lse, branch_keep, branch_send = attend(
        lengths, order.after(query), kv_a, kv_b, out_weight
    )
    order.ran(attended)
    grad_far = order.after(grad_far)
    order.wait(grad_far)

    share = q_down.shape[0] // (count * group)
    width = block_input.shape[1]

    def before_residual():
        grad_half = jnp.concatenate([cotangent, order.after(grad_far)], axis=0)
        order.ran(grad_half)
        grad_near = near(grad_half)
        normed_half = (rms_parts(order.after(input_half).astype(F32))[0] * norm1_gain).astype(BF16)
        scaled_q, inverse_q = rms_parts(dot(normed_half, q_down))
        order.ran(scaled_q)

        picked_mine, picked_other = share_of_columns(owner, mine, normed_half, share, group)
        order.ran(picked_mine)
        picked_near = near(picked_other)
        grad_all = jnp.concatenate([grad_half, order.after(grad_near)], axis=0)
        grad_hidden = dot(grad_all, down_weight, NT)
        order.ran(grad_hidden)
        picked_all = jnp.concatenate([picked_mine, order.after(picked_near)], axis=1)
        order.wait(picked_all)
        return scaled_q, inverse_q, picked_all, grad_half, grad_all, grad_hidden

    branch_near = near(order.after(branch_send))
    branch_chip = add(branch_keep, order.after(branch_near)).astype(BF16)
    order.ran(branch_chip)
    branch_far = far(swap(branch_chip))
    scaled_q, inverse_q, picked, grad_half, grad_all, grad_hidden = before_residual()
    branch = add(branch_chip, order.after(branch_far))
    residual = input_half.astype(F32) + branch
    scaled_two, inverse_two = rms_parts(residual)
    normed_half = (scaled_two * norm2_gain).astype(BF16)
    order.ran(normed_half)
    normed_two = jnp.concatenate([normed_half, order.after(near(normed_half))], axis=0)

    hidden, hidden_t, grad_gate, grad_up = hidden_units(normed_two, gate_weight, up_weight, grad_hidden)
    order.ran(hidden)

    slot_out = slot_of(jnp.arange(count, dtype=jnp.int32), count, seq) ^ seq
    slot_out = sum(((slot_out >> (bit.bit_length() - 1)) & 1) << (len(bits) - 1 - i) for i, bit in enumerate(bits))

    h = {}

    def keep(name, value):
        h[name] = value
        order.ran(value)

    def halving(name, send, kept, bits=bits):
        h[name] = Halving(order, bits, count, order.after(send), kept)

    def started(name, make, bits=bits):
        def step():
            parts = make()
            order.ran(parts)
            h[name] = Halving(order, bits, count, parts)

        return step

    def kept(name, make):
        def step():
            parts = make()
            order.ran(parts)
            h[name].keep(parts)

        return step

    def down_parts(which):
        return lambda: grad_by_columns(which, order.after(hidden_t), grad_all, count)

    def rows_parts(which, right):
        return lambda: grad_by_rows(which, order.after(normed_two), [right], count)[0]

    def units_back():
        h["units_keep"], send = product(
            [order.after(grad_gate), grad_up], [gate_weight, up_weight], NT
        )
        order.ran(send)
        h["units_near"] = near(send)

    def units_chip():
        keep("units_chip", add(h["units_keep"], order.after(h["units_near"])).astype(BF16))
        h["units_far"] = far(swap(h["units_chip"]))

    def feed_product():
        h["feed_keep"], send = product([order.after(hidden)], [down_weight], NN)
        order.ran(send)
        h["feed_near"] = near(send)

    def feed_chip():
        keep("feed_chip", add(h["feed_keep"], order.after(h["feed_near"])).astype(BF16))

    def feed_far():
        h["feed_far"] = far(order.after(h["feed_chip"])[own:])

    def branch_grad():
        h["back_two"] = add(h["units_chip"], order.after(h["units_far"]))
        h["grad_residual"] = grad_half.astype(F32) + rms_back(h["back_two"], scaled_two, inverse_two, norm2_gain)
        keep("branch_half", h["grad_residual"].astype(BF16))
        h["branch_near"] = near(h["branch_half"])

    def attended_back():
        h["grad_branch"] = jnp.concatenate([h["branch_half"], order.after(h["branch_near"])], axis=0)
        h["grad_attended"], h["delta"] = attended_grad(h["grad_branch"], out_weight, attended)
        order.ran(h["grad_attended"])

    def out_part(name, which, part):
        return lambda: keep(
            name, grad_by_columns(which, order.after(attended_t), h["grad_branch"], count, part, 2)
        )

    def attention_back():
        h["grad_query"], h["dkv_a"], dkv_b = attend_back(
            lengths, slot_out, query, order.after(h["grad_attended"]), kv_a, kv_b, lse, h["delta"], cos, sin
        )
        order.ran(h["grad_query"])
        h["dkv_near"] = near(dkv_b)

    def latent_product():
        h["latent_keep"], send = product([order.after(h["grad_query"])], [q_up], NT)
        order.ran(send)
        h["latent_near"] = near(send)

    def latent_chip():
        keep("latent_chip", add(h["latent_keep"], order.after(h["latent_near"])).astype(BF16))

    def latent_far():
        h["latent_far"] = far(swap(order.after(h["latent_chip"])))

    def compressed():
        h["grad_latent"] = add(h["latent_chip"], order.after(h["latent_far"]))
        keep("grad_compressed", rms_back(h["grad_latent"], scaled_q, inverse_q, q_gain).astype(BF16))
        h["compressed_near"] = near(h["grad_compressed"])

    def down_q_parts():
        both = jnp.concatenate([h["grad_compressed"], order.after(h["compressed_near"])], axis=0)
        keep("down_q_parts", dot(picked, both).astype(BF16))

    def feed():
        total = add(h["feed_chip"][:own], order.after(h["feed_far"]))
        keep("block_output", (residual[:own] + total).astype(BF16))

    def chip_keys():
        keep("chip_kv", add(h["dkv_a"], order.after(h["dkv_near"])).astype(BF16))
        h["kv_far"] = far(h["chip_kv"][:, own:])

    def keys():
        keep("chips_kv", add(h["chip_kv"][:, :own], order.after(h["kv_far"])).astype(BF16))
        halving("kv", h["chips_kv"][half:], h["chips_kv"][:half])

    def own_keys_grad():
        total = h["kv"].finish()
        former, latter = total[:, :mid], total[:, mid:HD]
        turned = [
            former * cos[:own] + latter * sin[:own],
            latter * cos[:own] - former * sin[:own],
            total[:, HD:],
        ]
        keep("kv_raw", jnp.concatenate(turned, axis=1).astype(BF16))
        h["kv_raw_far"] = far(h["kv_raw"])

    def half_keys():
        keep("kv_half", jnp.concatenate([h["kv_raw"], order.after(h["kv_raw_far"])], axis=0))
        h["kv_half_near"] = near(h["kv_half"])

    def kv_parts():
        both = jnp.concatenate([h["kv_half"], order.after(h["kv_half_near"])], axis=0)
        keep("kv_parts", dot(picked, both).astype(BF16))

    def normed_grad():
        scaled_one, inverse_one = rms_parts(order.after(block_input).astype(F32))
        grad_normed = dot(h["grad_compressed"][:own], q_down, NT) + dot(h["kv_raw"], kv_weight, NT)
        h["input_grad"] = h["grad_residual"][:own] + rms_back(grad_normed, scaled_one, inverse_one, norm1_gain)
        keep("gain_one", jnp.sum(grad_normed * scaled_one, axis=0))
        h["gain_far"] = far(h["gain_one"])

    def gains_own():
        gain_one = h["gain_one"] + order.after(h["gain_far"])
        gain_two = jnp.sum(h["back_two"] * scaled_two, axis=0)
        gain_q = jnp.sum(h["grad_latent"] * scaled_q, axis=0)
        keep("gains", jnp.concatenate([gain_one, gain_two, gain_q]))
        h["gains_moved"] = near(h["gains"])

    def gains_step(bit):
        def step():
            keep("gains", h["gains"] + order.after(h["gains_moved"]))
            if bit:
                h["gains_moved"] = swap_seq(h["gains"], bit, count)

        return step

    def gains_later():
        for bit in bits[3:]:
            gains_step(bit)()
        gains_step(None)()

    def query_send():
        [parts] = grad_by_rows(owner[half:], order.after(latent_all), [h["grad_query"]], count)
        keep("query_send", parts)

    def query_keep():
        [parts] = grad_by_rows(owner[:half], order.after(latent_all), [h["grad_query"]], count)
        keep("query_keep", parts)

    def shares(name, parts):
        def step():
            by_owner = h[parts].reshape(count, share, -1)
            halving(name, by_owner[half:], by_owner[:half])

        return step

    hop = lambda name: lambda: h[name].hop()
    finish = lambda name: lambda: h.update({name: h[name].finish()})
    steps = {
        "latent_product": latent_product, "latent_chip": latent_chip, "latent_far": latent_far,
        "compressed": compressed, "down_q_parts": down_q_parts, "feed": feed,
        "chip_keys": chip_keys, "keys": keys, "own_keys_grad": own_keys_grad, "half_keys": half_keys,
        "kv_parts": kv_parts, "normed_grad": normed_grad, "gains_own": gains_own,
        "gains_1": gains_step(bits[0]), "gains_2": gains_step(bits[1]), "gains_3": gains_step(bits[2]), "gains_4": gains_later,
        "out_keep0": out_part("out_keep0", owner[:half], 0), "out_keep1": out_part("out_keep1", owner[:half], 1),
        "out_send0": out_part("out_send0", owner[half:], 0), "out_send1": out_part("out_send1", owner[half:], 1),
        "down": started("down", down_parts(owner[half:])), "down_keep": kept("down", down_parts(owner[:half])),
        "up": started("up", rows_parts(owner_two[half:], grad_up), bits_two),
        "up_keep": kept("up", rows_parts(owner_two[:half], grad_up)),
        "gate": started("gate", rows_parts(owner[half:], grad_gate)),
        "gate_keep": kept("gate", rows_parts(owner[:half], grad_gate)),
        "units_back": units_back, "units_chip": units_chip, "feed_product": feed_product, "feed_chip": feed_chip,
        "feed_far": feed_far, "branch_grad": branch_grad, "attended_back": attended_back,
        "attention_back": attention_back, "down_1": hop("down"), "up_1": lambda: h["up"].hop(go=False),
        "query_send": query_send, "query_keep": query_keep,
        "up_go": lambda: h["up"].go(), "down_2": hop("down"), "down_end": finish("down"), "gate_1": hop("gate"),
        "gate_2": lambda: h["gate"].hop(go=False), "gate_go": lambda: h["gate"].go(), "gate_end": finish("gate"), "up_2": hop("up"), "up_end": finish("up"),
        "kv_1": hop("kv"), "kv_2": hop("kv"),
        "out_a": lambda: halving("out_a", h["out_send0"], h["out_keep0"]),
        "out_a_1": hop("out_a"), "out_a_2": hop("out_a"), "out_a_end": finish("out_a"),
        "out_b": lambda: halving("out_b", h["out_send1"], h["out_keep1"]),
        "out_b_1": hop("out_b"), "out_b_2": hop("out_b"), "out_b_end": finish("out_b"),
        "query": lambda: halving("query", h["query_send"], h["query_keep"]),
        "query_1": hop("query"), "query_2": hop("query"), "query_end": finish("query"),
        "q_down": shares("q_down", "down_q_parts"),
        "q_down_1": hop("q_down"), "q_down_2": hop("q_down"), "q_down_end": finish("q_down"),
        "kv_w": shares("kv_w", "kv_parts"),
        "kv_w_1": hop("kv_w"), "kv_w_2": hop("kv_w"), "kv_w_end": finish("kv_w"),
    }
    assert sorted(steps) == sorted(STEPS)
    for name in STEPS:
        steps[name]()

    place = seq * group + mine
    q_share = q_gain.shape[0] // (count * group)
    part_of = lambda first, size: lax.dynamic_slice(h["gains"], (first + place * size,), (size,))
    return (
        h["block_output"],
        h["input_grad"],
        part_of(0, share),
        h["q_down"],
        part_of(2 * width, q_share),
        h["query"],
        h["kv_w"],
        jnp.concatenate([h["out_a"], h["out_b"]], axis=0),
        part_of(width, share),
        h["gate"],
        h["up"],
        h["down"],
    )


def solution(mesh):
    both = P(("seq", "tensor"))
    rows = P(("seq", "tensor"), None)
    return jax.shard_map(
        body,
        mesh=mesh,
        in_specs=(
            rows, P(), P(), P(), P(), P(None, "tensor"), P(), P("tensor", None), P(),
            P(None, "tensor"), P(None, "tensor"), P("tensor", None), rows,
        ),
        out_specs=(
            rows, rows, both, rows, both, P("seq", "tensor"), rows, P("tensor", "seq"), both,
            P("seq", "tensor"), P("seq", "tensor"), P("tensor", "seq"),
        ),
        check_vma=False,
    )
```
